32 devices in a mesh: ctx: 16 (over z, x, core), head: 2 (over y).
Axes of the slice: x: 2, y: 2, z: 4, core: 2. Of those that a mesh axis runs over, the one named last changes fastest.
Arguments:
- queries: bfloat16 [4096, 4096], P('ctx', 'head')
- keys: bfloat16 [4096, 256], P('ctx', 'head')
- values: bfloat16 [4096, 256], P('ctx', 'head'), may hold values from -6 to 6
- comp_keys: bfloat16 [64, 256], P('ctx', 'head')
- comp_values: bfloat16 [64, 256], P('ctx', 'head'), may hold values from -6 to 6
- selected: int32 [64, 15], replicated, may hold values from -1 to 59, as said below
- inputs: bfloat16 [4096, 2560], P('ctx'), may hold values from -6 to 6
- w_gate: bfloat16 [2560, 64], P(None, 'head'), may hold values from -0.125 to 0.125
- d_out: bfloat16 [4096, 4096], P('ctx', 'head'), may hold values from -6 to 6
Outputs:
- d_queries: bfloat16 [4096, 4096], P('ctx', 'head')
- d_keys: bfloat16 [4096, 256], P('ctx', 'head')
- d_values: bfloat16 [4096, 256], P('ctx', 'head')
- d_comp_keys: bfloat16 [64, 256], P('ctx', 'head')
- d_comp_values: bfloat16 [64, 256], P('ctx', 'head')
- d_inputs: bfloat16 [4096, 2560], P('ctx', 'head')
The draws below stay inside these ranges and needn't reach their ends.
Inputs may be any that keep to these rules, and one draw needn't show every extreme that they name: `selected`: block c lies on index c // 4 of ctx. Let H = 16 // 2. Entry j of row b names a block on the index that lies r places before the index holding block b, where r = 1 + j * max(H - 1, 0) // 14 for even b and r = H + 1 + j * max(H - 2, 0) // 14 for odd b; the entry is -1 where that index would be below 0 or where r equals that of entry j - 1 of the same row. Over the 4 rows of one index of ctx, each index that is named is named exactly 2 times.
All inputs are finite; a program needn't handle non-finite values.
Results may differ from the reference program's by a relative error of at most 0.019.
Values may be sent and summed in bfloat16 or wider, within the bound.
No kernel may reach another device: no remote copies, remote signals or barrier semaphores. Data moves between devices by JAX's collectives and lax.ppermute only.
A program may use at most 128 MiB of HBM per device.

```python
import jax
import jax.numpy as jnp
from jax import lax

D = 2560
HD = 128
HEADS = 16
BLK = 64
PICKS = 15
GROUPS = 2
QB = 4
TOKENS = 4096
NBLK = 64


def draw_queries(key, part):
    own_key = jax.random.fold_in(key, 1)
    shape = (TOKENS, GROUPS * HEADS * HD)
    result = jnp.clip(jax.random.normal(own_key, shape, jnp.float32), -6.0, 6.0)
    return result.astype(jnp.bfloat16)


def draw_keys(key, part):
    own_key = jax.random.fold_in(key, 2)
    shape = (TOKENS, GROUPS * HD)
    result = jnp.clip(jax.random.normal(own_key, shape, jnp.float32), -6.0, 6.0)
    return result.astype(jnp.bfloat16)


def draw_comp_keys(key, part):
    own_key = jax.random.fold_in(key, 3)
    shape = (NBLK, GROUPS * HD)
    result = jnp.clip(jax.random.normal(own_key, shape, jnp.float32), -6.0, 6.0)
    return result.astype(jnp.bfloat16)


def reach_table(ranks, parity, column):
    half = ranks // 2
    near = 1 + column * max(half - 1, 0) // (PICKS - 1)
    far = half + 1 + column * max(half - 2, 0) // (PICKS - 1)
    return jnp.where(parity == 1, far, near)


def draw_selected(key, part):
    ranks = NBLK // QB
    device = jnp.arange(ranks, dtype=jnp.int32)[:, None, None]
    rowpos = jnp.arange(QB, dtype=jnp.int32)[None, :, None]
    parity = rowpos % 2
    column = jnp.arange(PICKS, dtype=jnp.int32)[None, None, :]
    reach = reach_table(ranks, parity, column)
    before = reach_table(ranks, parity, jnp.maximum(column - 1, 0))
    repeated = (column > 0) & (reach == before)
    owner = device - reach
    local = jax.random.randint(jax.random.fold_in(key, 12), (ranks, QB, PICKS), 0, QB)
    top_entry = (device == ranks - 1) & (rowpos == 0) & (column == 0)
    local = jnp.where(top_entry, QB - 1, local)
    picks = jnp.where((owner >= 0) & jnp.logical_not(repeated), owner * QB + local, -1)
    return picks.reshape(NBLK, PICKS).astype(jnp.int32)


def level_of(key, dims, shards, smallest, top_value):
    def one(position, parts):
        steps = jax.random.uniform(jax.random.fold_in(jax.random.fold_in(key, 6), position), (parts,), jnp.float32, smallest / len(shards), top_value / len(shards))
        return jnp.repeat(jnp.exp(steps), dims[position] // parts).reshape((-1,) + (1,) * (len(dims) - position - 1))

    gain = one(*shards[0])
    for cut in shards[1:]:
        gain = gain * one(*cut)
    return gain


def centred(key, shape, width, limit, cuts=(), held_as=jnp.bfloat16):
    factor_of = level_of(key, shape, cuts, -0.22, 0.18) if cuts else 1.0
    values = jax.random.normal(key, shape, jnp.float32) * width * factor_of
    return jnp.minimum(jnp.maximum(values, -limit), limit).astype(held_as)


def setup_inputs(seed: int = 0) -> dict:
    arg_keys = jax.random.split(jax.random.key(seed), 10)
    return {
        "queries": draw_queries(jax.random.fold_in(arg_keys[9], 71), 0),
        "keys": draw_keys(jax.random.fold_in(arg_keys[9], 71), 0),
        "values": centred(arg_keys[2], (TOKENS, GROUPS * HD), 1.0, 6.0, ((0, 16), (1, 2))),
        "comp_keys": draw_comp_keys(jax.random.fold_in(arg_keys[9], 71), 0),
        "comp_values": centred(arg_keys[4], (NBLK, GROUPS * HD), 1.0, 6.0, ((0, 16), (1, 2))),
        "selected": draw_selected(jax.random.fold_in(arg_keys[9], 71), 0),
        "inputs": centred(arg_keys[6], (TOKENS, D), 1.0, 6.0, ((0, 16),)),
        "w_gate": centred(arg_keys[7], (D, GROUPS * 2 * HEADS), D ** -0.5, 0.125, ((1, 2),)),
        "d_out": centred(arg_keys[8], (TOKENS, GROUPS * HEADS * HD), 1.0, 6.0, ((0, 16), (1, 2))),
    }


def attend(query_blk, key_set, value_set, visible, dout_blk, gate_blk):
    scale = HD ** -0.5
    scores = jnp.einsum('thd,kd->thk', query_blk.astype(jnp.float32), key_set.astype(jnp.float32)) * scale
    scores = jnp.where(visible[:, None, :], scores, -jnp.inf)
    top = jnp.max(scores, axis=-1, keepdims=True)
    expo = jnp.exp(scores - top)
    probs = (expo / jnp.sum(expo, axis=-1, keepdims=True)).astype(jnp.bfloat16)
    out = jnp.einsum('thk,kd->thd', probs.astype(jnp.float32), value_set.astype(jnp.float32))
    d_gate = jnp.sum(dout_blk.astype(jnp.float32) * out, axis=-1)
    d_branch = (gate_blk[:, :, None] * dout_blk.astype(jnp.float32)).astype(jnp.bfloat16)
    d_prob = jnp.einsum('thd,kd->thk', d_branch.astype(jnp.float32), value_set.astype(jnp.float32))
    delta = jnp.sum(probs.astype(jnp.float32) * d_prob, axis=-1, keepdims=True)
    d_score = (probs.astype(jnp.float32) * (d_prob - delta) * scale).astype(jnp.bfloat16)
    d_query = jnp.einsum('thk,kd->thd', d_score.astype(jnp.float32), key_set.astype(jnp.float32))
    d_key = jnp.einsum('thk,thd->kd', d_score.astype(jnp.float32), query_blk.astype(jnp.float32))
    d_value = jnp.einsum('thk,thd->kd', probs.astype(jnp.float32), d_branch.astype(jnp.float32))
    return d_query, d_key, d_value, d_gate


def reference(queries, keys, values, comp_keys, comp_values, selected, inputs, w_gate, d_out):
    gate = jax.nn.sigmoid(jnp.dot(inputs, w_gate, preferred_element_type=jnp.float32))
    lower = jnp.arange(BLK)[:, None] >= jnp.arange(BLK)[None, :]
    dq_parts, dk_parts, dv_parts, dck_parts, dcv_parts, dgate_parts = [], [], [], [], [], []
    for group in range(GROUPS):
        qsel = queries[:, group * HEADS * HD:(group + 1) * HEADS * HD].reshape(NBLK, BLK, HEADS, HD)
        dsel = d_out[:, group * HEADS * HD:(group + 1) * HEADS * HD].reshape(NBLK, BLK, HEADS, HD)
        kblocks = keys[:, group * HD:(group + 1) * HD].reshape(NBLK, BLK, HD)
        vblocks = values[:, group * HD:(group + 1) * HD].reshape(NBLK, BLK, HD)
        ckeys = comp_keys[:, group * HD:(group + 1) * HD]
        cvals = comp_values[:, group * HD:(group + 1) * HD]
        gates = gate[:, group * 2 * HEADS:(group + 1) * 2 * HEADS].reshape(NBLK, BLK, 2 * HEADS)

        def step(carry, block):
            dk_acc, dv_acc, dck_acc, dcv_acc = carry
            query_blk = qsel[block]
            dout_blk = dsel[block]
            gate_blk = gates[block]
            pos = block * BLK + jnp.arange(BLK, dtype=jnp.int32)
            vis_c = (jnp.arange(NBLK, dtype=jnp.int32)[None, :] * BLK) <= pos[:, None]
            dqc, dckb, dcvb, dgc = attend(query_blk, ckeys, cvals, vis_c, dout_blk, gate_blk[:, :HEADS])
            row = selected[block]
            valid = row >= 0
            index = jnp.where(valid, row, 0).astype(jnp.int32)
            key_set = jnp.concatenate([kblocks[block][None], kblocks[index]], axis=0).reshape((PICKS + 1) * BLK, HD)
            value_set = jnp.concatenate([vblocks[block][None], vblocks[index]], axis=0).reshape((PICKS + 1) * BLK, HD)
            vis_p = jnp.broadcast_to(jnp.repeat(valid, BLK)[None, :], (BLK, PICKS * BLK))
            vis_s = jnp.concatenate([lower, vis_p], axis=1)
            dqs, dks, dvs, dgs = attend(query_blk, key_set, value_set, vis_s, dout_blk, gate_blk[:, HEADS:])
            dks = dks.reshape(PICKS + 1, BLK, HD)
            dvs = dvs.reshape(PICKS + 1, BLK, HD)
            weight = valid.astype(jnp.float32)[:, None, None]
            dk_acc = dk_acc.at[block].add(dks[0]).at[index].add(dks[1:] * weight)
            dv_acc = dv_acc.at[block].add(dvs[0]).at[index].add(dvs[1:] * weight)
            d_query = (dqc + dqs).reshape(BLK, HEADS * HD).astype(jnp.bfloat16)
            d_gate = jnp.concatenate([dgc, dgs], axis=-1)
            return (dk_acc, dv_acc, dck_acc + dckb, dcv_acc + dcvb), (d_query, d_gate)

        start = (jnp.zeros((NBLK, BLK, HD), jnp.float32), jnp.zeros((NBLK, BLK, HD), jnp.float32),
                 jnp.zeros((NBLK, HD), jnp.float32), jnp.zeros((NBLK, HD), jnp.float32))
        carry, outs = lax.scan(step, start, jnp.arange(NBLK, dtype=jnp.int32))
        dq_parts.append(outs[0].reshape(TOKENS, HEADS * HD))
        dgate_parts.append(outs[1].reshape(TOKENS, 2 * HEADS))
        dk_parts.append(carry[0].reshape(TOKENS, HD))
        dv_parts.append(carry[1].reshape(TOKENS, HD))
        dck_parts.append(carry[2])
        dcv_parts.append(carry[3])
    d_gate = jnp.concatenate(dgate_parts, axis=1)
    d_z = (d_gate * gate * (1.0 - gate)).astype(jnp.bfloat16)
    d_inputs = lax.dot_general(d_z, w_gate, (((1,), (1,)), ((), ())), preferred_element_type=jnp.float32)
    return (jnp.concatenate(dq_parts, axis=1),
            jnp.concatenate(dk_parts, axis=1).astype(jnp.bfloat16),
            jnp.concatenate(dv_parts, axis=1).astype(jnp.bfloat16),
            jnp.concatenate(dck_parts, axis=1).astype(jnp.bfloat16),
            jnp.concatenate(dcv_parts, axis=1).astype(jnp.bfloat16),
            d_inputs.astype(jnp.bfloat16))
```

```python
import functools

import jax
import jax.numpy as jnp
from jax import lax
from jax.experimental import pallas as pl
from jax.experimental.pallas import tpu as pltpu
from jax.sharding import PartitionSpec as P

BLK = 64
PICKS = 15
LOG2E = 1.4426950408889634
LANES = 256
NEG = -1e30
F32, BF16 = jnp.float32, jnp.bfloat16


def reach_lists(ranks):
    half = ranks // 2
    even, odd = [], []
    for j in range(PICKS):
        near = 1 + j * max(half - 1, 0) // 14
        far = half + 1 + j * max(half - 2, 0) // 14
        if j == 0 or near != 1 + (j - 1) * max(half - 1, 0) // 14:
            even.append((j, near))
        if j == 0 or far != half + 1 + (j - 1) * max(half - 2, 0) // 14:
            odd.append((j, far))
    return even, odd


def in_vmem():
    return pl.BlockSpec(memory_space=pltpu.VMEM)


def in_smem():
    return pl.BlockSpec(memory_space=pltpu.SMEM)


def params():
    return pltpu.CompilerParams(vmem_limit_bytes=60 * 1024 * 1024)


def fill_picks(ranks, qb, lists, p, me, sel_ref, k_ref, v_ref, out_ref):
    for parity, reach in enumerate(lists):
        for j, r in reach:
            dest = jnp.where(me + r < ranks, me + r, me)
            named = sel_ref[j, dest * qb + 2 * p + parity]
            local = jnp.clip(named - me * qb, 0, qb - 1)
            rows = pl.ds(pl.multiple_of(local * BLK, BLK), BLK)
            out_ref[dest, :BLK, :] = k_ref[rows, :]
            out_ref[dest, BLK : 2 * BLK, :] = v_ref[rows, :]


def pack_kernel(ranks, qb, lists, rank_ref, sel_ref, k_ref, v_ref, ck_ref, cv_ref, out_ref):
    hd = k_ref.shape[1]
    me = rank_ref[0]
    comp = jnp.concatenate([ck_ref[...].astype(F32), cv_ref[...].astype(F32)], axis=0).astype(BF16)

    def every(n, carry):
        out_ref[n, 2 * BLK :, :] = comp
        return carry

    lax.fori_loop(0, ranks, every, 0)
    out_ref[me, : 2 * BLK, :] = jnp.zeros((2 * BLK, hd), BF16)
    fill_picks(ranks, qb, lists, 0, me, sel_ref, k_ref, v_ref, out_ref)


def restack(heads, q_ref, do_ref, out_ref):
    hd = out_ref.shape[2] // 4
    per = LANES // BLK
    for i in range(2):
        for c in range(heads // per):
            for n, src in enumerate((q_ref, do_ref)):
                piece = jnp.concatenate(
                    [
                        src[i * BLK : (i + 1) * BLK, h * hd : (h + 1) * hd]
                        for h in range(c * per, (c + 1) * per)
                    ],
                    axis=0,
                )
                out_ref[i, c, n * hd : (n + 1) * hd, :] = turned(piece)
                out_ref[i, c, 2 * hd :, n * hd : (n + 1) * hd] = piece


def parts_of(ref, i, c):
    hd = ref.shape[2] // 4
    return (
        ref[i, c, :hd, :],
        ref[i, c, hd : 2 * hd, :],
        ref[i, c, 2 * hd :, :hd],
        ref[i, c, 2 * hd :, hd:],
    )


def prep_kernel(qb, heads, x_ref, w_ref, q_ref, do_ref, gate_ref, stack_ref):
    nt = (((1,), (1,)), ((), ()))
    z = lax.dot_general(w_ref[...], x_ref[...], nt, preferred_element_type=F32)
    zt = jax.nn.sigmoid(z)
    for i in range(qb):
        for branch in range(2):
            for h in range(heads):
                row = branch * heads + h
                gate_ref[i, branch : branch + 1, h * BLK : (h + 1) * BLK] = zt[
                    row : row + 1, i * BLK : (i + 1) * BLK
                ]
    restack(heads, q_ref, do_ref, stack_ref)


def fold(x, op):
    return op(x.reshape(x.shape[0] // 8, 8, x.shape[1]), axis=0)


def branch_grad(parts, gate, s_scr, u_scr, w_scr, d_scr):
    c2 = 128 ** -0.5 * LOG2E
    top = jnp.full((8, LANES), NEG, F32)
    for at, live, mask in parts:
        s = s_scr[at, :]
        if mask is not None:
            s = jnp.where(mask, s, NEG)
            s_scr[at, :] = s
        part = fold(s, jnp.max)
        top = jnp.maximum(top, part if live is None else jnp.where(live, part, NEG))
    top = jnp.max(top, axis=0, keepdims=True) * c2
    total = jnp.zeros((8, LANES), F32)
    mixed = jnp.zeros((8, LANES), F32)
    for at, live, mask in parts:
        e = jnp.exp2(s_scr[at, :] * c2 - (top if live is None else jnp.where(live, top, -NEG)))
        total = total + fold(e, jnp.sum)
        mixed = mixed + fold(e * u_scr[at, :], jnp.sum)
        s_scr[at, :] = e
    inv = 1.0 / jnp.sum(total, axis=0, keepdims=True)
    d_gate = jnp.sum(mixed, axis=0, keepdims=True) * inv
    weight = gate * inv
    for at, live, mask in parts:
        pw = s_scr[at, :] * weight
        w_scr[at, :] = pw.astype(BF16)
        d_scr[at, :] = (pw * (u_scr[at, :] - d_gate)).astype(BF16)
    return d_gate


def lanes_of(c):
    return slice(c * LANES, (c + 1) * LANES)


def gather(me, row, reach, own_ref, picks_ref, offset, out):
    out[:BLK, :] = own_ref[row * BLK : (row + 1) * BLK, :]
    for n, (_, r) in enumerate(reach):
        src = jnp.where(me >= r, me - r, me)
        out[(n + 1) * BLK : (n + 2) * BLK, :] = picks_ref[src, offset : offset + BLK, :]


def spread(row_vectors, columns, out_ref, heads, first_row):
    for h in range(heads):
        out_ref[first_row + h : first_row + h + 1, columns] = row_vectors[:, h * BLK : (h + 1) * BLK]


def attend_kernel(ranks, qb, heads, lists, p, *refs):
    rank_ref, sel_ref, stack_hbm, k_ref, v_ref, gate_ref, picks_hbm = refs[:7]
    if p == 0:
        refs = refs[7:]
    else:
        dc_ref, *refs = refs[7:]
    own_hbm, dg_ref, dsel_hbm, send_hbm, kcat, vcat, s_scr, u_scr, w_scr, dv_acc, dk_acc = refs[:11]
    own_ref, dsel_ref, send_ref, stack, picks_ref, sems = refs[11:]
    hd = k_ref.shape[1]
    scale = hd ** -0.5
    me = rank_ref[0]
    chunks = heads * BLK // LANES
    copies = []

    def put(src, dst):
        copy = pltpu.make_async_copy(src, dst, sems.at[len(copies)])
        copy.start()
        copies.append(copy)

    put(picks_hbm.at[:, : 2 * BLK, :], picks_ref)
    for g in range(2 * chunks):
        put(stack_hbm.at[g // chunks, g % chunks], stack.at[g // chunks, g % chunks])

    send_ref[me] = jnp.zeros(send_ref.shape[1:], BF16)
    for parity, reach in enumerate(lists):
        if (1 + len(reach)) * BLK < dsel_ref.shape[2]:
            dsel_ref[parity, :, (1 + len(reach)) * BLK :, :] = jnp.zeros(
                (dsel_ref.shape[1], dsel_ref.shape[2] - (1 + len(reach)) * BLK, LANES), BF16
            )
    if p == 0:
        fill_picks(ranks, qb, lists, 1, me, sel_ref, k_ref, v_ref, send_ref)
    else:
        for r in range(1, ranks):
            dest = jnp.where(me >= r, me - r, me)
            at = slice(r * qb, (r + 1) * qb)
            piece = jnp.concatenate([dc_ref[at, :hd], dc_ref[at, hd:]], axis=0)
            send_ref[dest, 2 * BLK :, :] = piece.astype(BF16)

    key_pos = lax.broadcasted_iota(jnp.int32, (BLK, LANES), 0)
    tok_pos = lax.rem(lax.broadcasted_iota(jnp.int32, (BLK, LANES), 1), BLK)
    causal = key_pos <= tok_pos
    parts, sizes = [], []
    for parity, reach in enumerate(lists):
        parts.append([(slice(0, BLK), None, causal)])
        for n, (_, r) in enumerate(reach):
            parts[-1].append((slice((n + 1) * BLK, (n + 2) * BLK), me >= r, None))
        sizes.append((1 + len(reach)) * BLK)

    def fetch(parity):
        row = 2 * p + parity
        gather(me, row, lists[parity], k_ref, picks_ref, 0, kcat.at[parity])
        gather(me, row, lists[parity], v_ref, picks_ref, BLK, vcat.at[parity])

    def scores(g):
        parity, c = g // chunks, g % chunks
        nk = sizes[parity]
        copies[1 + g].wait()
        qt, dt, _, _ = parts_of(stack, parity, c)
        s_scr[g % 2, :nk, :] = jnp.dot(kcat[parity, :nk, :], qt, preferred_element_type=F32)
        u_scr[g % 2, :nk, :] = jnp.dot(vcat[parity, :nk, :], dt, preferred_element_type=F32)

    def soften(g):
        parity, lanes = g // chunks, lanes_of(g % chunks)
        gate = gate_ref[2 * p + parity, 1:2, lanes]
        dg = branch_grad(
            parts[parity], gate, s_scr.at[g % 2], u_scr.at[g % 2], w_scr.at[g % 2],
            dsel_ref.at[parity, g % chunks],
        )
        put(dsel_ref.at[parity, g % chunks], dsel_hbm.at[parity, g % chunks])
        dg_ref[parity : parity + 1, lanes] = dg * gate * (1.0 - gate)

    def gradients(g):
        parity, c = g // chunks, g % chunks
        nk = sizes[parity]
        _, _, qs, ds = parts_of(stack, parity, c)
        dv = jnp.dot(w_scr[g % 2, :nk, :], ds, preferred_element_type=F32)
        dk = jnp.dot(dsel_ref[parity, c, :nk, :], qs, preferred_element_type=F32)
        if c == 0:
            dv_acc[parity, :nk, :] = dv
            dk_acc[parity, :nk, :] = dk
        else:
            dv_acc[parity, :nk, :] += dv
            dk_acc[parity, :nk, :] += dk

    def deliver(parity):
        rows = slice(parity * BLK, (parity + 1) * BLK)
        own_ref[rows, :hd] = dk_acc[parity, :BLK, :] * scale
        own_ref[rows, hd:] = dv_acc[parity, :BLK, :]
        put(own_ref.at[rows], own_hbm.at[rows])
        for n, (_, r) in enumerate(lists[parity]):
            at = slice((n + 1) * BLK, (n + 2) * BLK)
            dest = jnp.where(me >= r, me - r, me)
            send_ref[dest, :BLK, :] = (dk_acc[parity, at, :] * scale).astype(BF16)
            send_ref[dest, BLK : 2 * BLK, :] = dv_acc[parity, at, :].astype(BF16)

    copies[0].wait()
    fetch(0)
    scores(0)
    fetch(1)
    for g in range(2 * chunks):
        if g + 1 < 2 * chunks:
            scores(g + 1)
        if g > 0:
            gradients(g - 1)
        if g == chunks:
            deliver(0)
        soften(g)
    gradients(2 * chunks - 1)
    deliver(1)
    put(send_ref, send_hbm)
    for copy in copies[1 + 2 * chunks :]:
        copy.wait()


def write_dq(row, heads, hd, pairs, dq_ref):
    per = LANES // BLK
    rows = slice(row * BLK, (row + 1) * BLK)
    for c in range(heads // per):
        total = None
        for kt, d_of in pairs:
            part = jnp.dot(kt, d_of(c), preferred_element_type=F32)
            total = part if total is None else total + part
        dq = (total.T * hd ** -0.5).astype(BF16)
        for h in range(per):
            head = c * per + h
            dq_ref[rows, head * hd : (head + 1) * hd] = dq[h * BLK : (h + 1) * BLK, :]


def turned(x):
    return x.astype(F32).T.astype(BF16)


def middle_kernel(ranks, qb, heads, lists, rank_ref, stack0, q_ref, do_ref, k_ref, gate_ref,
                  fetched_ref, dsel_ref, dg_ref, dq_ref, dz_ref, dc_ref, dcomp_ref, kct_ref,
                  stack1, kcat, ckey, cval, s_scr, u_scr, w_scr, d_scr):
    hd = k_ref.shape[1]
    me = rank_ref[0]
    nblocks = ranks * qb
    chunks = heads * BLK // LANES
    span = min(nblocks, BLK)
    pieces = []
    for r in range(ranks):
        pieces.append(fetched_ref[jnp.maximum(me - r, 0), 2 * BLK :, :].astype(F32))
    ckey[...] = jnp.concatenate([x[:qb] for x in pieces], axis=0).astype(BF16)
    cval[...] = jnp.concatenate([x[qb:] for x in pieces], axis=0).astype(BF16)
    kct_ref[...] = turned(ckey[...])
    dz_ref[...] = jnp.zeros_like(dz_ref)
    restack(heads, q_ref, do_ref, stack1)

    for row in range(qb):
        stack = stack0 if row < 2 else stack1
        parts = []
        for n in range(nblocks // span):
            place = lax.broadcasted_iota(jnp.int32, (span, LANES), 0) + n * span
            away, within = place // qb, lax.rem(place, qb)
            seen = (away <= me) & ((away > 0) | (within <= row))
            parts.append((slice(n * span, (n + 1) * span), None, seen))
        dgs, dvs, dks = [], [], []
        for c in range(chunks):
            lanes = lanes_of(c)
            qt, dt, qs, ds = parts_of(stack, row % 2, c)
            s_scr[c % 2] = jnp.dot(ckey[...], qt, preferred_element_type=F32)
            u_scr[c % 2] = jnp.dot(cval[...], dt, preferred_element_type=F32)
            gate = gate_ref[row, 0:1, lanes]
            dg = branch_grad(parts, gate, s_scr.at[c % 2], u_scr.at[c % 2], w_scr.at[:, lanes], d_scr.at[row, :, lanes])
            dgs.append(dg * gate * (1.0 - gate))
            dvs.append(jnp.dot(w_scr[:, lanes], ds, preferred_element_type=F32))
            dks.append(jnp.dot(d_scr[row, :, lanes], qs, preferred_element_type=F32))
        dv = sum(dvs[1:], dvs[0])
        dk = sum(dks[1:], dks[0]) * hd ** -0.5
        if row == 0:
            dc_ref[:, :hd] = dk
            dc_ref[:, hd:] = dv
        else:
            dc_ref[:, :hd] += dk
            dc_ref[:, hd:] += dv
        columns = slice(row * BLK, (row + 1) * BLK)
        spread(jnp.concatenate(dgs, axis=1), columns, dz_ref, heads, 0)

    for parity, reach in enumerate(lists):
        nk = (1 + len(reach)) * BLK
        gather(me, parity, reach, k_ref, fetched_ref, 0, kcat)
        write_dq(
            parity, heads, hd,
            [
                (turned(kcat[:nk, :]), lambda c, nk=nk, parity=parity: dsel_ref[parity, c, :nk, :]),
                (kct_ref[...], lambda c, parity=parity: d_scr[parity, :, lanes_of(c)]),
            ],
            dq_ref,
        )
        spread(dg_ref[parity : parity + 1, :], slice(parity * BLK, (parity + 1) * BLK), dz_ref, heads, heads)
    for i in range(2):
        dcomp_ref[i] = d_scr[2 + i]


def tail_kernel(ranks, qb, heads, lists, rank_ref, k_ref, picks_ref, dsel_ref, dcomp_ref, kct_ref, _, dq_ref, kcat):
    hd = k_ref.shape[1]
    me = rank_ref[0]
    for parity, reach in enumerate(lists):
        nk = (1 + len(reach)) * BLK
        gather(me, 2 + parity, reach, k_ref, picks_ref, 0, kcat)
        write_dq(
            parity, heads, hd,
            [
                (turned(kcat[:nk, :]), lambda c, nk=nk, parity=parity: dsel_ref[parity, c, :nk, :]),
                (kct_ref[...], lambda c, parity=parity: dcomp_ref[parity, :, lanes_of(c)]),
            ],
            dq_ref,
        )


def dz_kernel(heads, dz_in, dg_ref, dz_ref):
    dz = dz_in[...]
    dz_ref[...] = dz
    for i in range(2):
        spread(dg_ref[i : i + 1, :], slice((2 + i) * BLK, (3 + i) * BLK), dz_ref, heads, heads)


def add_homes(ranks, qb, lists, p, me, sel_ref, home_ref, acc):
    hd = home_ref.shape[2]
    for parity, reach in enumerate(lists):
        for j, r in reach:
            src = jnp.minimum(me + r, ranks - 1)
            named = sel_ref[j, src * qb + 2 * p + parity]
            local = jnp.clip(named - me * qb, 0, qb - 1)
            rows = pl.ds(pl.multiple_of(local * BLK, BLK), BLK)
            live = me + r < ranks
            acc[rows, :hd] += jnp.where(live, home_ref[src, :BLK, :].astype(F32), 0.0)
            acc[rows, hd:] += jnp.where(live, home_ref[src, BLK : 2 * BLK, :].astype(F32), 0.0)


def collect_kernel(ranks, qb, lists, rank_ref, sel_ref, own0_ref, own1_ref, home_ref, acc_ref):
    acc_ref[: 2 * BLK, :] = own0_ref[...]
    acc_ref[2 * BLK :, :] = own1_ref[...]
    add_homes(ranks, qb, lists, 0, rank_ref[0], sel_ref, home_ref, acc_ref)


def finish_kernel(ranks, qb, lists, rank_ref, sel_ref, part_ref, dc_ref, home_ref,
                  dk_ref, dv_ref, dck_ref, dcv_ref, acc):
    hd = dk_ref.shape[1]
    me = rank_ref[0]
    acc[...] = part_ref[...]
    add_homes(ranks, qb, lists, 1, me, sel_ref, home_ref, acc)
    dk_ref[...] = acc[:, :hd].astype(BF16)
    dv_ref[...] = acc[:, hd:].astype(BF16)

    def add(n, total):
        return total + home_ref[n, 2 * BLK :, :].astype(F32)

    total = lax.fori_loop(me + 1, ranks, add, jnp.zeros((2 * qb, hd), F32))
    dck_ref[...] = (total[:qb] + dc_ref[:qb, :hd]).astype(BF16)
    dcv_ref[...] = (total[qb:] + dc_ref[:qb, hd:]).astype(BF16)


def body(queries, keys, values, comp_keys, comp_values, selected, inputs, w_gate, d_out):
    tokens, width = queries.shape
    hd = keys.shape[1]
    heads = width // hd
    qb = tokens // BLK
    pair = qb // 2
    ranks = lax.axis_size("ctx")
    rank = lax.axis_index("ctx").astype(jnp.int32)
    me = rank.reshape(1)
    head = lax.axis_index("head")
    nblocks = ranks * qb
    lists = reach_lists(ranks)
    table = selected.T

    slot = 2 * BLK + 2 * qb

    def exchange(x):
        return lax.all_to_all(x, "ctx", split_axis=0, concat_axis=0, tiled=True)

    send = pl.pallas_call(
        functools.partial(pack_kernel, ranks, qb, lists),
        out_shape=jax.ShapeDtypeStruct((ranks, slot, hd), BF16),
        in_specs=[in_smem(), in_smem()] + [in_vmem()] * 4,
        out_specs=in_vmem(),
        compiler_params=params(),
        name="pack",
    )(me, table, keys, values, comp_keys, comp_values)
    fetched = exchange(send)

    def call(kernel, outs, args, name, scratch=(), specs=None, out_specs=None, aliases=None, cost=0, grid=(), sems=0):
        return pl.pallas_call(
            kernel,
            grid=grid,
            out_shape=[jax.ShapeDtypeStruct(shape, dtype) for shape, dtype in outs],
            in_specs=specs or [in_vmem()] * len(args),
            out_specs=out_specs or [in_vmem()] * len(outs),
            scratch_shapes=[pltpu.VMEM(shape, dtype) for shape, dtype in scratch]
            + [pltpu.SemaphoreType.DMA((sems,))] * (sems > 0),
            input_output_aliases=aliases or {},
            compiler_params=params(),
            cost_estimate=pl.CostEstimate(flops=cost, bytes_accessed=4 << 20, transcendentals=0),
            name=name,
        )(*args)

    wide = heads * BLK
    chunks = wide // LANES
    stack_shape = (2, chunks, 4 * hd, LANES)

    def rows_of(p):
        return pl.BlockSpec((2 * BLK, width), lambda i: (p, 0))

    gate, stack0 = call(
        functools.partial(prep_kernel, qb, heads),
        [((qb, 2, wide), F32), (stack_shape, BF16)],
        [inputs, w_gate.T, queries, d_out],
        "prep",
        specs=[in_vmem()] * 2 + [rows_of(0)] * 2,
        grid=(1,),
        cost=2 * inputs.size * w_gate.shape[1],
    )
    half = w_gate.shape[0] // 2
    swap = [(0, 1), (1, 0)]
    w_send = lax.dynamic_slice_in_dim(w_gate, (1 - head) * half, half, 0)
    w_mine = lax.dynamic_slice_in_dim(w_gate, head * half, half, 0)
    w_other = lax.ppermute(w_send, "head", swap)

    nsel = (1 + max(len(x) for x in lists)) * BLK
    smem2 = [in_smem(), in_smem()]

    in_any = pl.BlockSpec(memory_space=pl.ANY)

    def attend(p, picks, stack, previous):
        args = [me, table, stack, keys, values, gate, picks] + previous
        own, dsel, send = (2 * BLK, 2 * hd), (2, chunks, nsel, LANES), (ranks, slot if p else 2 * BLK, hd)
        return call(
            functools.partial(attend_kernel, ranks, qb, heads, lists, p),
            [(own, F32), ((2, wide), F32), (dsel, BF16), (send, BF16)],
            args,
            f"attend{p}",
            specs=smem2 + [in_any] + [in_vmem()] * 3 + [in_any] + [in_vmem()] * len(previous),
            out_specs=[in_any, in_vmem(), in_any, in_any],
            scratch=[
                ((2, nsel, hd), BF16),
                ((2, nsel, hd), BF16),
                ((2, nsel, LANES), F32),
                ((2, nsel, LANES), F32),
                ((2, nsel, LANES), BF16),
                ((2, nsel, hd), F32),
                ((2, nsel, hd), F32),
                (own, F32),
                (dsel, BF16),
                (send, BF16),
                (stack_shape, BF16),
                ((ranks, 2 * BLK, hd), BF16),
            ],
            sems=4 * chunks + 4,
            cost=8 * nsel * wide * 2 * hd,
        )

    own0, dg0, dsel0, send = attend(0, fetched, stack0, [])
    mixed = exchange(send)
    dq, dz, dc, dcomp, kct, stack1 = call(
        functools.partial(middle_kernel, ranks, qb, heads, lists),
        [
            (queries.shape, BF16),
            ((2 * heads, tokens), F32),
            ((nblocks, 2 * hd), F32),
            ((2, nblocks, wide), BF16),
            ((hd, nblocks), BF16),
            (stack_shape, BF16),
        ],
        [me, stack0, queries, d_out, keys, gate, fetched, dsel0, dg0],
        "middle",
        specs=[in_smem(), in_vmem()] + [rows_of(1)] * 2 + [in_vmem()] * 5,
        out_specs=[rows_of(0)] + [in_vmem()] * 5,
        grid=(1,),
        scratch=[
            ((nsel, hd), BF16),
            ((nblocks, hd), BF16),
            ((nblocks, hd), BF16),
            ((2, nblocks, LANES), F32),
            ((2, nblocks, LANES), F32),
            ((nblocks, wide), BF16),
            ((qb, nblocks, wide), BF16),
        ],
        cost=10 * nblocks * wide * qb * hd,
    )
    own1, dg1, dsel1, send = attend(1, mixed, stack1, [dc])
    home = exchange(send)
    (dz,) = call(functools.partial(dz_kernel, heads), [((2 * heads, tokens), F32)], [dz, dg1], "dz")
    (d_queries,) = call(
        functools.partial(tail_kernel, ranks, qb, heads, lists),
        [(queries.shape, BF16)],
        [me, keys, mixed, dsel1, dcomp, kct, dq],
        "tail",
        specs=[in_smem()] + [in_vmem()] * 5 + [pl.BlockSpec(memory_space=pl.ANY)],
        out_specs=[rows_of(1)],
        grid=(1,),
        scratch=[((nsel, hd), BF16)],
        aliases={6: 0},
        cost=2 * nsel * wide * 2 * hd,
    )

    part = pl.pallas_call(
        functools.partial(collect_kernel, ranks, qb, lists),
        out_shape=jax.ShapeDtypeStruct((tokens, 2 * hd), F32),
        in_specs=[in_smem(), in_smem()] + [in_vmem()] * 3,
        out_specs=in_vmem(),
        compiler_params=params(),
        name="collect",
    )(me, table, own0, own1, mixed)
    d_keys, d_values, d_ck, d_cv = pl.pallas_call(
        functools.partial(finish_kernel, ranks, qb, lists),
        out_shape=[
            jax.ShapeDtypeStruct(x.shape, BF16) for x in (keys, values, comp_keys, comp_values)
        ],
        in_specs=[in_smem(), in_smem()] + [in_vmem()] * 3,
        out_specs=[in_vmem()] * 4,
        scratch_shapes=[pltpu.VMEM((tokens, 2 * hd), F32)],
        compiler_params=params(),
        name="finish",
    )(me, table, part, dc, home)

    dz = dz.astype(BF16)
    dz_other = lax.ppermute(dz, "head", swap)
    tn = (((0,), (1,)), ((), ()))
    d_inputs = (
        lax.dot_general(dz, w_mine, tn, preferred_element_type=F32)
        + lax.dot_general(dz_other, w_other, tn, preferred_element_type=F32)
    ).astype(BF16)

    return d_queries, d_keys, d_values, d_ck, d_cv, d_inputs


def solution(mesh):
    split = P("ctx", "head")
    in_specs = (split,) * 5 + (P(), P("ctx", None), P(None, "head"), split)
    return jax.shard_map(
        body, mesh=mesh, in_specs=in_specs, out_specs=(split,) * 6, check_vma=False
    )
```

```python
import functools

import jax
import jax.numpy as jnp
from jax import lax
from jax.experimental import pallas as pl
from jax.experimental.pallas import tpu as pltpu
from jax.sharding import PartitionSpec as P

BLK = 64
PICKS = 15
LOG2E = 1.4426950408889634
LANES = 256
NEG = -1e30
F32, BF16 = jnp.float32, jnp.bfloat16


def reach_lists(ranks):
    half = ranks // 2
    even, odd = [], []
    for j in range(PICKS):
        near = 1 + j * max(half - 1, 0) // 14
        far = half + 1 + j * max(half - 2, 0) // 14
        if j == 0 or near != 1 + (j - 1) * max(half - 1, 0) // 14:
            even.append((j, near))
        if j == 0 or far != half + 1 + (j - 1) * max(half - 2, 0) // 14:
            odd.append((j, far))
    return even, odd


def in_vmem():
    return pl.BlockSpec(memory_space=pltpu.VMEM)


def in_smem():
    return pl.BlockSpec(memory_space=pltpu.SMEM)


def params(ranks, limit=16):
    return pltpu.CompilerParams(vmem_limit_bytes=(limit if ranks <= 16 else 60) * 1024 * 1024)


def fill_picks(ranks, qb, lists, p, me, sel_ref, k_ref, v_ref, out_ref):
    for parity, reach in enumerate(lists):
        for j, r in reach:
            dest = jnp.where(me + r < ranks, me + r, me)
            named = sel_ref[j, dest * qb + 2 * p + parity]
            local = jnp.clip(named - me * qb, 0, qb - 1)
            rows = pl.ds(pl.multiple_of(local * BLK, BLK), BLK)
            out_ref[dest, :BLK, :] = k_ref[rows, :]
            out_ref[dest, BLK : 2 * BLK, :] = v_ref[rows, :]


def pack_kernel(ranks, qb, lists, rank_ref, sel_ref, k_ref, v_ref, ck_ref, cv_ref, out_ref):
    hd = k_ref.shape[1]
    me = rank_ref[0]
    comp = jnp.concatenate([ck_ref[...].astype(F32), cv_ref[...].astype(F32)], axis=0).astype(BF16)

    def every(n, carry):
        out_ref[n, 2 * BLK :, :] = comp
        return carry

    lax.fori_loop(0, ranks, every, 0)
    out_ref[me, : 2 * BLK, :] = jnp.zeros((2 * BLK, hd), BF16)
    fill_picks(ranks, qb, lists, 0, me, sel_ref, k_ref, v_ref, out_ref)


def restack(heads, q_ref, do_ref, out_ref):
    hd = out_ref.shape[2] // 4
    per = LANES // BLK
    for i in range(2):
        for c in range(heads // per):
            for n, src in enumerate((q_ref, do_ref)):
                piece = jnp.concatenate(
                    [
                        src[i * BLK : (i + 1) * BLK, h * hd : (h + 1) * hd]
                        for h in range(c * per, (c + 1) * per)
                    ],
                    axis=0,
                )
                out_ref[i, c, n * hd : (n + 1) * hd, :] = turned(piece)
                out_ref[i, c, 2 * hd :, n * hd : (n + 1) * hd] = piece


def parts_of(ref, i, c):
    hd = ref.shape[2] // 4
    return (
        ref[i, c, :hd, :],
        ref[i, c, hd : 2 * hd, :],
        ref[i, c, 2 * hd :, :hd],
        ref[i, c, 2 * hd :, hd:],
    )


def prep_kernel(qb, heads, x_ref, w_ref, q_ref, do_ref, gate_ref, stack_ref):
    nt = (((1,), (1,)), ((), ()))
    z = lax.dot_general(w_ref[...], x_ref[...], nt, preferred_element_type=F32)
    zt = jax.nn.sigmoid(z)
    for i in range(qb):
        for branch in range(2):
            for h in range(heads):
                row = branch * heads + h
                gate_ref[i, branch : branch + 1, h * BLK : (h + 1) * BLK] = zt[
                    row : row + 1, i * BLK : (i + 1) * BLK
                ]
    restack(heads, q_ref, do_ref, stack_ref)


def fold(x, op):
    return op(x.reshape(x.shape[0] // 8, 8, x.shape[1]), axis=0)


def branch_grad(parts, gate, s_scr, u_scr, w_scr, d_scr):
    c2 = 128 ** -0.5 * LOG2E
    top = jnp.full((8, LANES), NEG, F32)
    for at, live, mask in parts:
        s = s_scr[at, :]
        if mask is not None:
            s = jnp.where(mask, s, NEG)
            s_scr[at, :] = s
        part = fold(s, jnp.max)
        top = jnp.maximum(top, part if live is None else jnp.where(live, part, NEG))
    top = jnp.max(top, axis=0, keepdims=True) * c2
    total = jnp.zeros((8, LANES), F32)
    mixed = jnp.zeros((8, LANES), F32)
    for at, live, mask in parts:
        e = jnp.exp2(s_scr[at, :] * c2 - (top if live is None else jnp.where(live, top, -NEG)))
        total = total + fold(e, jnp.sum)
        mixed = mixed + fold(e * u_scr[at, :], jnp.sum)
        s_scr[at, :] = e
    inv = 1.0 / jnp.sum(total, axis=0, keepdims=True)
    d_gate = jnp.sum(mixed, axis=0, keepdims=True) * inv
    weight = gate * inv
    for at, live, mask in parts:
        pw = s_scr[at, :] * weight
        w_scr[at, :] = pw.astype(BF16)
        d_scr[at, :] = (pw * (u_scr[at, :] - d_gate)).astype(BF16)
    return d_gate


def lanes_of(c):
    return slice(c * LANES, (c + 1) * LANES)


def gather(me, row, reach, own_ref, picks_ref, offset, out):
    out[:BLK, :] = own_ref[row * BLK : (row + 1) * BLK, :]
    for n, (_, r) in enumerate(reach):
        src = jnp.where(me >= r, me - r, me)
        out[(n + 1) * BLK : (n + 2) * BLK, :] = picks_ref[src, offset : offset + BLK, :]


def spread(row_vectors, columns, out_ref, heads, first_row):
    for h in range(heads):
        out_ref[first_row + h : first_row + h + 1, columns] = row_vectors[:, h * BLK : (h + 1) * BLK]


def attend_kernel(ranks, qb, heads, lists, p, *refs):
    rank_ref, sel_ref, stack, k_ref, v_ref, gate_ref, picks_ref = refs[:7]
    if p == 0:
        refs = refs[7:]
    else:
        dc_ref, *refs = refs[7:]
    own_hbm, dg_ref, dsel_hbm, send_ref, kcat, vcat, s_scr, u_scr, w_scr, dv_acc, dk_acc = refs[:11]
    own_ref, dsel_ref, sems = refs[11:]
    hd = k_ref.shape[1]
    scale = hd ** -0.5
    me = rank_ref[0]
    chunks = heads * BLK // LANES
    copies = []

    def put(src, dst):
        copy = pltpu.make_async_copy(src, dst, sems.at[len(copies)])
        copy.start()
        copies.append(copy)

    send_ref[me] = jnp.zeros(send_ref.shape[1:], BF16)
    for parity, reach in enumerate(lists):
        if (1 + len(reach)) * BLK < dsel_ref.shape[2]:
            dsel_ref[parity, :, (1 + len(reach)) * BLK :, :] = jnp.zeros(
                (dsel_ref.shape[1], dsel_ref.shape[2] - (1 + len(reach)) * BLK, LANES), BF16
            )
    if p == 0:
        fill_picks(ranks, qb, lists, 1, me, sel_ref, k_ref, v_ref, send_ref)
    else:
        for r in range(1, ranks):
            dest = jnp.where(me >= r, me - r, me)
            at = slice(r * qb, (r + 1) * qb)
            piece = jnp.concatenate([dc_ref[at, :hd], dc_ref[at, hd:]], axis=0)
            send_ref[dest, 2 * BLK :, :] = piece.astype(BF16)

    key_pos = lax.broadcasted_iota(jnp.int32, (BLK, LANES), 0)
    tok_pos = lax.rem(lax.broadcasted_iota(jnp.int32, (BLK, LANES), 1), BLK)
    causal = key_pos <= tok_pos
    parts, sizes = [], []
    for parity, reach in enumerate(lists):
        parts.append([(slice(0, BLK), None, causal)])
        for n, (_, r) in enumerate(reach):
            parts[-1].append((slice((n + 1) * BLK, (n + 2) * BLK), me >= r, None))
        sizes.append((1 + len(reach)) * BLK)

    def fetch(parity):
        row = 2 * p + parity
        gather(me, row, lists[parity], k_ref, picks_ref, 0, kcat.at[parity])
        gather(me, row, lists[parity], v_ref, picks_ref, BLK, vcat.at[parity])

    def scores(g):
        parity, c = g // chunks, g % chunks
        nk = sizes[parity]
        qt, dt, _, _ = parts_of(stack, parity, c)
        s_scr[g % 2, :nk, :] = jnp.dot(kcat[parity, :nk, :], qt, preferred_element_type=F32)
        u_scr[g % 2, :nk, :] = jnp.dot(vcat[parity, :nk, :], dt, preferred_element_type=F32)

    def soften(g):
        parity, lanes = g // chunks, lanes_of(g % chunks)
        gate = gate_ref[2 * p + parity, 1:2, lanes]
        dg = branch_grad(
            parts[parity], gate, s_scr.at[g % 2], u_scr.at[g % 2], w_scr.at[g % 2],
            dsel_ref.at[parity, g % chunks],
        )
        put(dsel_ref.at[parity, g % chunks], dsel_hbm.at[parity, g % chunks])
        dg_ref[parity : parity + 1, lanes] = dg * gate * (1.0 - gate)

    def gradients(g):
        parity, c = g // chunks, g % chunks
        nk = sizes[parity]
        _, _, qs, ds = parts_of(stack, parity, c)
        dv = jnp.dot(w_scr[g % 2, :nk, :], ds, preferred_element_type=F32)
        dk = jnp.dot(dsel_ref[parity, c, :nk, :], qs, preferred_element_type=F32)
        if c == 0:
            dv_acc[parity, :nk, :] = dv
            dk_acc[parity, :nk, :] = dk
        else:
            dv_acc[parity, :nk, :] += dv
            dk_acc[parity, :nk, :] += dk

    def deliver(parity):
        rows = slice(parity * BLK, (parity + 1) * BLK)
        own_ref[rows, :hd] = dk_acc[parity, :BLK, :] * scale
        own_ref[rows, hd:] = dv_acc[parity, :BLK, :]
        put(own_ref.at[rows], own_hbm.at[rows])
        for n, (_, r) in enumerate(lists[parity]):
            at = slice((n + 1) * BLK, (n + 2) * BLK)
            dest = jnp.where(me >= r, me - r, me)
            send_ref[dest, :BLK, :] = (dk_acc[parity, at, :] * scale).astype(BF16)
            send_ref[dest, BLK : 2 * BLK, :] = dv_acc[parity, at, :].astype(BF16)

    fetch(0)
    scores(0)
    fetch(1)
    for g in range(2 * chunks):
        if g + 1 < 2 * chunks:
            scores(g + 1)
        if g > 0:
            gradients(g - 1)
        if g == chunks:
            deliver(0)
        soften(g)
    gradients(2 * chunks - 1)
    deliver(1)
    for copy in copies:
        copy.wait()


def write_dq(row, heads, hd, pairs, dq_ref):
    per = LANES // BLK
    rows = slice(row * BLK, (row + 1) * BLK)
    for c in range(heads // per):
        total = None
        for kt, d_of in pairs:
            part = jnp.dot(kt, d_of(c), preferred_element_type=F32)
            total = part if total is None else total + part
        dq = (total.T * hd ** -0.5).astype(BF16)
        for h in range(per):
            head = c * per + h
            dq_ref[rows, head * hd : (head + 1) * hd] = dq[h * BLK : (h + 1) * BLK, :]


def turned(x):
    return x.astype(F32).T.astype(BF16)


def middle_kernel(ranks, qb, heads, lists, rank_ref, stack0, q_ref, do_ref, k_ref, gate_ref,
                  fetched_ref, dsel_ref, dg_ref, dq_ref, dz_ref, dc_ref, dcomp_ref, kct_ref,
                  stack1, kcat, ckey, cval, s_scr, u_scr, w_scr, d_scr):
    hd = k_ref.shape[1]
    me = rank_ref[0]
    nblocks = ranks * qb
    chunks = heads * BLK // LANES
    span = min(nblocks, BLK)
    pieces = []
    for r in range(ranks):
        pieces.append(fetched_ref[jnp.maximum(me - r, 0), 2 * BLK :, :].astype(F32))
    ckey[...] = jnp.concatenate([x[:qb] for x in pieces], axis=0).astype(BF16)
    cval[...] = jnp.concatenate([x[qb:] for x in pieces], axis=0).astype(BF16)
    kct_ref[...] = turned(ckey[...])
    dz_ref[...] = jnp.zeros_like(dz_ref)
    restack(heads, q_ref, do_ref, stack1)

    for row in range(qb):
        stack = stack0 if row < 2 else stack1
        parts = []
        for n in range(nblocks // span):
            place = lax.broadcasted_iota(jnp.int32, (span, LANES), 0) + n * span
            away, within = place // qb, lax.rem(place, qb)
            seen = (away <= me) & ((away > 0) | (within <= row))
            parts.append((slice(n * span, (n + 1) * span), None, seen))
        dgs, dvs, dks = [], [], []
        for c in range(chunks):
            lanes = lanes_of(c)
            qt, dt, qs, ds = parts_of(stack, row % 2, c)
            s_scr[c % 2] = jnp.dot(ckey[...], qt, preferred_element_type=F32)
            u_scr[c % 2] = jnp.dot(cval[...], dt, preferred_element_type=F32)
            gate = gate_ref[row, 0:1, lanes]
            dg = branch_grad(parts, gate, s_scr.at[c % 2], u_scr.at[c % 2], w_scr.at[:, lanes], d_scr.at[row, :, lanes])
            dgs.append(dg * gate * (1.0 - gate))
            dvs.append(jnp.dot(w_scr[:, lanes], ds, preferred_element_type=F32))
            dks.append(jnp.dot(d_scr[row, :, lanes], qs, preferred_element_type=F32))
        dv = sum(dvs[1:], dvs[0])
        dk = sum(dks[1:], dks[0]) * hd ** -0.5
        if row == 0:
            dc_ref[:, :hd] = dk
            dc_ref[:, hd:] = dv
        else:
            dc_ref[:, :hd] += dk
            dc_ref[:, hd:] += dv
        columns = slice(row * BLK, (row + 1) * BLK)
        spread(jnp.concatenate(dgs, axis=1), columns, dz_ref, heads, 0)

    for parity, reach in enumerate(lists):
        nk = (1 + len(reach)) * BLK
        gather(me, parity, reach, k_ref, fetched_ref, 0, kcat)
        write_dq(
            parity, heads, hd,
            [
                (turned(kcat[:nk, :]), lambda c, nk=nk, parity=parity: dsel_ref[parity, c, :nk, :]),
                (kct_ref[...], lambda c, parity=parity: d_scr[parity, :, lanes_of(c)]),
            ],
            dq_ref,
        )
        spread(dg_ref[parity : parity + 1, :], slice(parity * BLK, (parity + 1) * BLK), dz_ref, heads, heads)
    for i in range(2):
        dcomp_ref[i] = d_scr[2 + i]


def tail_kernel(ranks, qb, heads, lists, rank_ref, k_ref, picks_ref, dsel_ref, dcomp_ref, kct_ref, _, dq_ref, kcat):
    hd = k_ref.shape[1]
    me = rank_ref[0]
    for parity, reach in enumerate(lists):
        nk = (1 + len(reach)) * BLK
        gather(me, 2 + parity, reach, k_ref, picks_ref, 0, kcat)
        write_dq(
            parity, heads, hd,
            [
                (turned(kcat[:nk, :]), lambda c, nk=nk, parity=parity: dsel_ref[parity, c, :nk, :]),
                (kct_ref[...], lambda c, parity=parity: dcomp_ref[parity, :, lanes_of(c)]),
            ],
            dq_ref,
        )


def dz_kernel(heads, dz_in, dg_ref, dz_ref):
    dz = dz_in[...]
    dz_ref[...] = dz
    for i in range(2):
        spread(dg_ref[i : i + 1, :], slice((2 + i) * BLK, (3 + i) * BLK), dz_ref, heads, heads)


def add_homes(ranks, qb, lists, p, me, sel_ref, home_ref, acc):
    hd = home_ref.shape[2]
    for parity, reach in enumerate(lists):
        for j, r in reach:
            src = jnp.minimum(me + r, ranks - 1)
            named = sel_ref[j, src * qb + 2 * p + parity]
            local = jnp.clip(named - me * qb, 0, qb - 1)
            rows = pl.ds(pl.multiple_of(local * BLK, BLK), BLK)
            live = me + r < ranks
            acc[rows, :hd] += jnp.where(live, home_ref[src, :BLK, :].astype(F32), 0.0)
            acc[rows, hd:] += jnp.where(live, home_ref[src, BLK : 2 * BLK, :].astype(F32), 0.0)


def collect_kernel(ranks, qb, lists, rank_ref, sel_ref, own0_ref, own1_ref, home_ref, acc_ref):
    acc_ref[: 2 * BLK, :] = own0_ref[...]
    acc_ref[2 * BLK :, :] = own1_ref[...]
    add_homes(ranks, qb, lists, 0, rank_ref[0], sel_ref, home_ref, acc_ref)


def finish_kernel(ranks, qb, lists, rank_ref, sel_ref, part_ref, dc_ref, home_ref,
                  dk_ref, dv_ref, dck_ref, dcv_ref, acc):
    hd = dk_ref.shape[1]
    me = rank_ref[0]
    acc[...] = part_ref[...]
    add_homes(ranks, qb, lists, 1, me, sel_ref, home_ref, acc)
    dk_ref[...] = acc[:, :hd].astype(BF16)
    dv_ref[...] = acc[:, hd:].astype(BF16)

    def add(n, total):
        return total + home_ref[n, 2 * BLK :, :].astype(F32)

    total = lax.fori_loop(me + 1, ranks, add, jnp.zeros((2 * qb, hd), F32))
    dck_ref[...] = (total[:qb] + dc_ref[:qb, :hd]).astype(BF16)
    dcv_ref[...] = (total[qb:] + dc_ref[:qb, hd:]).astype(BF16)


def body(queries, keys, values, comp_keys, comp_values, selected, inputs, w_gate, d_out):
    tokens, width = queries.shape
    hd = keys.shape[1]
    heads = width // hd
    qb = tokens // BLK
    pair = qb // 2
    ranks = lax.axis_size("ctx")
    rank = lax.axis_index("ctx").astype(jnp.int32)
    me = rank.reshape(1)
    head = lax.axis_index("head")
    nblocks = ranks * qb
    lists = reach_lists(ranks)
    table = selected.T

    slot = 2 * BLK + 2 * qb

    def exchange(x):
        return lax.all_to_all(x, "ctx", split_axis=0, concat_axis=0, tiled=True)

    send = pl.pallas_call(
        functools.partial(pack_kernel, ranks, qb, lists),
        out_shape=jax.ShapeDtypeStruct((ranks, slot, hd), BF16),
        in_specs=[in_smem(), in_smem()] + [in_vmem()] * 4,
        out_specs=in_vmem(),
        compiler_params=params(ranks, 60),
        name="pack",
    )(me, table, keys, values, comp_keys, comp_values)
    fetched = exchange(send)

    def call(kernel, outs, args, name, scratch=(), specs=None, out_specs=None, aliases=None, cost=0, grid=(), sems=0, limit=16):
        return pl.pallas_call(
            kernel,
            grid=grid,
            out_shape=[jax.ShapeDtypeStruct(shape, dtype) for shape, dtype in outs],
            in_specs=specs or [in_vmem()] * len(args),
            out_specs=out_specs or [in_vmem()] * len(outs),
            scratch_shapes=[pltpu.VMEM(shape, dtype) for shape, dtype in scratch]
            + [pltpu.SemaphoreType.DMA((sems,))] * (sems > 0),
            input_output_aliases=aliases or {},
            compiler_params=params(ranks, limit),
            cost_estimate=pl.CostEstimate(flops=cost, bytes_accessed=4 << 20, transcendentals=0),
            name=name,
        )(*args)

    wide = heads * BLK
    chunks = wide // LANES
    stack_shape = (2, chunks, 4 * hd, LANES)

    def rows_of(p):
        return pl.BlockSpec((2 * BLK, width), lambda i: (p, 0))

    gate, stack0 = call(
        functools.partial(prep_kernel, qb, heads),
        [((qb, 2, wide), F32), (stack_shape, BF16)],
        [inputs, w_gate.T, queries, d_out],
        "prep",
        specs=[in_vmem()] * 2 + [rows_of(0)] * 2,
        grid=(1,),
        cost=2 * inputs.size * w_gate.shape[1],
    )
    half = w_gate.shape[0] // 2
    swap = [(0, 1), (1, 0)]
    w_send = lax.dynamic_slice_in_dim(w_gate, (1 - head) * half, half, 0)
    w_mine = lax.dynamic_slice_in_dim(w_gate, head * half, half, 0)
    w_other = lax.ppermute(w_send, "head", swap)

    nsel = (1 + max(len(x) for x in lists)) * BLK
    smem2 = [in_smem(), in_smem()]

    in_any = pl.BlockSpec(memory_space=pl.ANY)

    def attend(p, picks, stack, previous):
        args = [me, table, stack, keys, values, gate, picks] + previous
        own, dsel, send = (2 * BLK, 2 * hd), (2, chunks, nsel, LANES), (ranks, slot if p else 2 * BLK, hd)
        return call(
            functools.partial(attend_kernel, ranks, qb, heads, lists, p),
            [(own, F32), ((2, wide), F32), (dsel, BF16), (send, BF16)],
            args,
            f"attend{p}",
            specs=smem2 + [in_vmem()] * (len(args) - 2),
            out_specs=[in_any, in_vmem(), in_any, in_vmem()],
            scratch=[
                ((2, nsel, hd), BF16),
                ((2, nsel, hd), BF16),
                ((2, nsel, LANES), F32),
                ((2, nsel, LANES), F32),
                ((2, nsel, LANES), BF16),
                ((2, nsel, hd), F32),
                ((2, nsel, hd), F32),
                (own, F32),
                (dsel, BF16),
            ],
            sems=2 * chunks + 2,
            limit=60,
            cost=8 * nsel * wide * 2 * hd,
        )

    own0, dg0, dsel0, send = attend(0, fetched, stack0, [])
    mixed = exchange(send)
    dq, dz, dc, dcomp, kct, stack1 = call(
        functools.partial(middle_kernel, ranks, qb, heads, lists),
        [
            (queries.shape, BF16),
            ((2 * heads, tokens), F32),
            ((nblocks, 2 * hd), F32),
            ((2, nblocks, wide), BF16),
            ((hd, nblocks), BF16),
            (stack_shape, BF16),
        ],
        [me, stack0, queries, d_out, keys, gate, fetched, dsel0, dg0],
        "middle",
        specs=[in_smem(), in_vmem()] + [rows_of(1)] * 2 + [in_vmem()] * 5,
        out_specs=[rows_of(0)] + [in_vmem()] * 5,
        grid=(1,),
        scratch=[
            ((nsel, hd), BF16),
            ((nblocks, hd), BF16),
            ((nblocks, hd), BF16),
            ((2, nblocks, LANES), F32),
            ((2, nblocks, LANES), F32),
            ((nblocks, wide), BF16),
            ((qb, nblocks, wide), BF16),
        ],
        cost=10 * nblocks * wide * qb * hd,
    )
    own1, dg1, dsel1, send = attend(1, mixed, stack1, [dc])
    home = exchange(send)
    (dz,) = call(functools.partial(dz_kernel, heads), [((2 * heads, tokens), F32)], [dz, dg1], "dz")
    (d_queries,) = call(
        functools.partial(tail_kernel, ranks, qb, heads, lists),
        [(queries.shape, BF16)],
        [me, keys, mixed, dsel1, dcomp, kct, dq],
        "tail",
        specs=[in_smem()] + [in_vmem()] * 5 + [pl.BlockSpec(memory_space=pl.ANY)],
        out_specs=[rows_of(1)],
        grid=(1,),
        scratch=[((nsel, hd), BF16)],
        aliases={6: 0},
        limit=60,
        cost=2 * nsel * wide * 2 * hd,
    )

    part = pl.pallas_call(
        functools.partial(collect_kernel, ranks, qb, lists),
        out_shape=jax.ShapeDtypeStruct((tokens, 2 * hd), F32),
        in_specs=[in_smem(), in_smem()] + [in_vmem()] * 3,
        out_specs=in_vmem(),
        compiler_params=params(ranks),
        name="collect",
    )(me, table, own0, own1, mixed)
    d_keys, d_values, d_ck, d_cv = pl.pallas_call(
        functools.partial(finish_kernel, ranks, qb, lists),
        out_shape=[
            jax.ShapeDtypeStruct(x.shape, BF16) for x in (keys, values, comp_keys, comp_values)
        ],
        in_specs=[in_smem(), in_smem()] + [in_vmem()] * 3,
        out_specs=[in_vmem()] * 4,
        scratch_shapes=[pltpu.VMEM((tokens, 2 * hd), F32)],
        compiler_params=params(ranks),
        name="finish",
    )(me, table, part, dc, home)

    dz = dz.astype(BF16)
    dz_other = lax.ppermute(dz, "head", swap)
    tn = (((0,), (1,)), ((), ()))
    d_inputs = (
        lax.dot_general(dz, w_mine, tn, preferred_element_type=F32)
        + lax.dot_general(dz_other, w_other, tn, preferred_element_type=F32)
    ).astype(BF16)

    return d_queries, d_keys, d_values, d_ck, d_cv, d_inputs


def solution(mesh):
    split = P("ctx", "head")
    in_specs = (split,) * 5 + (P(), P("ctx", None), P(None, "head"), split)
    return jax.shard_map(
        body, mesh=mesh, in_specs=in_specs, out_specs=(split,) * 6, check_vma=False
    )
```

```python
import functools

import jax
import jax.numpy as jnp
from jax import lax
from jax.experimental import pallas as pl
from jax.experimental.pallas import tpu as pltpu
from jax.sharding import PartitionSpec as P

BLK = 64
PICKS = 15
LOG2E = 1.4426950408889634
LANES = 256
NEG = -1e30
F32, BF16 = jnp.float32, jnp.bfloat16


def reach_lists(ranks):
    half = ranks // 2
    even, odd = [], []
    for j in range(PICKS):
        near = 1 + j * max(half - 1, 0) // 14
        far = half + 1 + j * max(half - 2, 0) // 14
        if j == 0 or near != 1 + (j - 1) * max(half - 1, 0) // 14:
            even.append((j, near))
        if j == 0 or far != half + 1 + (j - 1) * max(half - 2, 0) // 14:
            odd.append((j, far))
    return even, odd


def in_vmem():
    return pl.BlockSpec(memory_space=pltpu.VMEM)


def in_smem():
    return pl.BlockSpec(memory_space=pltpu.SMEM)


def params(ranks, limit=16):
    return pltpu.CompilerParams(vmem_limit_bytes=(limit if ranks <= 16 else 48) * 1024 * 1024)


def fill_picks(ranks, qb, lists, p, me, sel_ref, k_ref, v_ref, out_ref):
    for parity, reach in enumerate(lists):
        for j, r in reach:
            dest = jnp.where(me + r < ranks, me + r, me)
            named = sel_ref[j, dest * qb + 2 * p + parity]
            local = jnp.clip(named - me * qb, 0, qb - 1)
            rows = pl.ds(pl.multiple_of(local * BLK, BLK), BLK)
            out_ref[dest, :BLK, :] = k_ref[rows, :]
            out_ref[dest, BLK : 2 * BLK, :] = v_ref[rows, :]


def pack_kernel(ranks, qb, lists, rank_ref, sel_ref, k_ref, v_ref, ck_ref, cv_ref, out_ref):
    hd = k_ref.shape[1]
    me = rank_ref[0]
    comp = jnp.concatenate([ck_ref[...].astype(F32), cv_ref[...].astype(F32)], axis=0).astype(BF16)

    def every(n, carry):
        out_ref[n, 2 * BLK :, :] = comp
        return carry

    lax.fori_loop(0, ranks, every, 0)
    out_ref[me, : 2 * BLK, :] = jnp.zeros((2 * BLK, hd), BF16)
    fill_picks(ranks, qb, lists, 0, me, sel_ref, k_ref, v_ref, out_ref)


def gate_kernel(qb, heads, x_ref, w_ref, q_ref, do_ref, out_ref):
    del q_ref, do_ref
    nt = (((1,), (1,)), ((), ()))
    z = lax.dot_general(w_ref[...], x_ref[...], nt, preferred_element_type=F32)
    zt = jax.nn.sigmoid(z)
    for i in range(qb):
        for branch in range(2):
            for h in range(heads):
                row = branch * heads + h
                out_ref[i, branch : branch + 1, h * BLK : (h + 1) * BLK] = zt[
                    row : row + 1, i * BLK : (i + 1) * BLK
                ]


def fold(x, op):
    return op(x.reshape(x.shape[0] // 8, 8, x.shape[1]), axis=0)


def branch_grad(parts, lanes, gate, s_scr, u_scr, w_scr, d_scr):
    c2 = 128 ** -0.5 * LOG2E
    top = jnp.full((8, LANES), NEG, F32)
    for at, live, mask in parts:
        s = s_scr[at, :]
        if mask is not None:
            s = jnp.where(mask, s, NEG)
            s_scr[at, :] = s
        part = fold(s, jnp.max)
        top = jnp.maximum(top, part if live is None else jnp.where(live, part, NEG))
    top = jnp.max(top, axis=0, keepdims=True) * c2
    total = jnp.zeros((8, LANES), F32)
    mixed = jnp.zeros((8, LANES), F32)
    for at, live, mask in parts:
        e = jnp.exp2(s_scr[at, :] * c2 - (top if live is None else jnp.where(live, top, -NEG)))
        total = total + fold(e, jnp.sum)
        mixed = mixed + fold(e * u_scr[at, :], jnp.sum)
        s_scr[at, :] = e
    inv = 1.0 / jnp.sum(total, axis=0, keepdims=True)
    d_gate = jnp.sum(mixed, axis=0, keepdims=True) * inv
    weight = gate * inv
    for at, live, mask in parts:
        pw = s_scr[at, :] * weight
        w_scr[at, lanes] = pw.astype(BF16)
        d_scr[at, lanes] = (pw * (u_scr[at, :] - d_gate)).astype(BF16)
    return d_gate


def attend_kernel(ranks, qb, heads, lists, p, *refs):
    (rank_ref, sel_ref, q_ref, do_ref, k_ref, v_ref, gate_ref, comp_ref, picks_ref) = refs[:9]
    if p == 0:
        dq_ref, own_ref, dz_ref, dc_ref, send_ref, *scratch = refs[9:]
    else:
        _, dz_in, dc_in, dq_ref, own_ref, dz_ref, dc_ref, send_ref, *scratch = refs[9:]
    hd = k_ref.shape[1]
    me = rank_ref[0]
    step = pl.program_id(0)
    dg_scr, dc_scr = scratch[-2:]

    @pl.when(step == 0)
    def _():
        if p == 0:
            dc_scr[...] = jnp.zeros_like(dc_scr)
            dz_ref[...] = jnp.zeros_like(dz_ref)
            send_ref[me] = jnp.zeros(send_ref.shape[1:], BF16)
            fill_picks(ranks, qb, lists, 1, me, sel_ref, k_ref, v_ref, send_ref)
        else:
            dc_scr[...] = dc_in[...]
            dz_ref[...] = dz_in[...]

    for parity in range(2):

        @pl.when(step == parity)
        def _(parity=parity):
            attend_row(ranks, qb, heads, lists[parity], me, 2 * p + parity, parity, q_ref, do_ref, k_ref, v_ref,
                       gate_ref, comp_ref, picks_ref, dq_ref, own_ref, send_ref, *scratch)

    @pl.when(step == 1)
    def _():
        dc_ref[...] = dc_scr[...]
        if p == 1:
            for r in range(1, ranks):

                @pl.when(me >= r)
                def _(r=r):
                    at = slice(r * qb, (r + 1) * qb)
                    piece = jnp.concatenate([dc_scr[at, :hd], dc_scr[at, hd:]], axis=0)
                    send_ref[me - r, 2 * BLK :, :] = piece.astype(BF16)

        for i in range(2):
            for branch in range(2):
                for h in range(heads):
                    row = branch * heads + h
                    lane = (2 * p + i) * BLK
                    dz_ref[row : row + 1, lane : lane + BLK] = dg_scr[
                        i, branch : branch + 1, h * BLK : (h + 1) * BLK
                    ]


def attend_row(ranks, qb, heads, reach, me, row, parity, q_ref, do_ref, k_ref, v_ref, gate_ref,
               comp_ref, picks_ref, dq_ref, own_ref, send_ref, kcat, vcat, kt, qs, ds,
               s_scr, u_scr, w_scr, d_scr, dv_acc, dk_acc, dg_scr, dc_scr):
    npick = len(reach)
    hd = k_ref.shape[1]
    nblocks = ranks * qb
    nsel = (1 + npick) * BLK
    nk = nsel + nblocks
    per = LANES // BLK
    scale = hd ** -0.5

    pieces = []
    for r in range(ranks):
        pieces.append(comp_ref[jnp.maximum(me - r, 0)].astype(F32))
    kcat[nsel:nk, :] = jnp.concatenate([x[:qb] for x in pieces], axis=0).astype(BF16)
    vcat[nsel:nk, :] = jnp.concatenate([x[qb:] for x in pieces], axis=0).astype(BF16)
    kcat[:BLK, :] = k_ref[row * BLK : (row + 1) * BLK, :]
    vcat[:BLK, :] = v_ref[row * BLK : (row + 1) * BLK, :]
    for n, (_, r) in enumerate(reach):
        src = jnp.where(me >= r, me - r, me)
        kcat[(n + 1) * BLK : (n + 2) * BLK, :] = picks_ref[src, :BLK, :]
        vcat[(n + 1) * BLK : (n + 2) * BLK, :] = picks_ref[src, BLK : 2 * BLK, :]
    kt[:, :nk] = kcat[:nk, :].astype(F32).T.astype(BF16)
    for h in range(heads):
        qs[h * BLK : (h + 1) * BLK, :] = q_ref[:, h * hd : (h + 1) * hd]
        ds[h * BLK : (h + 1) * BLK, :] = do_ref[:, h * hd : (h + 1) * hd]

    key_pos = lax.broadcasted_iota(jnp.int32, (BLK, LANES), 0)
    tok_pos = lax.rem(lax.broadcasted_iota(jnp.int32, (BLK, LANES), 1), BLK)
    sel_parts = [(slice(0, BLK), None, key_pos <= tok_pos)]
    for n, (_, r) in enumerate(reach):
        sel_parts.append((slice((n + 1) * BLK, (n + 2) * BLK), me >= r, None))
    comp_parts = []
    span = min(nblocks, BLK)
    for n in range(nblocks // span):
        place = lax.broadcasted_iota(jnp.int32, (span, LANES), 0) + n * span
        away, within = place // qb, lax.rem(place, qb)
        seen = (away <= me) & ((away > 0) | (within <= row))
        comp_parts.append((slice(nsel + n * span, nsel + (n + 1) * span), None, seen))

    nt = (((1,), (1,)), ((), ()))
    chunks = heads // per

    def lanes_of(c):
        return slice(c * LANES, (c + 1) * LANES)

    def scores(c):
        lanes = lanes_of(c)
        s_scr[c % 2, :nk, :] = lax.dot_general(kcat[:nk, :], qs[lanes, :], nt, preferred_element_type=F32)
        u_scr[c % 2, :nk, :] = lax.dot_general(vcat[:nk, :], ds[lanes, :], nt, preferred_element_type=F32)

    def soften(c):
        lanes = lanes_of(c)
        work = (s_scr.at[c % 2], u_scr.at[c % 2], w_scr, d_scr)
        for branch, parts in ((1, sel_parts), (0, comp_parts)):
            gate = gate_ref[0, branch : branch + 1, lanes]
            dg = branch_grad(parts, lanes, gate, *work)
            dg_scr[parity, branch : branch + 1, lanes] = dg * gate * (1.0 - gate)

    def gradients(c):
        lanes = lanes_of(c)
        dv = jnp.dot(w_scr[:nk, lanes], ds[lanes, :], preferred_element_type=F32)
        dk = jnp.dot(d_scr[:nk, lanes], qs[lanes, :], preferred_element_type=F32)
        if c == 0:
            dv_acc[:nk, :] = dv
            dk_acc[:nk, :] = dk
        else:
            dv_acc[:nk, :] += dv
            dk_acc[:nk, :] += dk
        dqt = jnp.dot(kt[:, :nk], d_scr[:nk, lanes], preferred_element_type=F32)
        dq = (dqt.T * scale).astype(BF16)
        for h in range(per):
            head = c * per + h
            dq_ref[:, head * hd : (head + 1) * hd] = dq[h * BLK : (h + 1) * BLK, :]

    scores(0)
    for c in range(chunks):
        if c + 1 < chunks:
            scores(c + 1)
        if c > 0:
            gradients(c - 1)
        soften(c)
    gradients(chunks - 1)

    own_ref[parity * BLK : (parity + 1) * BLK, :hd] = dk_acc[:BLK, :] * scale
    own_ref[parity * BLK : (parity + 1) * BLK, hd:] = dv_acc[:BLK, :]
    dc_scr[:, :hd] += dk_acc[nsel:nk, :] * scale
    dc_scr[:, hd:] += dv_acc[nsel:nk, :]
    for n, (_, r) in enumerate(reach):
        at = slice((n + 1) * BLK, (n + 2) * BLK)
        dest = jnp.where(me >= r, me - r, me)
        send_ref[dest, :BLK, :] = (dk_acc[at, :] * scale).astype(BF16)
        send_ref[dest, BLK : 2 * BLK, :] = dv_acc[at, :].astype(BF16)


def add_homes(ranks, qb, lists, p, me, sel_ref, home_ref, acc):
    hd = home_ref.shape[2]
    for parity, reach in enumerate(lists):
        for j, r in reach:
            src = jnp.minimum(me + r, ranks - 1)
            named = sel_ref[j, src * qb + 2 * p + parity]
            local = jnp.clip(named - me * qb, 0, qb - 1)
            rows = pl.ds(pl.multiple_of(local * BLK, BLK), BLK)
            live = me + r < ranks
            acc[rows, :hd] += jnp.where(live, home_ref[src, :BLK, :].astype(F32), 0.0)
            acc[rows, hd:] += jnp.where(live, home_ref[src, BLK : 2 * BLK, :].astype(F32), 0.0)


def collect_kernel(ranks, qb, lists, rank_ref, sel_ref, own0_ref, own1_ref, home_ref, acc_ref):
    acc_ref[: 2 * BLK, :] = own0_ref[...]
    acc_ref[2 * BLK :, :] = own1_ref[...]
    add_homes(ranks, qb, lists, 0, rank_ref[0], sel_ref, home_ref, acc_ref)


def finish_kernel(ranks, qb, lists, rank_ref, sel_ref, part_ref, dc_ref, home_ref,
                  dk_ref, dv_ref, dck_ref, dcv_ref, acc):
    hd = dk_ref.shape[1]
    me = rank_ref[0]
    acc[...] = part_ref[...]
    add_homes(ranks, qb, lists, 1, me, sel_ref, home_ref, acc)
    dk_ref[...] = acc[:, :hd].astype(BF16)
    dv_ref[...] = acc[:, hd:].astype(BF16)

    def add(n, total):
        return total + home_ref[n, 2 * BLK :, :].astype(F32)

    total = lax.fori_loop(me + 1, ranks, add, jnp.zeros((2 * qb, hd), F32))
    dck_ref[...] = (total[:qb] + dc_ref[:qb, :hd]).astype(BF16)
    dcv_ref[...] = (total[qb:] + dc_ref[:qb, hd:]).astype(BF16)


def body(queries, keys, values, comp_keys, comp_values, selected, inputs, w_gate, d_out):
    tokens, width = queries.shape
    hd = keys.shape[1]
    heads = width // hd
    qb = tokens // BLK
    pair = qb // 2
    ranks = lax.axis_size("ctx")
    rank = lax.axis_index("ctx").astype(jnp.int32)
    me = rank.reshape(1)
    head = lax.axis_index("head")
    nblocks = ranks * qb
    lists = reach_lists(ranks)
    table = selected.T

    slot = 2 * BLK + 2 * qb

    def exchange(x):
        return lax.all_to_all(x, "ctx", split_axis=0, concat_axis=0, tiled=True)

    send = pl.pallas_call(
        functools.partial(pack_kernel, ranks, qb, lists),
        out_shape=jax.ShapeDtypeStruct((ranks, slot, hd), BF16),
        in_specs=[in_smem(), in_smem()] + [in_vmem()] * 4,
        out_specs=in_vmem(),
        compiler_params=params(ranks, 56),
        name="pack",
    )(me, table, keys, values, comp_keys, comp_values)
    fetched = exchange(send)

    gate = pl.pallas_call(
        functools.partial(gate_kernel, qb, heads),
        out_shape=jax.ShapeDtypeStruct((qb, 2, heads * BLK), F32),
        in_specs=[in_vmem()] * 4,
        out_specs=in_vmem(),
        compiler_params=params(ranks),
        cost_estimate=pl.CostEstimate(
            flops=2 * inputs.size * w_gate.shape[1], bytes_accessed=2 * inputs.size, transcendentals=0
        ),
        name="gate",
    )(inputs, w_gate.T, queries, d_out)
    half = w_gate.shape[0] // 2
    swap = [(0, 1), (1, 0)]
    w_send = lax.dynamic_slice_in_dim(w_gate, (1 - head) * half, half, 0)
    w_mine = lax.dynamic_slice_in_dim(w_gate, head * half, half, 0)
    w_other = lax.ppermute(w_send, "head", swap)

    nk = (1 + max(len(x) for x in lists)) * BLK + nblocks

    def attend(p, picks, previous):
        row = lambda i: (2 * p + i, 0)
        out_slot = slot if p else 2 * BLK
        args = [me, table, queries, d_out, keys, values, gate, fetched, picks] + previous
        in_specs = [
            in_smem(),
            in_smem(),
            pl.BlockSpec((BLK, width), row),
            pl.BlockSpec((BLK, width), row),
            in_vmem(),
            in_vmem(),
            pl.BlockSpec((1, 2, heads * BLK), lambda i: (2 * p + i, 0, 0)),
            pl.BlockSpec((ranks, 2 * qb, hd), lambda i: (0, 2 * BLK // (2 * qb), 0)),
            pl.BlockSpec((ranks, 2 * BLK, hd), lambda i: (0, 0, 0)),
        ]
        if previous:
            in_specs += [pl.BlockSpec(memory_space=pl.ANY), in_vmem(), in_vmem()]
        return pl.pallas_call(
            functools.partial(attend_kernel, ranks, qb, heads, lists, p),
            grid=(2,),
            out_shape=[
                jax.ShapeDtypeStruct(queries.shape, BF16),
                jax.ShapeDtypeStruct((2 * BLK, 2 * hd), F32),
                jax.ShapeDtypeStruct((2 * heads, tokens), F32),
                jax.ShapeDtypeStruct((nblocks, 2 * hd), F32),
                jax.ShapeDtypeStruct((ranks, out_slot, hd), BF16),
            ],
            in_specs=in_specs,
            out_specs=[pl.BlockSpec((BLK, width), row)] + [in_vmem()] * 4,
            scratch_shapes=[
                pltpu.VMEM((nk, hd), BF16),
                pltpu.VMEM((nk, hd), BF16),
                pltpu.VMEM((hd, nk), BF16),
                pltpu.VMEM((heads * BLK, hd), BF16),
                pltpu.VMEM((heads * BLK, hd), BF16),
                pltpu.VMEM((2, nk, LANES), F32),
                pltpu.VMEM((2, nk, LANES), F32),
                pltpu.VMEM((nk, heads * BLK), BF16),
                pltpu.VMEM((nk, heads * BLK), BF16),
                pltpu.VMEM((nk, hd), F32),
                pltpu.VMEM((nk, hd), F32),
                pltpu.VMEM((2, 2, heads * BLK), F32),
                pltpu.VMEM((nblocks, 2 * hd), F32),
            ],
            input_output_aliases={9: 0} if previous else {},
            compiler_params=params(ranks),
            cost_estimate=pl.CostEstimate(
                flops=10 * nk * heads * 2 * BLK * hd, bytes_accessed=4 << 20, transcendentals=0
            ),
            name=f"attend{p}",
        )(*args)

    dq, own0, dz, dc, send = attend(0, fetched, [])
    mixed = exchange(send)
    d_queries, own1, dz, dc, send = attend(1, mixed, [dq, dz, dc])
    home = exchange(send)

    part = pl.pallas_call(
        functools.partial(collect_kernel, ranks, qb, lists),
        out_shape=jax.ShapeDtypeStruct((tokens, 2 * hd), F32),
        in_specs=[in_smem(), in_smem()] + [in_vmem()] * 3,
        out_specs=in_vmem(),
        compiler_params=params(ranks),
        name="collect",
    )(me, table, own0, own1, mixed)
    d_keys, d_values, d_ck, d_cv = pl.pallas_call(
        functools.partial(finish_kernel, ranks, qb, lists),
        out_shape=[
            jax.ShapeDtypeStruct(x.shape, BF16) for x in (keys, values, comp_keys, comp_values)
        ],
        in_specs=[in_smem(), in_smem()] + [in_vmem()] * 3,
        out_specs=[in_vmem()] * 4,
        scratch_shapes=[pltpu.VMEM((tokens, 2 * hd), F32)],
        compiler_params=params(ranks),
        name="finish",
    )(me, table, part, dc, home)

    dz = dz.astype(BF16)
    dz_other = lax.ppermute(dz, "head", swap)
    tn = (((0,), (1,)), ((), ()))
    d_inputs = (
        lax.dot_general(dz, w_mine, tn, preferred_element_type=F32)
        + lax.dot_general(dz_other, w_other, tn, preferred_element_type=F32)
    ).astype(BF16)

    return d_queries, d_keys, d_values, d_ck, d_cv, d_inputs


def solution(mesh):
    split = P("ctx", "head")
    in_specs = (split,) * 5 + (P(), P("ctx", None), P(None, "head"), split)
    return jax.shard_map(
        body, mesh=mesh, in_specs=in_specs, out_specs=(split,) * 6, check_vma=False
    )
```

```python
import functools

import jax
import jax.numpy as jnp
from jax import lax
from jax.experimental import pallas as pl
from jax.experimental.pallas import tpu as pltpu
from jax.sharding import PartitionSpec as P

BLK = 64
PICKS = 15
LOG2E = 1.4426950408889634
LANES = 256
NEG = -1e30
F32, BF16 = jnp.float32, jnp.bfloat16


def reach_lists(ranks):
    half = ranks // 2
    even, odd = [], []
    for j in range(PICKS):
        near = 1 + j * max(half - 1, 0) // 14
        far = half + 1 + j * max(half - 2, 0) // 14
        if j == 0 or near != 1 + (j - 1) * max(half - 1, 0) // 14:
            even.append((j, near))
        if j == 0 or far != half + 1 + (j - 1) * max(half - 2, 0) // 14:
            odd.append((j, far))
    return even, odd


def in_vmem():
    return pl.BlockSpec(memory_space=pltpu.VMEM)


def in_smem():
    return pl.BlockSpec(memory_space=pltpu.SMEM)


def params(ranks, limit=16):
    return pltpu.CompilerParams(vmem_limit_bytes=(limit if ranks <= 16 else 48) * 1024 * 1024)


def fill_picks(ranks, qb, lists, p, me, sel_ref, k_ref, v_ref, out_ref):
    for parity, reach in enumerate(lists):
        for j, r in reach:
            dest = jnp.where(me + r < ranks, me + r, me)
            named = sel_ref[j, dest * qb + 2 * p + parity]
            local = jnp.clip(named - me * qb, 0, qb - 1)
            rows = pl.ds(pl.multiple_of(local * BLK, BLK), BLK)
            out_ref[dest, :BLK, :] = k_ref[rows, :]
            out_ref[dest, BLK : 2 * BLK, :] = v_ref[rows, :]


def pack_kernel(ranks, qb, lists, rank_ref, sel_ref, k_ref, v_ref, ck_ref, cv_ref, out_ref):
    hd = k_ref.shape[1]
    me = rank_ref[0]
    comp = jnp.concatenate([ck_ref[...].astype(F32), cv_ref[...].astype(F32)], axis=0).astype(BF16)

    def every(n, carry):
        out_ref[n, 2 * BLK :, :] = comp
        return carry

    lax.fori_loop(0, ranks, every, 0)
    out_ref[me, : 2 * BLK, :] = jnp.zeros((2 * BLK, hd), BF16)
    fill_picks(ranks, qb, lists, 0, me, sel_ref, k_ref, v_ref, out_ref)


def gate_kernel(qb, heads, x_ref, w_ref, out_ref):
    nt = (((1,), (1,)), ((), ()))
    z = lax.dot_general(w_ref[...], x_ref[...], nt, preferred_element_type=F32)
    zt = jax.nn.sigmoid(z)
    for i in range(qb):
        for branch in range(2):
            for h in range(heads):
                row = branch * heads + h
                out_ref[i, branch : branch + 1, h * BLK : (h + 1) * BLK] = zt[
                    row : row + 1, i * BLK : (i + 1) * BLK
                ]


def fold(x, op):
    return op(x.reshape(x.shape[0] // 8, 8, x.shape[1]), axis=0)


def branch_grad(parts, lanes, gate, s_scr, u_scr, w_scr, d_scr):
    c2 = 128 ** -0.5 * LOG2E
    top = jnp.full((8, LANES), NEG, F32)
    for at, live, mask in parts:
        s = s_scr[at, :]
        if mask is not None:
            s = jnp.where(mask, s, NEG)
            s_scr[at, :] = s
        part = fold(s, jnp.max)
        top = jnp.maximum(top, part if live is None else jnp.where(live, part, NEG))
    top = jnp.max(top, axis=0, keepdims=True) * c2
    total = jnp.zeros((8, LANES), F32)
    mixed = jnp.zeros((8, LANES), F32)
    for at, live, mask in parts:
        e = jnp.exp2(s_scr[at, :] * c2 - (top if live is None else jnp.where(live, top, -NEG)))
        total = total + fold(e, jnp.sum)
        mixed = mixed + fold(e * u_scr[at, :], jnp.sum)
        s_scr[at, :] = e
    inv = 1.0 / jnp.sum(total, axis=0, keepdims=True)
    d_gate = jnp.sum(mixed, axis=0, keepdims=True) * inv
    weight = gate * inv
    for at, live, mask in parts:
        pw = s_scr[at, :] * weight
        w_scr[at, lanes] = pw.astype(BF16)
        d_scr[at, lanes] = (pw * (u_scr[at, :] - d_gate)).astype(BF16)
    return d_gate


def attend_kernel(ranks, qb, heads, lists, p, *refs):
    (rank_ref, sel_ref, q_ref, do_ref, k_ref, v_ref, gate_ref, comp_ref, picks_ref) = refs[:9]
    if p == 0:
        dq_ref, own_ref, dz_ref, dc_ref, send_ref, *scratch = refs[9:]
    else:
        _, dz_in, dc_in, own_in, dq_ref, own_ref, dz_ref, dc_ref, send_ref, *scratch = refs[9:]
    hd = k_ref.shape[1]
    me = rank_ref[0]
    step = pl.program_id(0)
    dg_scr, dc_scr = scratch[-2:]

    @pl.when(step == 0)
    def _():
        if p == 0:
            dc_scr[...] = jnp.zeros_like(dc_scr)
            dz_ref[...] = jnp.zeros_like(dz_ref)
            send_ref[me] = jnp.zeros(send_ref.shape[1:], BF16)
            fill_picks(ranks, qb, lists, 1, me, sel_ref, k_ref, v_ref, send_ref)
        else:
            dc_scr[...] = dc_in[...]
            dz_ref[...] = dz_in[...]
            own_ref[: 2 * BLK, :] = own_in[...]
            own_ref[2 * BLK :, :] = jnp.zeros((own_ref.shape[0] - 2 * BLK, own_ref.shape[1]), F32)
            add_homes(ranks, qb, lists, 0, me, sel_ref, picks_ref, own_ref)

    for parity in range(2):

        @pl.when(step == parity)
        def _(parity=parity):
            attend_row(ranks, qb, heads, lists[parity], me, 2 * p + parity, parity, q_ref, do_ref, k_ref, v_ref,
                       gate_ref, comp_ref, picks_ref, dq_ref, own_ref, send_ref, *scratch)

    @pl.when(step == 1)
    def _():
        dc_ref[...] = dc_scr[...]
        if p == 1:
            for r in range(1, ranks):

                @pl.when(me >= r)
                def _(r=r):
                    at = slice(r * qb, (r + 1) * qb)
                    piece = jnp.concatenate([dc_scr[at, :hd], dc_scr[at, hd:]], axis=0)
                    send_ref[me - r, 2 * BLK :, :] = piece.astype(BF16)

        for i in range(2):
            for branch in range(2):
                for h in range(heads):
                    row = branch * heads + h
                    lane = (2 * p + i) * BLK
                    dz_ref[row : row + 1, lane : lane + BLK] = dg_scr[
                        i, branch : branch + 1, h * BLK : (h + 1) * BLK
                    ]


def attend_row(ranks, qb, heads, reach, me, row, parity, q_ref, do_ref, k_ref, v_ref, gate_ref,
               comp_ref, picks_ref, dq_ref, own_ref, send_ref, kcat, vcat, kt, qs, ds,
               s_scr, u_scr, w_scr, d_scr, dv_acc, dk_acc, dg_scr, dc_scr):
    npick = len(reach)
    hd = k_ref.shape[1]
    nblocks = ranks * qb
    nsel = (1 + npick) * BLK
    nk = nsel + nblocks
    per = LANES // BLK
    scale = hd ** -0.5

    pieces = []
    for r in range(ranks):
        pieces.append(comp_ref[jnp.maximum(me - r, 0)].astype(F32))
    kcat[nsel:nk, :] = jnp.concatenate([x[:qb] for x in pieces], axis=0).astype(BF16)
    vcat[nsel:nk, :] = jnp.concatenate([x[qb:] for x in pieces], axis=0).astype(BF16)
    kcat[:BLK, :] = k_ref[row * BLK : (row + 1) * BLK, :]
    vcat[:BLK, :] = v_ref[row * BLK : (row + 1) * BLK, :]
    for n, (_, r) in enumerate(reach):
        src = jnp.where(me >= r, me - r, me)
        kcat[(n + 1) * BLK : (n + 2) * BLK, :] = picks_ref[src, :BLK, :]
        vcat[(n + 1) * BLK : (n + 2) * BLK, :] = picks_ref[src, BLK : 2 * BLK, :]
    kt[:, :nk] = kcat[:nk, :].astype(F32).T.astype(BF16)
    for h in range(heads):
        qs[h * BLK : (h + 1) * BLK, :] = q_ref[:, h * hd : (h + 1) * hd]
        ds[h * BLK : (h + 1) * BLK, :] = do_ref[:, h * hd : (h + 1) * hd]

    key_pos = lax.broadcasted_iota(jnp.int32, (BLK, LANES), 0)
    tok_pos = lax.rem(lax.broadcasted_iota(jnp.int32, (BLK, LANES), 1), BLK)
    sel_parts = [(slice(0, BLK), None, key_pos <= tok_pos)]
    for n, (_, r) in enumerate(reach):
        sel_parts.append((slice((n + 1) * BLK, (n + 2) * BLK), me >= r, None))
    comp_parts = []
    span = min(nblocks, BLK)
    for n in range(nblocks // span):
        place = lax.broadcasted_iota(jnp.int32, (span, LANES), 0) + n * span
        away, within = place // qb, lax.rem(place, qb)
        seen = (away <= me) & ((away > 0) | (within <= row))
        comp_parts.append((slice(nsel + n * span, nsel + (n + 1) * span), None, seen))

    nt = (((1,), (1,)), ((), ()))
    chunks = heads // per

    def lanes_of(c):
        return slice(c * LANES, (c + 1) * LANES)

    def scores(c):
        lanes = lanes_of(c)
        s_scr[c % 2, :nk, :] = lax.dot_general(kcat[:nk, :], qs[lanes, :], nt, preferred_element_type=F32)
        u_scr[c % 2, :nk, :] = lax.dot_general(vcat[:nk, :], ds[lanes, :], nt, preferred_element_type=F32)

    def soften(c):
        lanes = lanes_of(c)
        work = (s_scr.at[c % 2], u_scr.at[c % 2], w_scr, d_scr)
        for branch, parts in ((1, sel_parts), (0, comp_parts)):
            gate = gate_ref[0, branch : branch + 1, lanes]
            dg = branch_grad(parts, lanes, gate, *work)
            dg_scr[parity, branch : branch + 1, lanes] = dg * gate * (1.0 - gate)

    def gradients(c):
        lanes = lanes_of(c)
        dv = jnp.dot(w_scr[:nk, lanes], ds[lanes, :], preferred_element_type=F32)
        dk = jnp.dot(d_scr[:nk, lanes], qs[lanes, :], preferred_element_type=F32)
        if c == 0:
            dv_acc[:nk, :] = dv
            dk_acc[:nk, :] = dk
        else:
            dv_acc[:nk, :] += dv
            dk_acc[:nk, :] += dk
        dqt = jnp.dot(kt[:, :nk], d_scr[:nk, lanes], preferred_element_type=F32)
        dq = (dqt.T * scale).astype(BF16)
        for h in range(per):
            head = c * per + h
            dq_ref[:, head * hd : (head + 1) * hd] = dq[h * BLK : (h + 1) * BLK, :]

    scores(0)
    for c in range(chunks):
        if c + 1 < chunks:
            scores(c + 1)
        if c > 0:
            gradients(c - 1)
        soften(c)
    gradients(chunks - 1)

    own = slice(row * BLK, (row + 1) * BLK)
    if row < 2:
        own_ref[own, :hd] = dk_acc[:BLK, :] * scale
        own_ref[own, hd:] = dv_acc[:BLK, :]
    else:
        own_ref[own, :hd] += dk_acc[:BLK, :] * scale
        own_ref[own, hd:] += dv_acc[:BLK, :]
    dc_scr[:, :hd] += dk_acc[nsel:nk, :] * scale
    dc_scr[:, hd:] += dv_acc[nsel:nk, :]
    for n, (_, r) in enumerate(reach):
        at = slice((n + 1) * BLK, (n + 2) * BLK)
        dest = jnp.where(me >= r, me - r, me)
        send_ref[dest, :BLK, :] = (dk_acc[at, :] * scale).astype(BF16)
        send_ref[dest, BLK : 2 * BLK, :] = dv_acc[at, :].astype(BF16)


def add_homes(ranks, qb, lists, p, me, sel_ref, home_ref, acc):
    hd = home_ref.shape[2]
    for parity, reach in enumerate(lists):
        for j, r in reach:
            src = jnp.minimum(me + r, ranks - 1)
            named = sel_ref[j, src * qb + 2 * p + parity]
            local = jnp.clip(named - me * qb, 0, qb - 1)
            rows = pl.ds(pl.multiple_of(local * BLK, BLK), BLK)
            live = me + r < ranks
            acc[rows, :hd] += jnp.where(live, home_ref[src, :BLK, :].astype(F32), 0.0)
            acc[rows, hd:] += jnp.where(live, home_ref[src, BLK : 2 * BLK, :].astype(F32), 0.0)


def finish_kernel(ranks, qb, lists, rank_ref, sel_ref, part_ref, dc_ref, home_ref,
                  dk_ref, dv_ref, dck_ref, dcv_ref, acc):
    hd = dk_ref.shape[1]
    me = rank_ref[0]
    acc[...] = part_ref[...]
    add_homes(ranks, qb, lists, 1, me, sel_ref, home_ref, acc)
    dk_ref[...] = acc[:, :hd].astype(BF16)
    dv_ref[...] = acc[:, hd:].astype(BF16)

    def add(n, total):
        return total + home_ref[n, 2 * BLK :, :].astype(F32)

    total = lax.fori_loop(me + 1, ranks, add, jnp.zeros((2 * qb, hd), F32))
    dck_ref[...] = (total[:qb] + dc_ref[:qb, :hd]).astype(BF16)
    dcv_ref[...] = (total[qb:] + dc_ref[:qb, hd:]).astype(BF16)


def body(queries, keys, values, comp_keys, comp_values, selected, inputs, w_gate, d_out):
    tokens, width = queries.shape
    hd = keys.shape[1]
    heads = width // hd
    qb = tokens // BLK
    pair = qb // 2
    ranks = lax.axis_size("ctx")
    rank = lax.axis_index("ctx").astype(jnp.int32)
    me = rank.reshape(1)
    head = lax.axis_index("head")
    nblocks = ranks * qb
    lists = reach_lists(ranks)
    table = selected.T

    slot = 2 * BLK + 2 * qb

    def exchange(x):
        return lax.all_to_all(x, "ctx", split_axis=0, concat_axis=0, tiled=True)

    send = pl.pallas_call(
        functools.partial(pack_kernel, ranks, qb, lists),
        out_shape=jax.ShapeDtypeStruct((ranks, slot, hd), BF16),
        in_specs=[in_smem(), in_smem()] + [in_vmem()] * 4,
        out_specs=in_vmem(),
        compiler_params=params(ranks, 56),
        name="pack",
    )(me, table, keys, values, comp_keys, comp_values)
    fetched = exchange(send)

    gate = pl.pallas_call(
        functools.partial(gate_kernel, qb, heads),
        out_shape=jax.ShapeDtypeStruct((qb, 2, heads * BLK), F32),
        in_specs=[in_vmem()] * 2,
        out_specs=in_vmem(),
        compiler_params=params(ranks, 60),
        cost_estimate=pl.CostEstimate(
            flops=2 * inputs.size * w_gate.shape[1], bytes_accessed=2 * inputs.size, transcendentals=0
        ),
        name="gate",
    )(inputs, w_gate.T)
    half = w_gate.shape[0] // 2
    swap = [(0, 1), (1, 0)]
    w_send = lax.dynamic_slice_in_dim(w_gate, (1 - head) * half, half, 0)
    w_mine = lax.dynamic_slice_in_dim(w_gate, head * half, half, 0)
    w_other = lax.ppermute(w_send, "head", swap)

    nk = (1 + max(len(x) for x in lists)) * BLK + nblocks

    def attend(p, picks, previous):
        row = lambda i: (2 * p + i, 0)
        out_slot = slot if p else 2 * BLK
        args = [me, table, queries, d_out, keys, values, gate, fetched, picks] + previous
        in_specs = [
            in_smem(),
            in_smem(),
            pl.BlockSpec((BLK, width), row),
            pl.BlockSpec((BLK, width), row),
            in_vmem(),
            in_vmem(),
            pl.BlockSpec((1, 2, heads * BLK), lambda i: (2 * p + i, 0, 0)),
            pl.BlockSpec((ranks, 2 * qb, hd), lambda i: (0, 2 * BLK // (2 * qb), 0)),
            pl.BlockSpec((ranks, 2 * BLK, hd), lambda i: (0, 0, 0)),
        ]
        if previous:
            in_specs += [pl.BlockSpec(memory_space=pl.ANY)] + [in_vmem()] * 3
        return pl.pallas_call(
            functools.partial(attend_kernel, ranks, qb, heads, lists, p),
            grid=(2,),
            out_shape=[
                jax.ShapeDtypeStruct(queries.shape, BF16),
                jax.ShapeDtypeStruct((tokens if p else 2 * BLK, 2 * hd), F32),
                jax.ShapeDtypeStruct((2 * heads, tokens), F32),
                jax.ShapeDtypeStruct((nblocks, 2 * hd), F32),
                jax.ShapeDtypeStruct((ranks, out_slot, hd), BF16),
            ],
            in_specs=in_specs,
            out_specs=[pl.BlockSpec((BLK, width), row)] + [in_vmem()] * 4,
            scratch_shapes=[
                pltpu.VMEM((nk, hd), BF16),
                pltpu.VMEM((nk, hd), BF16),
                pltpu.VMEM((hd, nk), BF16),
                pltpu.VMEM((heads * BLK, hd), BF16),
                pltpu.VMEM((heads * BLK, hd), BF16),
                pltpu.VMEM((2, nk, LANES), F32),
                pltpu.VMEM((2, nk, LANES), F32),
                pltpu.VMEM((nk, heads * BLK), BF16),
                pltpu.VMEM((nk, heads * BLK), BF16),
                pltpu.VMEM((nk, hd), F32),
                pltpu.VMEM((nk, hd), F32),
                pltpu.VMEM((2, 2, heads * BLK), F32),
                pltpu.VMEM((nblocks, 2 * hd), F32),
            ],
            input_output_aliases={9: 0} if previous else {},
            compiler_params=params(ranks),
            cost_estimate=pl.CostEstimate(
                flops=10 * nk * heads * 2 * BLK * hd, bytes_accessed=4 << 20, transcendentals=0
            ),
            name=f"attend{p}",
        )(*args)

    dq, own0, dz, dc, send = attend(0, fetched, [])
    mixed = exchange(send)
    d_queries, part, dz, dc, send = attend(1, mixed, [dq, dz, dc, own0])
    home = exchange(send)

    d_keys, d_values, d_ck, d_cv = pl.pallas_call(
        functools.partial(finish_kernel, ranks, qb, lists),
        out_shape=[
            jax.ShapeDtypeStruct(x.shape, BF16) for x in (keys, values, comp_keys, comp_values)
        ],
        in_specs=[in_smem(), in_smem()] + [in_vmem()] * 3,
        out_specs=[in_vmem()] * 4,
        scratch_shapes=[pltpu.VMEM((tokens, 2 * hd), F32)],
        compiler_params=params(ranks),
        name="finish",
    )(me, table, part, dc, home)

    dz = dz.astype(BF16)
    dz_other = lax.ppermute(dz, "head", swap)
    tn = (((0,), (1,)), ((), ()))
    d_inputs = (
        lax.dot_general(dz, w_mine, tn, preferred_element_type=F32)
        + lax.dot_general(dz_other, w_other, tn, preferred_element_type=F32)
    ).astype(BF16)

    return d_queries, d_keys, d_values, d_ck, d_cv, d_inputs


def solution(mesh):
    split = P("ctx", "head")
    in_specs = (split,) * 5 + (P(), P("ctx", None), P(None, "head"), split)
    return jax.shard_map(
        body, mesh=mesh, in_specs=in_specs, out_specs=(split,) * 6, check_vma=False
    )
```

```python
import functools

import jax
import jax.numpy as jnp
from jax import lax
from jax.experimental import pallas as pl
from jax.experimental.pallas import tpu as pltpu
from jax.sharding import PartitionSpec as P

BLK = 64
PICKS = 15
LOG2E = 1.4426950408889634
LANES = 256
NEG = -1e30
F32, BF16 = jnp.float32, jnp.bfloat16


def reach_lists(ranks):
    half = ranks // 2
    even, odd = [], []
    for j in range(PICKS):
        near = 1 + j * max(half - 1, 0) // 14
        far = half + 1 + j * max(half - 2, 0) // 14
        if j == 0 or near != 1 + (j - 1) * max(half - 1, 0) // 14:
            even.append((j, near))
        if j == 0 or far != half + 1 + (j - 1) * max(half - 2, 0) // 14:
            odd.append((j, far))
    return even, odd


def in_vmem():
    return pl.BlockSpec(memory_space=pltpu.VMEM)


def in_smem():
    return pl.BlockSpec(memory_space=pltpu.SMEM)


def params(ranks, limit=16):
    return pltpu.CompilerParams(vmem_limit_bytes=(limit if ranks <= 16 else 48) * 1024 * 1024)


def fill_picks(ranks, qb, lists, p, me, sel_ref, k_ref, v_ref, out_ref):
    for parity, reach in enumerate(lists):
        for j, r in reach:
            dest = jnp.where(me + r < ranks, me + r, me)
            named = sel_ref[j, dest * qb + 2 * p + parity]
            local = jnp.clip(named - me * qb, 0, qb - 1)
            rows = pl.ds(pl.multiple_of(local * BLK, BLK), BLK)
            out_ref[dest, :BLK, :] = k_ref[rows, :]
            out_ref[dest, BLK : 2 * BLK, :] = v_ref[rows, :]


def pack_kernel(ranks, qb, lists, rank_ref, sel_ref, k_ref, v_ref, ck_ref, cv_ref, out_ref):
    hd = k_ref.shape[1]
    me = rank_ref[0]
    comp = jnp.concatenate([ck_ref[...].astype(F32), cv_ref[...].astype(F32)], axis=0).astype(BF16)

    def every(n, carry):
        out_ref[n, 2 * BLK :, :] = comp
        return carry

    lax.fori_loop(0, ranks, every, 0)
    out_ref[me, : 2 * BLK, :] = jnp.zeros((2 * BLK, hd), BF16)
    fill_picks(ranks, qb, lists, 0, me, sel_ref, k_ref, v_ref, out_ref)


def gate_kernel(qb, heads, x_hbm, w_ref, out_ref, x_ref, sem):
    copy = pltpu.make_async_copy(x_hbm, x_ref, sem)
    copy.start()
    copy.wait()
    nt = (((1,), (1,)), ((), ()))
    z = lax.dot_general(w_ref[...], x_ref[...], nt, preferred_element_type=F32)
    zt = jax.nn.sigmoid(z)
    for i in range(qb):
        for branch in range(2):
            for h in range(heads):
                row = branch * heads + h
                out_ref[i, branch : branch + 1, h * BLK : (h + 1) * BLK] = zt[
                    row : row + 1, i * BLK : (i + 1) * BLK
                ]


def fold(x, op):
    return op(x.reshape(x.shape[0] // 8, 8, x.shape[1]), axis=0)


def branch_grad(parts, lanes, gate, s_scr, u_scr, w_scr, d_scr):
    c2 = 128 ** -0.5 * LOG2E
    top = jnp.full((8, LANES), NEG, F32)
    for at, live, mask in parts:
        s = s_scr[at, :]
        if mask is not None:
            s = jnp.where(mask, s, NEG)
            s_scr[at, :] = s
        part = fold(s, jnp.max)
        top = jnp.maximum(top, part if live is None else jnp.where(live, part, NEG))
    top = jnp.max(top, axis=0, keepdims=True) * c2
    total = jnp.zeros((8, LANES), F32)
    mixed = jnp.zeros((8, LANES), F32)
    for at, live, mask in parts:
        e = jnp.exp2(s_scr[at, :] * c2 - (top if live is None else jnp.where(live, top, -NEG)))
        total = total + fold(e, jnp.sum)
        mixed = mixed + fold(e * u_scr[at, :], jnp.sum)
        s_scr[at, :] = e
    inv = 1.0 / jnp.sum(total, axis=0, keepdims=True)
    d_gate = jnp.sum(mixed, axis=0, keepdims=True) * inv
    weight = gate * inv
    for at, live, mask in parts:
        pw = s_scr[at, :] * weight
        w_scr[at, lanes] = pw.astype(BF16)
        d_scr[at, lanes] = (pw * (u_scr[at, :] - d_gate)).astype(BF16)
    return d_gate


def attend_kernel(ranks, qb, heads, lists, p, *refs):
    (rank_ref, sel_ref, q_ref, do_ref, k_ref, v_ref, gate_ref, comp_ref, picks_ref) = refs[:9]
    if p == 0:
        dq_ref, own_ref, dz_ref, dc_ref, send_ref, *scratch = refs[9:]
    else:
        _, dz_in, dc_in, own_in, dq_ref, own_ref, dz_ref, dc_ref, send_ref, *scratch = refs[9:]
    hd = k_ref.shape[1]
    me = rank_ref[0]
    step = pl.program_id(0)
    dg_scr, dc_scr = scratch[-2:]

    @pl.when(step == 0)
    def _():
        if p == 0:
            dc_scr[...] = jnp.zeros_like(dc_scr)
            dz_ref[...] = jnp.zeros_like(dz_ref)
            send_ref[me] = jnp.zeros(send_ref.shape[1:], BF16)
            fill_picks(ranks, qb, lists, 1, me, sel_ref, k_ref, v_ref, send_ref)
        else:
            dc_scr[...] = dc_in[...]
            dz_ref[...] = dz_in[...]
            own_ref[: 2 * BLK, :] = own_in[...]
            own_ref[2 * BLK :, :] = jnp.zeros((own_ref.shape[0] - 2 * BLK, own_ref.shape[1]), F32)
            add_homes(ranks, qb, lists, 0, me, sel_ref, picks_ref, own_ref)

    for parity in range(2):

        @pl.when(step == parity)
        def _(parity=parity):
            attend_row(ranks, qb, heads, lists[parity], me, 2 * p + parity, parity, q_ref, do_ref, k_ref, v_ref,
                       gate_ref, comp_ref, picks_ref, dq_ref, own_ref, send_ref, *scratch)

    @pl.when(step == 1)
    def _():
        dc_ref[...] = dc_scr[...]
        if p == 1:
            for r in range(1, ranks):

                @pl.when(me >= r)
                def _(r=r):
                    at = slice(r * qb, (r + 1) * qb)
                    piece = jnp.concatenate([dc_scr[at, :hd], dc_scr[at, hd:]], axis=0)
                    send_ref[me - r, 2 * BLK :, :] = piece.astype(BF16)

        for i in range(2):
            for branch in range(2):
                for h in range(heads):
                    row = branch * heads + h
                    lane = (2 * p + i) * BLK
                    dz_ref[row : row + 1, lane : lane + BLK] = dg_scr[
                        i, branch : branch + 1, h * BLK : (h + 1) * BLK
                    ]


def attend_row(ranks, qb, heads, reach, me, row, parity, q_ref, do_ref, k_ref, v_ref, gate_ref,
               comp_ref, picks_ref, dq_ref, own_ref, send_ref, kcat, vcat, qs, ds,
               s_scr, u_scr, w_scr, d_scr, dv_acc, dk_acc, dg_scr, dc_scr):
    npick = len(reach)
    hd = k_ref.shape[1]
    nblocks = ranks * qb
    nsel = (1 + npick) * BLK
    nk = nsel + nblocks
    per = LANES // BLK
    scale = hd ** -0.5

    pieces = []
    for r in range(ranks):
        pieces.append(comp_ref[jnp.maximum(me - r, 0)].astype(F32))
    kcat[nsel:nk, :] = jnp.concatenate([x[:qb] for x in pieces], axis=0).astype(BF16)
    vcat[nsel:nk, :] = jnp.concatenate([x[qb:] for x in pieces], axis=0).astype(BF16)
    kcat[:BLK, :] = k_ref[row * BLK : (row + 1) * BLK, :]
    vcat[:BLK, :] = v_ref[row * BLK : (row + 1) * BLK, :]
    for n, (_, r) in enumerate(reach):
        src = jnp.where(me >= r, me - r, me)
        kcat[(n + 1) * BLK : (n + 2) * BLK, :] = picks_ref[src, :BLK, :]
        vcat[(n + 1) * BLK : (n + 2) * BLK, :] = picks_ref[src, BLK : 2 * BLK, :]
    for h in range(heads):
        qs[h * BLK : (h + 1) * BLK, :] = q_ref[:, h * hd : (h + 1) * hd]
        ds[h * BLK : (h + 1) * BLK, :] = do_ref[:, h * hd : (h + 1) * hd]

    key_pos = lax.broadcasted_iota(jnp.int32, (BLK, LANES), 0)
    tok_pos = lax.rem(lax.broadcasted_iota(jnp.int32, (BLK, LANES), 1), BLK)
    sel_parts = [(slice(0, BLK), None, key_pos <= tok_pos)]
    for n, (_, r) in enumerate(reach):
        sel_parts.append((slice((n + 1) * BLK, (n + 2) * BLK), me >= r, None))
    comp_parts = []
    span = min(nblocks, BLK)
    for n in range(nblocks // span):
        place = lax.broadcasted_iota(jnp.int32, (span, LANES), 0) + n * span
        away, within = place // qb, lax.rem(place, qb)
        seen = (away <= me) & ((away > 0) | (within <= row))
        comp_parts.append((slice(nsel + n * span, nsel + (n + 1) * span), None, seen))

    nt = (((1,), (1,)), ((), ()))
    chunks = heads // per

    def lanes_of(c):
        return slice(c * LANES, (c + 1) * LANES)

    def scores(c):
        lanes = lanes_of(c)
        s_scr[c % 2, :nk, :] = lax.dot_general(kcat[:nk, :], qs[lanes, :], nt, preferred_element_type=F32)
        u_scr[c % 2, :nk, :] = lax.dot_general(vcat[:nk, :], ds[lanes, :], nt, preferred_element_type=F32)

    def soften(c):
        lanes = lanes_of(c)
        work = (s_scr.at[c % 2], u_scr.at[c % 2], w_scr, d_scr)
        for branch, parts in ((1, sel_parts), (0, comp_parts)):
            gate = gate_ref[0, branch : branch + 1, lanes]
            dg = branch_grad(parts, lanes, gate, *work)
            dg_scr[parity, branch : branch + 1, lanes] = dg * gate * (1.0 - gate)

    def gradients(c):
        lanes = lanes_of(c)
        dv = jnp.dot(w_scr[:nk, lanes], ds[lanes, :], preferred_element_type=F32)
        dk = jnp.dot(d_scr[:nk, lanes], qs[lanes, :], preferred_element_type=F32)
        if c == 0:
            dv_acc[:nk, :] = dv
            dk_acc[:nk, :] = dk
        else:
            dv_acc[:nk, :] += dv
            dk_acc[:nk, :] += dk
        tn = (((0,), (0,)), ((), ()))
        dq = lax.dot_general(d_scr[:nk, lanes], kcat[:nk, :], tn, preferred_element_type=F32)
        dq = (dq * scale).astype(BF16)
        for h in range(per):
            head = c * per + h
            dq_ref[:, head * hd : (head + 1) * hd] = dq[h * BLK : (h + 1) * BLK, :]

    scores(0)
    for c in range(chunks):
        if c + 1 < chunks:
            scores(c + 1)
        if c > 0:
            gradients(c - 1)
        soften(c)
    gradients(chunks - 1)

    own = slice(row * BLK, (row + 1) * BLK)
    if row < 2:
        own_ref[own, :hd] = dk_acc[:BLK, :] * scale
        own_ref[own, hd:] = dv_acc[:BLK, :]
    else:
        own_ref[own, :hd] += dk_acc[:BLK, :] * scale
        own_ref[own, hd:] += dv_acc[:BLK, :]
    dc_scr[:, :hd] += dk_acc[nsel:nk, :] * scale
    dc_scr[:, hd:] += dv_acc[nsel:nk, :]
    for n, (_, r) in enumerate(reach):
        at = slice((n + 1) * BLK, (n + 2) * BLK)
        dest = jnp.where(me >= r, me - r, me)
        send_ref[dest, :BLK, :] = (dk_acc[at, :] * scale).astype(BF16)
        send_ref[dest, BLK : 2 * BLK, :] = dv_acc[at, :].astype(BF16)


def add_homes(ranks, qb, lists, p, me, sel_ref, home_ref, acc):
    hd = home_ref.shape[2]
    for parity, reach in enumerate(lists):
        for j, r in reach:
            src = jnp.minimum(me + r, ranks - 1)
            named = sel_ref[j, src * qb + 2 * p + parity]
            local = jnp.clip(named - me * qb, 0, qb - 1)
            rows = pl.ds(pl.multiple_of(local * BLK, BLK), BLK)
            live = me + r < ranks
            acc[rows, :hd] += jnp.where(live, home_ref[src, :BLK, :].astype(F32), 0.0)
            acc[rows, hd:] += jnp.where(live, home_ref[src, BLK : 2 * BLK, :].astype(F32), 0.0)


def finish_kernel(ranks, qb, lists, rank_ref, sel_ref, part_ref, dc_ref, home_ref,
                  dk_ref, dv_ref, dck_ref, dcv_ref, acc):
    hd = dk_ref.shape[1]
    me = rank_ref[0]
    acc[...] = part_ref[...]
    add_homes(ranks, qb, lists, 1, me, sel_ref, home_ref, acc)
    dk_ref[...] = acc[:, :hd].astype(BF16)
    dv_ref[...] = acc[:, hd:].astype(BF16)

    def add(n, total):
        return total + home_ref[n, 2 * BLK :, :].astype(F32)

    total = lax.fori_loop(me + 1, ranks, add, jnp.zeros((2 * qb, hd), F32))
    dck_ref[...] = (total[:qb] + dc_ref[:qb, :hd]).astype(BF16)
    dcv_ref[...] = (total[qb:] + dc_ref[:qb, hd:]).astype(BF16)


def body(queries, keys, values, comp_keys, comp_values, selected, inputs, w_gate, d_out):
    tokens, width = queries.shape
    hd = keys.shape[1]
    heads = width // hd
    qb = tokens // BLK
    pair = qb // 2
    ranks = lax.axis_size("ctx")
    rank = lax.axis_index("ctx").astype(jnp.int32)
    me = rank.reshape(1)
    head = lax.axis_index("head")
    nblocks = ranks * qb
    lists = reach_lists(ranks)
    table = selected.T

    slot = 2 * BLK + 2 * qb

    def exchange(x):
        return lax.all_to_all(x, "ctx", split_axis=0, concat_axis=0, tiled=True)

    send = pl.pallas_call(
        functools.partial(pack_kernel, ranks, qb, lists),
        out_shape=jax.ShapeDtypeStruct((ranks, slot, hd), BF16),
        in_specs=[in_smem(), in_smem()] + [in_vmem()] * 4,
        out_specs=in_vmem(),
        compiler_params=params(ranks, 56),
        name="pack",
    )(me, table, keys, values, comp_keys, comp_values)
    fetched = exchange(send)

    gate = pl.pallas_call(
        functools.partial(gate_kernel, qb, heads),
        out_shape=jax.ShapeDtypeStruct((qb, 2, heads * BLK), F32),
        in_specs=[pl.BlockSpec(memory_space=pl.ANY), in_vmem()],
        out_specs=in_vmem(),
        scratch_shapes=[pltpu.VMEM(inputs.shape, BF16), pltpu.SemaphoreType.DMA],
        compiler_params=params(ranks),
        cost_estimate=pl.CostEstimate(
            flops=2 * inputs.size * w_gate.shape[1], bytes_accessed=2 * inputs.size, transcendentals=0
        ),
        name="gate",
    )(inputs, w_gate.T)
    half = w_gate.shape[0] // 2
    swap = [(0, 1), (1, 0)]
    w_send = lax.dynamic_slice_in_dim(w_gate, (1 - head) * half, half, 0)
    w_mine = lax.dynamic_slice_in_dim(w_gate, head * half, half, 0)
    w_other = lax.ppermute(w_send, "head", swap)

    nk = (1 + max(len(x) for x in lists)) * BLK + nblocks

    def attend(p, picks, previous):
        row = lambda i: (2 * p + i, 0)
        out_slot = slot if p else 2 * BLK
        args = [me, table, queries, d_out, keys, values, gate, fetched, picks] + previous
        in_specs = [
            in_smem(),
            in_smem(),
            pl.BlockSpec((BLK, width), row),
            pl.BlockSpec((BLK, width), row),
            in_vmem(),
            in_vmem(),
            pl.BlockSpec((1, 2, heads * BLK), lambda i: (2 * p + i, 0, 0)),
            pl.BlockSpec((ranks, 2 * qb, hd), lambda i: (0, 2 * BLK // (2 * qb), 0)),
            pl.BlockSpec((ranks, 2 * BLK, hd), lambda i: (0, 0, 0)),
        ]
        if previous:
            in_specs += [pl.BlockSpec(memory_space=pl.ANY)] + [in_vmem()] * 3
        return pl.pallas_call(
            functools.partial(attend_kernel, ranks, qb, heads, lists, p),
            grid=(2,),
            out_shape=[
                jax.ShapeDtypeStruct(queries.shape, BF16),
                jax.ShapeDtypeStruct((tokens if p else 2 * BLK, 2 * hd), F32),
                jax.ShapeDtypeStruct((2 * heads, tokens), F32),
                jax.ShapeDtypeStruct((nblocks, 2 * hd), F32),
                jax.ShapeDtypeStruct((ranks, out_slot, hd), BF16),
            ],
            in_specs=in_specs,
            out_specs=[pl.BlockSpec((BLK, width), row)] + [in_vmem()] * 4,
            scratch_shapes=[
                pltpu.VMEM((nk, hd), BF16),
                pltpu.VMEM((nk, hd), BF16),
                pltpu.VMEM((heads * BLK, hd), BF16),
                pltpu.VMEM((heads * BLK, hd), BF16),
                pltpu.VMEM((2, nk, LANES), F32),
                pltpu.VMEM((2, nk, LANES), F32),
                pltpu.VMEM((nk, heads * BLK), BF16),
                pltpu.VMEM((nk, heads * BLK), BF16),
                pltpu.VMEM((nk, hd), F32),
                pltpu.VMEM((nk, hd), F32),
                pltpu.VMEM((2, 2, heads * BLK), F32),
                pltpu.VMEM((nblocks, 2 * hd), F32),
            ],
            input_output_aliases={9: 0} if previous else {},
            compiler_params=params(ranks),
            cost_estimate=pl.CostEstimate(
                flops=10 * nk * heads * 2 * BLK * hd, bytes_accessed=4 << 20, transcendentals=0
            ),
            name=f"attend{p}",
        )(*args)

    dq, own0, dz, dc, send = attend(0, fetched, [])
    mixed = exchange(send)
    d_queries, part, dz, dc, send = attend(1, mixed, [dq, dz, dc, own0])
    home = exchange(send)

    d_keys, d_values, d_ck, d_cv = pl.pallas_call(
        functools.partial(finish_kernel, ranks, qb, lists),
        out_shape=[
            jax.ShapeDtypeStruct(x.shape, BF16) for x in (keys, values, comp_keys, comp_values)
        ],
        in_specs=[in_smem(), in_smem()] + [in_vmem()] * 3,
        out_specs=[in_vmem()] * 4,
        scratch_shapes=[pltpu.VMEM((tokens, 2 * hd), F32)],
        compiler_params=params(ranks),
        name="finish",
    )(me, table, part, dc, home)

    dz = dz.astype(BF16)
    dz_other = lax.ppermute(dz, "head", swap)
    tn = (((0,), (1,)), ((), ()))
    d_inputs = (
        lax.dot_general(dz, w_mine, tn, preferred_element_type=F32)
        + lax.dot_general(dz_other, w_other, tn, preferred_element_type=F32)
    ).astype(BF16)

    return d_queries, d_keys, d_values, d_ck, d_cv, d_inputs


def solution(mesh):
    split = P("ctx", "head")
    in_specs = (split,) * 5 + (P(), P("ctx", None), P(None, "head"), split)
    return jax.shard_map(
        body, mesh=mesh, in_specs=in_specs, out_specs=(split,) * 6, check_vma=False
    )
```

```python
import functools

import jax
import jax.numpy as jnp
from jax import lax
from jax.experimental import pallas as pl
from jax.experimental.pallas import tpu as pltpu
from jax.sharding import PartitionSpec as P

BLK = 64
PICKS = 15
LOG2E = 1.4426950408889634
LANES = 256
NEG = -1e30
F32, BF16 = jnp.float32, jnp.bfloat16


def reach_lists(ranks):
    half = ranks // 2
    even, odd = [], []
    for j in range(PICKS):
        near = 1 + j * max(half - 1, 0) // 14
        far = half + 1 + j * max(half - 2, 0) // 14
        if j == 0 or near != 1 + (j - 1) * max(half - 1, 0) // 14:
            even.append((j, near))
        if j == 0 or far != half + 1 + (j - 1) * max(half - 2, 0) // 14:
            odd.append((j, far))
    return even, odd


def in_vmem():
    return pl.BlockSpec(memory_space=pltpu.VMEM)


def in_smem():
    return pl.BlockSpec(memory_space=pltpu.SMEM)


def params(ranks, limit=16):
    return pltpu.CompilerParams(vmem_limit_bytes=(limit if ranks <= 16 else 48) * 1024 * 1024)


def fill_picks(ranks, qb, lists, p, me, sel_ref, k_ref, v_ref, out_ref):
    for parity, reach in enumerate(lists):
        for j, r in reach:
            dest = jnp.where(me + r < ranks, me + r, me)
            named = sel_ref[j, dest * qb + 2 * p + parity]
            local = jnp.clip(named - me * qb, 0, qb - 1)
            rows = pl.ds(pl.multiple_of(local * BLK, BLK), BLK)
            out_ref[dest, :BLK, :] = k_ref[rows, :]
            out_ref[dest, BLK : 2 * BLK, :] = v_ref[rows, :]


def pack_kernel(ranks, qb, lists, rank_ref, sel_ref, k_ref, v_ref, ck_ref, cv_ref, out_ref):
    hd = k_ref.shape[1]
    me = rank_ref[0]
    comp = jnp.concatenate([ck_ref[...].astype(F32), cv_ref[...].astype(F32)], axis=0).astype(BF16)

    def every(n, carry):
        out_ref[n, 2 * BLK :, :] = comp
        return carry

    lax.fori_loop(0, ranks, every, 0)
    out_ref[me, : 2 * BLK, :] = jnp.zeros((2 * BLK, hd), BF16)
    fill_picks(ranks, qb, lists, 0, me, sel_ref, k_ref, v_ref, out_ref)


def gate_kernel(qb, heads, x_ref, w_ref, out_ref):
    nt = (((1,), (1,)), ((), ()))
    z = lax.dot_general(w_ref[...], x_ref[...], nt, preferred_element_type=F32)
    zt = jax.nn.sigmoid(z)
    for i in range(qb):
        for branch in range(2):
            for h in range(heads):
                row = branch * heads + h
                out_ref[i, branch : branch + 1, h * BLK : (h + 1) * BLK] = zt[
                    row : row + 1, i * BLK : (i + 1) * BLK
                ]


def fold(x, op):
    return op(x.reshape(x.shape[0] // 8, 8, x.shape[1]), axis=0)


def branch_grad(parts, lanes, gate, s_scr, u_scr, w_scr, d_scr):
    c2 = 128 ** -0.5 * LOG2E
    top = jnp.full((8, LANES), NEG, F32)
    for at, live, mask in parts:
        s = s_scr[at, :]
        if mask is not None:
            s = jnp.where(mask, s, NEG)
            s_scr[at, :] = s
        part = fold(s, jnp.max)
        top = jnp.maximum(top, part if live is None else jnp.where(live, part, NEG))
    top = jnp.max(top, axis=0, keepdims=True) * c2
    total = jnp.zeros((8, LANES), F32)
    mixed = jnp.zeros((8, LANES), F32)
    for at, live, mask in parts:
        e = jnp.exp2(s_scr[at, :] * c2 - (top if live is None else jnp.where(live, top, -NEG)))
        total = total + fold(e, jnp.sum)
        mixed = mixed + fold(e * u_scr[at, :], jnp.sum)
        s_scr[at, :] = e
    inv = 1.0 / jnp.sum(total, axis=0, keepdims=True)
    d_gate = jnp.sum(mixed, axis=0, keepdims=True) * inv
    weight = gate * inv
    for at, live, mask in parts:
        pw = s_scr[at, :] * weight
        w_scr[at, lanes] = pw.astype(BF16)
        d_scr[at, lanes] = (pw * (u_scr[at, :] - d_gate)).astype(BF16)
    return d_gate


def attend_kernel(ranks, qb, heads, lists, p, *refs):
    (rank_ref, sel_ref, q_ref, do_ref, k_ref, v_ref, gate_ref, comp_ref, picks_ref) = refs[:9]
    if p == 0:
        dq_ref, own_ref, dz_ref, dc_ref, send_ref, ckv_ref, *scratch = refs[9:]
    else:
        dz_in, dc_in, own_in, own_ref, dz_ref, dc_ref, send_ref, *scratch = refs[9:]
        dq_ref, ckv_ref = None, None
    hd = k_ref.shape[1]
    me = rank_ref[0]
    step = pl.program_id(0)
    dg_scr, dc_scr = scratch[-2:]

    @pl.when(step == 0)
    def _():
        if p == 0:
            dc_scr[...] = jnp.zeros_like(dc_scr)
            dz_ref[...] = jnp.zeros_like(dz_ref)
            send_ref[me] = jnp.zeros(send_ref.shape[1:], BF16)
            fill_picks(ranks, qb, lists, 1, me, sel_ref, k_ref, v_ref, send_ref)
        else:
            dc_scr[...] = dc_in[...]
            dz_ref[...] = dz_in[...]
            own_ref[: 2 * BLK, :] = own_in[...]
            own_ref[2 * BLK :, :] = jnp.zeros((own_ref.shape[0] - 2 * BLK, own_ref.shape[1]), F32)
            add_homes(ranks, qb, lists, 0, me, sel_ref, picks_ref, own_ref)

    for parity in range(2):

        @pl.when(step == parity)
        def _(parity=parity):
            attend_row(ranks, qb, heads, lists[parity], me, 2 * p + parity, parity, q_ref, do_ref, k_ref, v_ref,
                       gate_ref, comp_ref, picks_ref, dq_ref, own_ref, send_ref, ckv_ref, *scratch)

    @pl.when(step == 1)
    def _():
        dc_ref[...] = dc_scr[...]
        if p == 1:
            for r in range(1, ranks):

                @pl.when(me >= r)
                def _(r=r):
                    at = slice(r * qb, (r + 1) * qb)
                    piece = jnp.concatenate([dc_scr[at, :hd], dc_scr[at, hd:]], axis=0)
                    send_ref[me - r, 2 * BLK :, :] = piece.astype(BF16)

        for i in range(2):
            for branch in range(2):
                for h in range(heads):
                    row = branch * heads + h
                    lane = (2 * p + i) * BLK
                    dz_ref[row : row + 1, lane : lane + BLK] = dg_scr[
                        i, branch : branch + 1, h * BLK : (h + 1) * BLK
                    ]


def tail_kernel(ranks, qb, heads, lists, rank_ref, q_ref, do_ref, k_ref, v_ref, gate_ref, ckv_ref,
                picks_ref, _, dq_ref, *scratch):
    me = rank_ref[0]
    step = pl.program_id(0)
    for parity in range(2):

        @pl.when(step == parity)
        def _(parity=parity):
            attend_row(ranks, qb, heads, lists[parity], me, 2 + parity, parity, q_ref, do_ref, k_ref, v_ref,
                       gate_ref, ckv_ref, picks_ref, dq_ref, None, None, None, *scratch)


def attend_row(ranks, qb, heads, reach, me, row, parity, q_ref, do_ref, k_ref, v_ref, gate_ref,
               comp_ref, picks_ref, dq_ref, own_ref, send_ref, ckv_ref, kcat, vcat, kt, qs, ds,
               s_scr, u_scr, w_scr, d_scr, dv_acc, dk_acc, dg_scr, dc_scr):
    npick = len(reach)
    hd = k_ref.shape[1]
    nblocks = ranks * qb
    nsel = (1 + npick) * BLK
    nk = nsel + nblocks
    per = LANES // BLK
    scale = hd ** -0.5

    if len(comp_ref.shape) == 3:
        pieces = []
        for r in range(ranks):
            pieces.append(comp_ref[jnp.maximum(me - r, 0)].astype(F32))
        kcat[nsel:nk, :] = jnp.concatenate([x[:qb] for x in pieces], axis=0).astype(BF16)
        vcat[nsel:nk, :] = jnp.concatenate([x[qb:] for x in pieces], axis=0).astype(BF16)
        ckv_ref[:, :hd] = kcat[nsel:nk, :]
        ckv_ref[:, hd:] = vcat[nsel:nk, :]
    else:
        kcat[nsel:nk, :] = comp_ref[:, :hd]
        vcat[nsel:nk, :] = comp_ref[:, hd:]
    kcat[:BLK, :] = k_ref[row * BLK : (row + 1) * BLK, :]
    vcat[:BLK, :] = v_ref[row * BLK : (row + 1) * BLK, :]
    for n, (_, r) in enumerate(reach):
        src = jnp.where(me >= r, me - r, me)
        kcat[(n + 1) * BLK : (n + 2) * BLK, :] = picks_ref[src, :BLK, :]
        vcat[(n + 1) * BLK : (n + 2) * BLK, :] = picks_ref[src, BLK : 2 * BLK, :]
    if dq_ref is not None:
        kt[:, :nk] = kcat[:nk, :].astype(F32).T.astype(BF16)
    for h in range(heads):
        qs[h * BLK : (h + 1) * BLK, :] = q_ref[:, h * hd : (h + 1) * hd]
        ds[h * BLK : (h + 1) * BLK, :] = do_ref[:, h * hd : (h + 1) * hd]

    key_pos = lax.broadcasted_iota(jnp.int32, (BLK, LANES), 0)
    tok_pos = lax.rem(lax.broadcasted_iota(jnp.int32, (BLK, LANES), 1), BLK)
    sel_parts = [(slice(0, BLK), None, key_pos <= tok_pos)]
    for n, (_, r) in enumerate(reach):
        sel_parts.append((slice((n + 1) * BLK, (n + 2) * BLK), me >= r, None))
    comp_parts = []
    span = min(nblocks, BLK)
    for n in range(nblocks // span):
        place = lax.broadcasted_iota(jnp.int32, (span, LANES), 0) + n * span
        away, within = place // qb, lax.rem(place, qb)
        seen = (away <= me) & ((away > 0) | (within <= row))
        comp_parts.append((slice(nsel + n * span, nsel + (n + 1) * span), None, seen))

    nt = (((1,), (1,)), ((), ()))
    chunks = heads // per

    def lanes_of(c):
        return slice(c * LANES, (c + 1) * LANES)

    def scores(c):
        lanes = lanes_of(c)
        s_scr[c % 2, :nk, :] = lax.dot_general(kcat[:nk, :], qs[lanes, :], nt, preferred_element_type=F32)
        u_scr[c % 2, :nk, :] = lax.dot_general(vcat[:nk, :], ds[lanes, :], nt, preferred_element_type=F32)

    def soften(c):
        lanes = lanes_of(c)
        work = (s_scr.at[c % 2], u_scr.at[c % 2], w_scr, d_scr)
        for branch, parts in ((1, sel_parts), (0, comp_parts)):
            gate = gate_ref[0, branch : branch + 1, lanes]
            dg = branch_grad(parts, lanes, gate, *work)
            dg_scr[parity, branch : branch + 1, lanes] = dg * gate * (1.0 - gate)

    def gradients(c):
        lanes = lanes_of(c)
        if send_ref is not None:
            dv = jnp.dot(w_scr[:nk, lanes], ds[lanes, :], preferred_element_type=F32)
            dk = jnp.dot(d_scr[:nk, lanes], qs[lanes, :], preferred_element_type=F32)
            if c == 0:
                dv_acc[:nk, :] = dv
                dk_acc[:nk, :] = dk
            else:
                dv_acc[:nk, :] += dv
                dk_acc[:nk, :] += dk
        if dq_ref is not None:
            dqt = jnp.dot(kt[:, :nk], d_scr[:nk, lanes], preferred_element_type=F32)
            dq = (dqt.T * scale).astype(BF16)
            for h in range(per):
                head = c * per + h
                dq_ref[:, head * hd : (head + 1) * hd] = dq[h * BLK : (h + 1) * BLK, :]

    scores(0)
    for c in range(chunks):
        if c + 1 < chunks:
            scores(c + 1)
        if c > 0:
            gradients(c - 1)
        soften(c)
    gradients(chunks - 1)
    if send_ref is None:
        return

    own = slice(row * BLK, (row + 1) * BLK)
    if row < 2:
        own_ref[own, :hd] = dk_acc[:BLK, :] * scale
        own_ref[own, hd:] = dv_acc[:BLK, :]
    else:
        own_ref[own, :hd] += dk_acc[:BLK, :] * scale
        own_ref[own, hd:] += dv_acc[:BLK, :]
    dc_scr[:, :hd] += dk_acc[nsel:nk, :] * scale
    dc_scr[:, hd:] += dv_acc[nsel:nk, :]
    for n, (_, r) in enumerate(reach):
        at = slice((n + 1) * BLK, (n + 2) * BLK)
        dest = jnp.where(me >= r, me - r, me)
        send_ref[dest, :BLK, :] = (dk_acc[at, :] * scale).astype(BF16)
        send_ref[dest, BLK : 2 * BLK, :] = dv_acc[at, :].astype(BF16)


def add_homes(ranks, qb, lists, p, me, sel_ref, home_ref, acc):
    hd = home_ref.shape[2]
    for parity, reach in enumerate(lists):
        for j, r in reach:
            src = jnp.minimum(me + r, ranks - 1)
            named = sel_ref[j, src * qb + 2 * p + parity]
            local = jnp.clip(named - me * qb, 0, qb - 1)
            rows = pl.ds(pl.multiple_of(local * BLK, BLK), BLK)
            live = me + r < ranks
            acc[rows, :hd] += jnp.where(live, home_ref[src, :BLK, :].astype(F32), 0.0)
            acc[rows, hd:] += jnp.where(live, home_ref[src, BLK : 2 * BLK, :].astype(F32), 0.0)


def finish_kernel(ranks, qb, lists, rank_ref, sel_ref, part_ref, dc_ref, home_ref,
                  dk_ref, dv_ref, dck_ref, dcv_ref, acc):
    hd = dk_ref.shape[1]
    me = rank_ref[0]
    acc[...] = part_ref[...]
    add_homes(ranks, qb, lists, 1, me, sel_ref, home_ref, acc)
    dk_ref[...] = acc[:, :hd].astype(BF16)
    dv_ref[...] = acc[:, hd:].astype(BF16)

    def add(n, total):
        return total + home_ref[n, 2 * BLK :, :].astype(F32)

    total = lax.fori_loop(me + 1, ranks, add, jnp.zeros((2 * qb, hd), F32))
    dck_ref[...] = (total[:qb] + dc_ref[:qb, :hd]).astype(BF16)
    dcv_ref[...] = (total[qb:] + dc_ref[:qb, hd:]).astype(BF16)


def body(queries, keys, values, comp_keys, comp_values, selected, inputs, w_gate, d_out):
    tokens, width = queries.shape
    hd = keys.shape[1]
    heads = width // hd
    qb = tokens // BLK
    pair = qb // 2
    ranks = lax.axis_size("ctx")
    rank = lax.axis_index("ctx").astype(jnp.int32)
    me = rank.reshape(1)
    head = lax.axis_index("head")
    nblocks = ranks * qb
    lists = reach_lists(ranks)
    table = selected.T

    slot = 2 * BLK + 2 * qb

    def exchange(x):
        return lax.all_to_all(x, "ctx", split_axis=0, concat_axis=0, tiled=True)

    send = pl.pallas_call(
        functools.partial(pack_kernel, ranks, qb, lists),
        out_shape=jax.ShapeDtypeStruct((ranks, slot, hd), BF16),
        in_specs=[in_smem(), in_smem()] + [in_vmem()] * 4,
        out_specs=in_vmem(),
        compiler_params=params(ranks, 56),
        name="pack",
    )(me, table, keys, values, comp_keys, comp_values)
    fetched = exchange(send)

    gate = pl.pallas_call(
        functools.partial(gate_kernel, qb, heads),
        out_shape=jax.ShapeDtypeStruct((qb, 2, heads * BLK), F32),
        in_specs=[in_vmem()] * 2,
        out_specs=in_vmem(),
        compiler_params=params(ranks, 60),
        cost_estimate=pl.CostEstimate(
            flops=2 * inputs.size * w_gate.shape[1], bytes_accessed=2 * inputs.size, transcendentals=0
        ),
        name="gate",
    )(inputs, w_gate.T)
    half = w_gate.shape[0] // 2
    swap = [(0, 1), (1, 0)]
    w_send = lax.dynamic_slice_in_dim(w_gate, (1 - head) * half, half, 0)
    w_mine = lax.dynamic_slice_in_dim(w_gate, head * half, half, 0)
    w_other = lax.ppermute(w_send, "head", swap)

    nk = (1 + max(len(x) for x in lists)) * BLK + nblocks

    def row_specs(p):
        row = lambda i: (2 * p + i, 0)
        return [
            pl.BlockSpec((BLK, width), row),
            pl.BlockSpec((BLK, width), row),
            in_vmem(),
            in_vmem(),
            pl.BlockSpec((1, 2, heads * BLK), lambda i: (2 * p + i, 0, 0)),
        ]

    scratch = [
        pltpu.VMEM((nk, hd), BF16),
        pltpu.VMEM((nk, hd), BF16),
        pltpu.VMEM((hd, nk), BF16),
        pltpu.VMEM((heads * BLK, hd), BF16),
        pltpu.VMEM((heads * BLK, hd), BF16),
        pltpu.VMEM((2, nk, LANES), F32),
        pltpu.VMEM((2, nk, LANES), F32),
        pltpu.VMEM((nk, heads * BLK), BF16),
        pltpu.VMEM((nk, heads * BLK), BF16),
        pltpu.VMEM((nk, hd), F32),
        pltpu.VMEM((nk, hd), F32),
        pltpu.VMEM((2, 2, heads * BLK), F32),
        pltpu.VMEM((nblocks, 2 * hd), F32),
    ]
    cost = pl.CostEstimate(
        flops=10 * nk * heads * 2 * BLK * hd, bytes_accessed=4 << 20, transcendentals=0
    )
    pick_spec = pl.BlockSpec((ranks, 2 * BLK, hd), lambda i: (0, 0, 0))

    def attend(p, comp, picks, previous):
        out_slot = slot if p else 2 * BLK
        comp_spec = in_vmem()
        out_shape = [
            jax.ShapeDtypeStruct((tokens if p else 2 * BLK, 2 * hd), F32),
            jax.ShapeDtypeStruct((2 * heads, tokens), F32),
            jax.ShapeDtypeStruct((nblocks, 2 * hd), F32),
            jax.ShapeDtypeStruct((ranks, out_slot, hd), BF16),
        ]
        out_specs = [in_vmem()] * 4
        if p == 0:
            comp_spec = pl.BlockSpec((ranks, 2 * qb, hd), lambda i: (0, 2 * BLK // (2 * qb), 0))
            out_shape = (
                [jax.ShapeDtypeStruct(queries.shape, BF16)]
                + out_shape
                + [jax.ShapeDtypeStruct((nblocks, 2 * hd), BF16)]
            )
            out_specs = [pl.BlockSpec((BLK, width), lambda i: (i, 0))] + out_specs + [in_vmem()]
        return pl.pallas_call(
            functools.partial(attend_kernel, ranks, qb, heads, lists, p),
            grid=(2,),
            out_shape=out_shape,
            in_specs=[in_smem(), in_smem()] + row_specs(p) + [comp_spec, pick_spec]
            + [in_vmem()] * len(previous),
            out_specs=out_specs,
            scratch_shapes=scratch,
            compiler_params=params(ranks),
            cost_estimate=cost,
            name=f"attend{p}",
        )(me, table, queries, d_out, keys, values, gate, comp, picks, *previous)

    dq, own0, dz, dc, send, ckv = attend(0, fetched, fetched, [])
    mixed = exchange(send)
    part, dz, dc, send = attend(1, ckv, mixed, [dz, dc, own0])
    home = exchange(send)
    d_queries = pl.pallas_call(
        functools.partial(tail_kernel, ranks, qb, heads, lists),
        grid=(2,),
        out_shape=jax.ShapeDtypeStruct(queries.shape, BF16),
        in_specs=[in_smem()] + row_specs(1) + [in_vmem(), pick_spec, pl.BlockSpec(memory_space=pl.ANY)],
        out_specs=pl.BlockSpec((BLK, width), lambda i: (2 + i, 0)),
        scratch_shapes=scratch,
        input_output_aliases={8: 0},
        compiler_params=params(ranks),
        cost_estimate=cost,
        name="tail",
    )(me, queries, d_out, keys, values, gate, ckv, mixed, dq)

    d_keys, d_values, d_ck, d_cv = pl.pallas_call(
        functools.partial(finish_kernel, ranks, qb, lists),
        out_shape=[
            jax.ShapeDtypeStruct(x.shape, BF16) for x in (keys, values, comp_keys, comp_values)
        ],
        in_specs=[in_smem(), in_smem()] + [in_vmem()] * 3,
        out_specs=[in_vmem()] * 4,
        scratch_shapes=[pltpu.VMEM((tokens, 2 * hd), F32)],
        compiler_params=params(ranks),
        name="finish",
    )(me, table, part, dc, home)

    dz = dz.astype(BF16)
    dz_other = lax.ppermute(dz, "head", swap)
    tn = (((0,), (1,)), ((), ()))
    d_inputs = (
        lax.dot_general(dz, w_mine, tn, preferred_element_type=F32)
        + lax.dot_general(dz_other, w_other, tn, preferred_element_type=F32)
    ).astype(BF16)

    return d_queries, d_keys, d_values, d_ck, d_cv, d_inputs


def solution(mesh):
    split = P("ctx", "head")
    in_specs = (split,) * 5 + (P(), P("ctx", None), P(None, "head"), split)
    return jax.shard_map(
        body, mesh=mesh, in_specs=in_specs, out_specs=(split,) * 6, check_vma=False
    )
```

```python
import functools

import jax
import jax.numpy as jnp
from jax import lax
from jax.experimental import pallas as pl
from jax.experimental.pallas import tpu as pltpu
from jax.sharding import PartitionSpec as P

BLK = 64
PICKS = 15
LOG2E = 1.4426950408889634
LANES = 256
NEG = -1e30
F32, BF16 = jnp.float32, jnp.bfloat16


def reach_lists(ranks):
    half = ranks // 2
    even, odd = [], []
    for j in range(PICKS):
        near = 1 + j * max(half - 1, 0) // 14
        far = half + 1 + j * max(half - 2, 0) // 14
        if j == 0 or near != 1 + (j - 1) * max(half - 1, 0) // 14:
            even.append((j, near))
        if j == 0 or far != half + 1 + (j - 1) * max(half - 2, 0) // 14:
            odd.append((j, far))
    return even, odd


def in_vmem():
    return pl.BlockSpec(memory_space=pltpu.VMEM)


def in_smem():
    return pl.BlockSpec(memory_space=pltpu.SMEM)


def params(ranks, limit=16):
    return pltpu.CompilerParams(vmem_limit_bytes=(limit if ranks <= 16 else 48) * 1024 * 1024)


def fill_picks(ranks, qb, lists, p, me, sel_ref, k_ref, v_ref, out_ref):
    for parity, reach in enumerate(lists):
        for j, r in reach:
            dest = jnp.where(me + r < ranks, me + r, me)
            named = sel_ref[j, dest * qb + 2 * p + parity]
            local = jnp.clip(named - me * qb, 0, qb - 1)
            rows = pl.ds(pl.multiple_of(local * BLK, BLK), BLK)
            out_ref[dest, :BLK, :] = k_ref[rows, :]
            out_ref[dest, BLK : 2 * BLK, :] = v_ref[rows, :]


def pack_kernel(ranks, qb, lists, rank_ref, sel_ref, k_ref, v_ref, ck_ref, cv_ref, out_ref):
    hd = k_ref.shape[1]
    me = rank_ref[0]
    comp = jnp.concatenate([ck_ref[...].astype(F32), cv_ref[...].astype(F32)], axis=0).astype(BF16)

    def every(n, carry):
        out_ref[n, 2 * BLK :, :] = comp
        return carry

    lax.fori_loop(0, ranks, every, 0)
    out_ref[me, : 2 * BLK, :] = jnp.zeros((2 * BLK, hd), BF16)
    fill_picks(ranks, qb, lists, 0, me, sel_ref, k_ref, v_ref, out_ref)


def gate_kernel(qb, heads, x_ref, w_ref, out_ref):
    nt = (((1,), (1,)), ((), ()))
    z = lax.dot_general(w_ref[...], x_ref[...], nt, preferred_element_type=F32)
    zt = jax.nn.sigmoid(z)
    for i in range(qb):
        for branch in range(2):
            for h in range(heads):
                row = branch * heads + h
                out_ref[i, branch : branch + 1, h * BLK : (h + 1) * BLK] = zt[
                    row : row + 1, i * BLK : (i + 1) * BLK
                ]


def fold(x, op):
    return op(x.reshape(x.shape[0] // 8, 8, x.shape[1]), axis=0)


def branch_grad(parts, lanes, gate, s_scr, u_scr, w_scr, d_scr):
    c2 = 128 ** -0.5 * LOG2E
    top = jnp.full((8, LANES), NEG, F32)
    for at, live, mask in parts:
        s = s_scr[at, :]
        if mask is not None:
            s = jnp.where(mask, s, NEG)
            s_scr[at, :] = s
        part = fold(s, jnp.max)
        top = jnp.maximum(top, part if live is None else jnp.where(live, part, NEG))
    top = jnp.max(top, axis=0, keepdims=True) * c2
    total = jnp.zeros((8, LANES), F32)
    mixed = jnp.zeros((8, LANES), F32)
    for at, live, mask in parts:
        e = jnp.exp2(s_scr[at, :] * c2 - (top if live is None else jnp.where(live, top, -NEG)))
        total = total + fold(e, jnp.sum)
        mixed = mixed + fold(e * u_scr[at, :], jnp.sum)
        s_scr[at, :] = e
    inv = 1.0 / jnp.sum(total, axis=0, keepdims=True)
    d_gate = jnp.sum(mixed, axis=0, keepdims=True) * inv
    weight = gate * inv
    for at, live, mask in parts:
        pw = s_scr[at, :] * weight
        w_scr[at, lanes] = pw.astype(BF16)
        d_scr[at, lanes] = (pw * (u_scr[at, :] - d_gate)).astype(BF16)
    return d_gate


def attend_kernel(ranks, qb, heads, lists, p, *refs):
    (rank_ref, sel_ref, q_ref, do_ref, k_ref, v_ref, gate_ref, comp_ref, picks_ref) = refs[:9]
    if p == 0:
        dq_ref, own_ref, dz_ref, dc_ref, send_ref, ckv_ref, *scratch = refs[9:]
    else:
        dz_in, dc_in, own_in, own_ref, dz_ref, dc_ref, send_ref, *scratch = refs[9:]
        dq_ref, ckv_ref = None, None
    hd = k_ref.shape[1]
    me = rank_ref[0]
    step = pl.program_id(0)
    dg_scr, dc_scr = scratch[-2:]

    @pl.when(step == 0)
    def _():
        if p == 0:
            dc_scr[...] = jnp.zeros_like(dc_scr)
            dz_ref[...] = jnp.zeros_like(dz_ref)
            send_ref[me] = jnp.zeros(send_ref.shape[1:], BF16)
            fill_picks(ranks, qb, lists, 1, me, sel_ref, k_ref, v_ref, send_ref)
        else:
            dc_scr[...] = dc_in[...]
            dz_ref[...] = dz_in[...]
            own_ref[: 2 * BLK, :] = own_in[...]
            own_ref[2 * BLK :, :] = jnp.zeros((own_ref.shape[0] - 2 * BLK, own_ref.shape[1]), F32)
            add_homes(ranks, qb, lists, 0, me, sel_ref, picks_ref, own_ref)

    for parity in range(2):

        @pl.when(step == parity)
        def _(parity=parity):
            attend_row(ranks, qb, heads, lists[parity], me, 2 * p + parity, parity, q_ref, do_ref, k_ref, v_ref,
                       gate_ref, comp_ref, picks_ref, dq_ref, own_ref, send_ref, ckv_ref, *scratch)

    @pl.when(step == 1)
    def _():
        dc_ref[...] = dc_scr[...]
        if p == 1:
            for r in range(1, ranks):

                @pl.when(me >= r)
                def _(r=r):
                    at = slice(r * qb, (r + 1) * qb)
                    piece = jnp.concatenate([dc_scr[at, :hd], dc_scr[at, hd:]], axis=0)
                    send_ref[me - r, 2 * BLK :, :] = piece.astype(BF16)

        for i in range(2):
            for branch in range(2):
                for h in range(heads):
                    row = branch * heads + h
                    lane = (2 * p + i) * BLK
                    dz_ref[row : row + 1, lane : lane + BLK] = dg_scr[
                        i, branch : branch + 1, h * BLK : (h + 1) * BLK
                    ]


def tail_kernel(ranks, qb, heads, lists, rank_ref, q_ref, do_ref, k_ref, v_ref, gate_ref, ckv_ref,
                picks_ref, _, dq_ref, *scratch):
    me = rank_ref[0]
    step = pl.program_id(0)
    for parity in range(2):

        @pl.when(step == parity)
        def _(parity=parity):
            attend_row(ranks, qb, heads, lists[parity], me, 2 + parity, parity, q_ref, do_ref, k_ref, v_ref,
                       gate_ref, ckv_ref, picks_ref, dq_ref, None, None, None, *scratch)


def attend_row(ranks, qb, heads, reach, me, row, parity, q_ref, do_ref, k_ref, v_ref, gate_ref,
               comp_ref, picks_ref, dq_ref, own_ref, send_ref, ckv_ref, kcat, vcat, kt, qs, ds,
               s_scr, u_scr, w_scr, d_scr, dv_acc, dk_acc, dg_scr, dc_scr):
    npick = len(reach)
    hd = k_ref.shape[1]
    nblocks = ranks * qb
    nsel = (1 + npick) * BLK
    nk = nsel + nblocks
    per = LANES // BLK
    scale = hd ** -0.5

    if len(comp_ref.shape) == 3:
        pieces = []
        for r in range(ranks):
            pieces.append(comp_ref[jnp.maximum(me - r, 0)].astype(F32))
        kcat[nsel:nk, :] = jnp.concatenate([x[:qb] for x in pieces], axis=0).astype(BF16)
        vcat[nsel:nk, :] = jnp.concatenate([x[qb:] for x in pieces], axis=0).astype(BF16)
        ckv_ref[:, :hd] = kcat[nsel:nk, :]
        ckv_ref[:, hd:] = vcat[nsel:nk, :]
    else:
        kcat[nsel:nk, :] = comp_ref[:, :hd]
        vcat[nsel:nk, :] = comp_ref[:, hd:]
    kcat[:BLK, :] = k_ref[row * BLK : (row + 1) * BLK, :]
    vcat[:BLK, :] = v_ref[row * BLK : (row + 1) * BLK, :]
    for n, (_, r) in enumerate(reach):
        src = jnp.where(me >= r, me - r, me)
        kcat[(n + 1) * BLK : (n + 2) * BLK, :] = picks_ref[src, :BLK, :]
        vcat[(n + 1) * BLK : (n + 2) * BLK, :] = picks_ref[src, BLK : 2 * BLK, :]
    if dq_ref is not None:
        kt[:, :nk] = kcat[:nk, :].astype(F32).T.astype(BF16)
    for h in range(heads):
        qs[h * BLK : (h + 1) * BLK, :] = q_ref[:, h * hd : (h + 1) * hd]
        ds[h * BLK : (h + 1) * BLK, :] = do_ref[:, h * hd : (h + 1) * hd]

    key_pos = lax.broadcasted_iota(jnp.int32, (BLK, LANES), 0)
    tok_pos = lax.rem(lax.broadcasted_iota(jnp.int32, (BLK, LANES), 1), BLK)
    sel_parts = [(slice(0, BLK), None, key_pos <= tok_pos)]
    for n, (_, r) in enumerate(reach):
        sel_parts.append((slice((n + 1) * BLK, (n + 2) * BLK), me >= r, None))
    comp_parts = []
    span = min(nblocks, BLK)
    for n in range(nblocks // span):
        place = lax.broadcasted_iota(jnp.int32, (span, LANES), 0) + n * span
        away, within = place // qb, lax.rem(place, qb)
        seen = (away <= me) & ((away > 0) | (within <= row))
        comp_parts.append((slice(nsel + n * span, nsel + (n + 1) * span), None, seen))

    nt = (((1,), (1,)), ((), ()))
    chunks = heads // per

    def lanes_of(c):
        return slice(c * LANES, (c + 1) * LANES)

    def scores(c):
        lanes = lanes_of(c)
        s_scr[c % 2, :nk, :] = lax.dot_general(kcat[:nk, :], qs[lanes, :], nt, preferred_element_type=F32)
        u_scr[c % 2, :nk, :] = lax.dot_general(vcat[:nk, :], ds[lanes, :], nt, preferred_element_type=F32)

    def soften(c):
        lanes = lanes_of(c)
        work = (s_scr.at[c % 2], u_scr.at[c % 2], w_scr, d_scr)
        for branch, parts in ((1, sel_parts), (0, comp_parts)):
            gate = gate_ref[0, branch : branch + 1, lanes]
            dg = branch_grad(parts, lanes, gate, *work)
            dg_scr[parity, branch : branch + 1, lanes] = dg * gate * (1.0 - gate)

    def gradients(c):
        lanes = lanes_of(c)
        if send_ref is not None:
            dv = jnp.dot(w_scr[:nk, lanes], ds[lanes, :], preferred_element_type=F32)
            dk = jnp.dot(d_scr[:nk, lanes], qs[lanes, :], preferred_element_type=F32)
            if c == 0:
                dv_acc[:nk, :] = dv
                dk_acc[:nk, :] = dk
            else:
                dv_acc[:nk, :] += dv
                dk_acc[:nk, :] += dk
        if dq_ref is not None:
            dqt = jnp.dot(kt[:, :nk], d_scr[:nk, lanes], preferred_element_type=F32)
            dq = (dqt.T * scale).astype(BF16)
            for h in range(per):
                head = c * per + h
                dq_ref[:, head * hd : (head + 1) * hd] = dq[h * BLK : (h + 1) * BLK, :]

    scores(0)
    for c in range(chunks):
        if c + 1 < chunks:
            scores(c + 1)
        if c > 0:
            gradients(c - 1)
        soften(c)
    gradients(chunks - 1)
    if send_ref is None:
        return

    own = slice(row * BLK, (row + 1) * BLK)
    if row < 2:
        own_ref[own, :hd] = dk_acc[:BLK, :] * scale
        own_ref[own, hd:] = dv_acc[:BLK, :]
    else:
        own_ref[own, :hd] += dk_acc[:BLK, :] * scale
        own_ref[own, hd:] += dv_acc[:BLK, :]
    dc_scr[:, :hd] += dk_acc[nsel:nk, :] * scale
    dc_scr[:, hd:] += dv_acc[nsel:nk, :]
    for n, (_, r) in enumerate(reach):
        at = slice((n + 1) * BLK, (n + 2) * BLK)
        dest = jnp.where(me >= r, me - r, me)
        send_ref[dest, :BLK, :] = (dk_acc[at, :] * scale).astype(BF16)
        send_ref[dest, BLK : 2 * BLK, :] = dv_acc[at, :].astype(BF16)


def add_homes(ranks, qb, lists, p, me, sel_ref, home_ref, acc):
    hd = home_ref.shape[2]
    for parity, reach in enumerate(lists):
        for j, r in reach:
            src = jnp.minimum(me + r, ranks - 1)
            named = sel_ref[j, src * qb + 2 * p + parity]
            local = jnp.clip(named - me * qb, 0, qb - 1)
            rows = pl.ds(pl.multiple_of(local * BLK, BLK), BLK)
            live = me + r < ranks
            acc[rows, :hd] += jnp.where(live, home_ref[src, :BLK, :].astype(F32), 0.0)
            acc[rows, hd:] += jnp.where(live, home_ref[src, BLK : 2 * BLK, :].astype(F32), 0.0)


def finish_kernel(ranks, qb, lists, rank_ref, sel_ref, part_ref, dc_ref, home_ref,
                  dk_ref, dv_ref, dck_ref, dcv_ref, acc):
    hd = dk_ref.shape[1]
    me = rank_ref[0]
    acc[...] = part_ref[...]
    add_homes(ranks, qb, lists, 1, me, sel_ref, home_ref, acc)
    dk_ref[...] = acc[:, :hd].astype(BF16)
    dv_ref[...] = acc[:, hd:].astype(BF16)

    def add(n, total):
        return total + home_ref[n, 2 * BLK :, :].astype(F32)

    total = lax.fori_loop(me + 1, ranks, add, jnp.zeros((2 * qb, hd), F32))
    dck_ref[...] = (total[:qb] + dc_ref[:qb, :hd]).astype(BF16)
    dcv_ref[...] = (total[qb:] + dc_ref[:qb, hd:]).astype(BF16)


def body(queries, keys, values, comp_keys, comp_values, selected, inputs, w_gate, d_out):
    tokens, width = queries.shape
    hd = keys.shape[1]
    heads = width // hd
    qb = tokens // BLK
    pair = qb // 2
    ranks = lax.axis_size("ctx")
    rank = lax.axis_index("ctx").astype(jnp.int32)
    me = rank.reshape(1)
    head = lax.axis_index("head")
    nblocks = ranks * qb
    lists = reach_lists(ranks)
    table = selected.T

    slot = 2 * BLK + 2 * qb

    def exchange(x):
        return lax.all_to_all(x, "ctx", split_axis=0, concat_axis=0, tiled=True)

    send = pl.pallas_call(
        functools.partial(pack_kernel, ranks, qb, lists),
        out_shape=jax.ShapeDtypeStruct((ranks, slot, hd), BF16),
        in_specs=[in_smem(), in_smem()] + [in_vmem()] * 4,
        out_specs=in_vmem(),
        compiler_params=params(ranks, 56),
        name="pack",
    )(me, table, keys, values, comp_keys, comp_values)
    fetched = exchange(send)

    gate = pl.pallas_call(
        functools.partial(gate_kernel, qb, heads),
        out_shape=jax.ShapeDtypeStruct((qb, 2, heads * BLK), F32),
        in_specs=[in_vmem()] * 2,
        out_specs=in_vmem(),
        compiler_params=params(ranks, 60),
        cost_estimate=pl.CostEstimate(
            flops=2 * inputs.size * w_gate.shape[1], bytes_accessed=2 * inputs.size, transcendentals=0
        ),
        name="gate",
    )(inputs, w_gate.T)
    half = w_gate.shape[0] // 2
    swap = [(0, 1), (1, 0)]
    w_send = lax.dynamic_slice_in_dim(w_gate, (1 - head) * half, half, 0)
    w_mine = lax.dynamic_slice_in_dim(w_gate, head * half, half, 0)
    w_other = lax.ppermute(w_send, "head", swap)

    nk = (1 + max(len(x) for x in lists)) * BLK + nblocks

    def row_specs(p):
        row = lambda i: (2 * p + i, 0)
        return [
            pl.BlockSpec((BLK, width), row),
            pl.BlockSpec((BLK, width), row),
            in_vmem(),
            in_vmem(),
            pl.BlockSpec((1, 2, heads * BLK), lambda i: (2 * p + i, 0, 0)),
        ]

    scratch = [
        pltpu.VMEM((nk, hd), BF16),
        pltpu.VMEM((nk, hd), BF16),
        pltpu.VMEM((hd, nk), BF16),
        pltpu.VMEM((heads * BLK, hd), BF16),
        pltpu.VMEM((heads * BLK, hd), BF16),
        pltpu.VMEM((2, nk, LANES), F32),
        pltpu.VMEM((2, nk, LANES), F32),
        pltpu.VMEM((nk, heads * BLK), BF16),
        pltpu.VMEM((nk, heads * BLK), BF16),
        pltpu.VMEM((nk, hd), F32),
        pltpu.VMEM((nk, hd), F32),
        pltpu.VMEM((2, 2, heads * BLK), F32),
        pltpu.VMEM((nblocks, 2 * hd), F32),
    ]
    cost = pl.CostEstimate(
        flops=10 * nk * heads * 2 * BLK * hd, bytes_accessed=4 << 20, transcendentals=0
    )
    pick_spec = pl.BlockSpec((ranks, 2 * BLK, hd), lambda i: (0, 0, 0))

    def attend(p, comp, picks, previous):
        out_slot = slot if p else 2 * BLK
        comp_spec = in_vmem()
        out_shape = [
            jax.ShapeDtypeStruct((tokens if p else 2 * BLK, 2 * hd), F32),
            jax.ShapeDtypeStruct((2 * heads, tokens), F32),
            jax.ShapeDtypeStruct((nblocks, 2 * hd), F32),
            jax.ShapeDtypeStruct((ranks, out_slot, hd), BF16),
        ]
        out_specs = [in_vmem()] * 4
        if p == 0:
            comp_spec = pl.BlockSpec((ranks, 2 * qb, hd), lambda i: (0, 2 * BLK // (2 * qb), 0))
            out_shape = (
                [jax.ShapeDtypeStruct(queries.shape, BF16)]
                + out_shape
                + [jax.ShapeDtypeStruct((nblocks, 2 * hd), BF16)]
            )
            out_specs = [pl.BlockSpec((BLK, width), lambda i: (i, 0))] + out_specs + [in_vmem()]
        return pl.pallas_call(
            functools.partial(attend_kernel, ranks, qb, heads, lists, p),
            grid=(2,),
            out_shape=out_shape,
            in_specs=[in_smem(), in_smem()] + row_specs(p) + [comp_spec, pick_spec]
            + [in_vmem()] * len(previous),
            out_specs=out_specs,
            scratch_shapes=scratch,
            compiler_params=params(ranks),
            cost_estimate=cost,
            name=f"attend{p}",
        )(me, table, queries, d_out, keys, values, gate, comp, picks, *previous)

    dq, own0, dz, dc, send, ckv = attend(0, fetched, fetched, [])
    mixed = exchange(send)
    part, dz, dc, send = attend(1, ckv, mixed, [dz, dc, own0])
    home = exchange(send)
    d_queries = pl.pallas_call(
        functools.partial(tail_kernel, ranks, qb, heads, lists),
        grid=(2,),
        out_shape=jax.ShapeDtypeStruct(queries.shape, BF16),
        in_specs=[in_smem()] + row_specs(1) + [in_vmem(), pick_spec, pl.BlockSpec(memory_space=pl.ANY)],
        out_specs=pl.BlockSpec((BLK, width), lambda i: (2 + i, 0)),
        scratch_shapes=scratch,
        input_output_aliases={8: 0},
        compiler_params=params(ranks, 60),
        cost_estimate=cost,
        name="tail",
    )(me, queries, d_out, keys, values, gate, ckv, mixed, dq)

    d_keys, d_values, d_ck, d_cv = pl.pallas_call(
        functools.partial(finish_kernel, ranks, qb, lists),
        out_shape=[
            jax.ShapeDtypeStruct(x.shape, BF16) for x in (keys, values, comp_keys, comp_values)
        ],
        in_specs=[in_smem(), in_smem()] + [in_vmem()] * 3,
        out_specs=[in_vmem()] * 4,
        scratch_shapes=[pltpu.VMEM((tokens, 2 * hd), F32)],
        compiler_params=params(ranks),
        name="finish",
    )(me, table, part, dc, home)

    dz = dz.astype(BF16)
    dz_other = lax.ppermute(dz, "head", swap)
    tn = (((0,), (1,)), ((), ()))
    d_inputs = (
        lax.dot_general(dz, w_mine, tn, preferred_element_type=F32)
        + lax.dot_general(dz_other, w_other, tn, preferred_element_type=F32)
    ).astype(BF16)

    return d_queries, d_keys, d_values, d_ck, d_cv, d_inputs


def solution(mesh):
    split = P("ctx", "head")
    in_specs = (split,) * 5 + (P(), P("ctx", None), P(None, "head"), split)
    return jax.shard_map(
        body, mesh=mesh, in_specs=in_specs, out_specs=(split,) * 6, check_vma=False
    )
```

```python
import functools

import jax
import jax.numpy as jnp
from jax import lax
from jax.experimental import pallas as pl
from jax.experimental.pallas import tpu as pltpu
from jax.sharding import PartitionSpec as P

BLK = 64
PICKS = 15
LOG2E = 1.4426950408889634
LANES = 256
NEG = -1e30
F32, BF16 = jnp.float32, jnp.bfloat16


def reach_lists(ranks):
    half = ranks // 2
    even, odd = [], []
    for j in range(PICKS):
        near = 1 + j * max(half - 1, 0) // 14
        far = half + 1 + j * max(half - 2, 0) // 14
        if j == 0 or near != 1 + (j - 1) * max(half - 1, 0) // 14:
            even.append((j, near))
        if j == 0 or far != half + 1 + (j - 1) * max(half - 2, 0) // 14:
            odd.append((j, far))
    return even, odd


def in_vmem():
    return pl.BlockSpec(memory_space=pltpu.VMEM)


def in_smem():
    return pl.BlockSpec(memory_space=pltpu.SMEM)


def params(ranks, limit=16):
    return pltpu.CompilerParams(vmem_limit_bytes=(limit if ranks <= 16 else 48) * 1024 * 1024)


def fill_picks(ranks, qb, lists, p, me, sel_ref, k_ref, v_ref, out_ref):
    for parity, reach in enumerate(lists):
        for j, r in reach:
            dest = jnp.where(me + r < ranks, me + r, me)
            named = sel_ref[j, dest * qb + 2 * p + parity]
            local = jnp.clip(named - me * qb, 0, qb - 1)
            rows = pl.ds(pl.multiple_of(local * BLK, BLK), BLK)
            out_ref[dest, :BLK, :] = k_ref[rows, :]
            out_ref[dest, BLK : 2 * BLK, :] = v_ref[rows, :]


def pack_kernel(ranks, qb, lists, rank_ref, sel_ref, k_ref, v_ref, ck_ref, cv_ref, out_ref):
    hd = k_ref.shape[1]
    me = rank_ref[0]
    comp = jnp.concatenate([ck_ref[...].astype(F32), cv_ref[...].astype(F32)], axis=0).astype(BF16)

    def every(n, carry):
        out_ref[n, 2 * BLK :, :] = comp
        return carry

    lax.fori_loop(0, ranks, every, 0)
    out_ref[me, : 2 * BLK, :] = jnp.zeros((2 * BLK, hd), BF16)
    fill_picks(ranks, qb, lists, 0, me, sel_ref, k_ref, v_ref, out_ref)


def gate_kernel(qb, heads, x_ref, w_ref, out_ref):
    nt = (((1,), (1,)), ((), ()))
    z = lax.dot_general(w_ref[...], x_ref[...], nt, preferred_element_type=F32)
    zt = jax.nn.sigmoid(z)
    for i in range(qb):
        for branch in range(2):
            for h in range(heads):
                row = branch * heads + h
                out_ref[i, branch : branch + 1, h * BLK : (h + 1) * BLK] = zt[
                    row : row + 1, i * BLK : (i + 1) * BLK
                ]


def fold(x, op):
    return op(x.reshape(x.shape[0] // 8, 8, x.shape[1]), axis=0)


def branch_grad(parts, lanes, gate, s_scr, u_scr, w_scr, d_scr):
    c2 = 128 ** -0.5 * LOG2E
    top = jnp.full((8, LANES), NEG, F32)
    for at, live, mask in parts:
        s = s_scr[at, :]
        if mask is not None:
            s = jnp.where(mask, s, NEG)
            s_scr[at, :] = s
        part = fold(s, jnp.max)
        top = jnp.maximum(top, part if live is None else jnp.where(live, part, NEG))
    top = jnp.max(top, axis=0, keepdims=True) * c2
    total = jnp.zeros((8, LANES), F32)
    mixed = jnp.zeros((8, LANES), F32)
    for at, live, mask in parts:
        e = jnp.exp2(s_scr[at, :] * c2 - (top if live is None else jnp.where(live, top, -NEG)))
        total = total + fold(e, jnp.sum)
        mixed = mixed + fold(e * u_scr[at, :], jnp.sum)
        s_scr[at, :] = e
    inv = 1.0 / jnp.sum(total, axis=0, keepdims=True)
    d_gate = jnp.sum(mixed, axis=0, keepdims=True) * inv
    weight = gate * inv
    for at, live, mask in parts:
        pw = s_scr[at, :] * weight
        w_scr[at, lanes] = pw.astype(BF16)
        d_scr[at, lanes] = (pw * (u_scr[at, :] - d_gate)).astype(BF16)
    return d_gate


def attend_kernel(ranks, qb, heads, lists, p, *refs):
    (rank_ref, sel_ref, q_ref, do_ref, k_ref, v_ref, gate_ref, comp_ref, picks_ref) = refs[:9]
    if p == 0:
        dq_ref, own_ref, dz_ref, dc_ref, send_ref, *scratch = refs[9:]
    else:
        dz_in, dc_in, own_in, own_ref, dz_ref, dc_ref, send_ref, *scratch = refs[9:]
        dq_ref = None
    hd = k_ref.shape[1]
    me = rank_ref[0]
    step = pl.program_id(0)
    dg_scr, dc_scr = scratch[-2:]

    @pl.when(step == 0)
    def _():
        if p == 0:
            dc_scr[...] = jnp.zeros_like(dc_scr)
            dz_ref[...] = jnp.zeros_like(dz_ref)
            send_ref[me] = jnp.zeros(send_ref.shape[1:], BF16)
            fill_picks(ranks, qb, lists, 1, me, sel_ref, k_ref, v_ref, send_ref)
        else:
            dc_scr[...] = dc_in[...]
            dz_ref[...] = dz_in[...]
            own_ref[: 2 * BLK, :] = own_in[...]
            own_ref[2 * BLK :, :] = jnp.zeros((own_ref.shape[0] - 2 * BLK, own_ref.shape[1]), F32)
            add_homes(ranks, qb, lists, 0, me, sel_ref, picks_ref, own_ref)

    for parity in range(2):

        @pl.when(step == parity)
        def _(parity=parity):
            attend_row(ranks, qb, heads, lists[parity], me, 2 * p + parity, parity, q_ref, do_ref, k_ref, v_ref,
                       gate_ref, comp_ref, picks_ref, dq_ref, own_ref, send_ref, *scratch)

    @pl.when(step == 1)
    def _():
        dc_ref[...] = dc_scr[...]
        if p == 1:
            for r in range(1, ranks):

                @pl.when(me >= r)
                def _(r=r):
                    at = slice(r * qb, (r + 1) * qb)
                    piece = jnp.concatenate([dc_scr[at, :hd], dc_scr[at, hd:]], axis=0)
                    send_ref[me - r, 2 * BLK :, :] = piece.astype(BF16)

        for i in range(2):
            for branch in range(2):
                for h in range(heads):
                    row = branch * heads + h
                    lane = (2 * p + i) * BLK
                    dz_ref[row : row + 1, lane : lane + BLK] = dg_scr[
                        i, branch : branch + 1, h * BLK : (h + 1) * BLK
                    ]


def tail_kernel(ranks, qb, heads, lists, rank_ref, q_ref, do_ref, k_ref, v_ref, gate_ref, comp_ref,
                picks_ref, _, dq_ref, *scratch):
    me = rank_ref[0]
    step = pl.program_id(0)
    for parity in range(2):

        @pl.when(step == parity)
        def _(parity=parity):
            attend_row(ranks, qb, heads, lists[parity], me, 2 + parity, parity, q_ref, do_ref, k_ref, v_ref,
                       gate_ref, comp_ref, picks_ref, dq_ref, None, None, *scratch)


def attend_row(ranks, qb, heads, reach, me, row, parity, q_ref, do_ref, k_ref, v_ref, gate_ref,
               comp_ref, picks_ref, dq_ref, own_ref, send_ref, kcat, vcat, kt, qs, ds,
               s_scr, u_scr, w_scr, d_scr, dv_acc, dk_acc, dg_scr, dc_scr):
    npick = len(reach)
    hd = k_ref.shape[1]
    nblocks = ranks * qb
    nsel = (1 + npick) * BLK
    nk = nsel + nblocks
    per = LANES // BLK
    scale = hd ** -0.5

    pieces = []
    for r in range(ranks):
        pieces.append(comp_ref[jnp.maximum(me - r, 0)].astype(F32))
    kcat[nsel:nk, :] = jnp.concatenate([x[:qb] for x in pieces], axis=0).astype(BF16)
    vcat[nsel:nk, :] = jnp.concatenate([x[qb:] for x in pieces], axis=0).astype(BF16)
    kcat[:BLK, :] = k_ref[row * BLK : (row + 1) * BLK, :]
    vcat[:BLK, :] = v_ref[row * BLK : (row + 1) * BLK, :]
    for n, (_, r) in enumerate(reach):
        src = jnp.where(me >= r, me - r, me)
        kcat[(n + 1) * BLK : (n + 2) * BLK, :] = picks_ref[src, :BLK, :]
        vcat[(n + 1) * BLK : (n + 2) * BLK, :] = picks_ref[src, BLK : 2 * BLK, :]
    if dq_ref is not None:
        kt[:, :nk] = kcat[:nk, :].astype(F32).T.astype(BF16)
    for h in range(heads):
        qs[h * BLK : (h + 1) * BLK, :] = q_ref[:, h * hd : (h + 1) * hd]
        ds[h * BLK : (h + 1) * BLK, :] = do_ref[:, h * hd : (h + 1) * hd]

    key_pos = lax.broadcasted_iota(jnp.int32, (BLK, LANES), 0)
    tok_pos = lax.rem(lax.broadcasted_iota(jnp.int32, (BLK, LANES), 1), BLK)
    sel_parts = [(slice(0, BLK), None, key_pos <= tok_pos)]
    for n, (_, r) in enumerate(reach):
        sel_parts.append((slice((n + 1) * BLK, (n + 2) * BLK), me >= r, None))
    comp_parts = []
    span = min(nblocks, BLK)
    for n in range(nblocks // span):
        place = lax.broadcasted_iota(jnp.int32, (span, LANES), 0) + n * span
        away, within = place // qb, lax.rem(place, qb)
        seen = (away <= me) & ((away > 0) | (within <= row))
        comp_parts.append((slice(nsel + n * span, nsel + (n + 1) * span), None, seen))

    nt = (((1,), (1,)), ((), ()))
    chunks = heads // per

    def lanes_of(c):
        return slice(c * LANES, (c + 1) * LANES)

    def scores(c):
        lanes = lanes_of(c)
        s_scr[c % 2, :nk, :] = lax.dot_general(kcat[:nk, :], qs[lanes, :], nt, preferred_element_type=F32)
        u_scr[c % 2, :nk, :] = lax.dot_general(vcat[:nk, :], ds[lanes, :], nt, preferred_element_type=F32)

    def soften(c):
        lanes = lanes_of(c)
        work = (s_scr.at[c % 2], u_scr.at[c % 2], w_scr, d_scr)
        for branch, parts in ((1, sel_parts), (0, comp_parts)):
            gate = gate_ref[0, branch : branch + 1, lanes]
            dg = branch_grad(parts, lanes, gate, *work)
            dg_scr[parity, branch : branch + 1, lanes] = dg * gate * (1.0 - gate)

    def gradients(c):
        lanes = lanes_of(c)
        if send_ref is not None:
            dv = jnp.dot(w_scr[:nk, lanes], ds[lanes, :], preferred_element_type=F32)
            dk = jnp.dot(d_scr[:nk, lanes], qs[lanes, :], preferred_element_type=F32)
            if c == 0:
                dv_acc[:nk, :] = dv
                dk_acc[:nk, :] = dk
            else:
                dv_acc[:nk, :] += dv
                dk_acc[:nk, :] += dk
        if dq_ref is not None:
            dqt = jnp.dot(kt[:, :nk], d_scr[:nk, lanes], preferred_element_type=F32)
            dq = (dqt.T * scale).astype(BF16)
            for h in range(per):
                head = c * per + h
                dq_ref[:, head * hd : (head + 1) * hd] = dq[h * BLK : (h + 1) * BLK, :]

    scores(0)
    for c in range(chunks):
        if c + 1 < chunks:
            scores(c + 1)
        if c > 0:
            gradients(c - 1)
        soften(c)
    gradients(chunks - 1)
    if send_ref is None:
        return

    own = slice(row * BLK, (row + 1) * BLK)
    if row < 2:
        own_ref[own, :hd] = dk_acc[:BLK, :] * scale
        own_ref[own, hd:] = dv_acc[:BLK, :]
    else:
        own_ref[own, :hd] += dk_acc[:BLK, :] * scale
        own_ref[own, hd:] += dv_acc[:BLK, :]
    dc_scr[:, :hd] += dk_acc[nsel:nk, :] * scale
    dc_scr[:, hd:] += dv_acc[nsel:nk, :]
    for n, (_, r) in enumerate(reach):
        at = slice((n + 1) * BLK, (n + 2) * BLK)
        dest = jnp.where(me >= r, me - r, me)
        send_ref[dest, :BLK, :] = (dk_acc[at, :] * scale).astype(BF16)
        send_ref[dest, BLK : 2 * BLK, :] = dv_acc[at, :].astype(BF16)


def add_homes(ranks, qb, lists, p, me, sel_ref, home_ref, acc):
    hd = home_ref.shape[2]
    for parity, reach in enumerate(lists):
        for j, r in reach:
            src = jnp.minimum(me + r, ranks - 1)
            named = sel_ref[j, src * qb + 2 * p + parity]
            local = jnp.clip(named - me * qb, 0, qb - 1)
            rows = pl.ds(pl.multiple_of(local * BLK, BLK), BLK)
            live = me + r < ranks
            acc[rows, :hd] += jnp.where(live, home_ref[src, :BLK, :].astype(F32), 0.0)
            acc[rows, hd:] += jnp.where(live, home_ref[src, BLK : 2 * BLK, :].astype(F32), 0.0)


def finish_kernel(ranks, qb, lists, rank_ref, sel_ref, part_ref, dc_ref, home_ref,
                  dk_ref, dv_ref, dck_ref, dcv_ref, acc):
    hd = dk_ref.shape[1]
    me = rank_ref[0]
    acc[...] = part_ref[...]
    add_homes(ranks, qb, lists, 1, me, sel_ref, home_ref, acc)
    dk_ref[...] = acc[:, :hd].astype(BF16)
    dv_ref[...] = acc[:, hd:].astype(BF16)

    def add(n, total):
        return total + home_ref[n, 2 * BLK :, :].astype(F32)

    total = lax.fori_loop(me + 1, ranks, add, jnp.zeros((2 * qb, hd), F32))
    dck_ref[...] = (total[:qb] + dc_ref[:qb, :hd]).astype(BF16)
    dcv_ref[...] = (total[qb:] + dc_ref[:qb, hd:]).astype(BF16)


def body(queries, keys, values, comp_keys, comp_values, selected, inputs, w_gate, d_out):
    tokens, width = queries.shape
    hd = keys.shape[1]
    heads = width // hd
    qb = tokens // BLK
    pair = qb // 2
    ranks = lax.axis_size("ctx")
    rank = lax.axis_index("ctx").astype(jnp.int32)
    me = rank.reshape(1)
    head = lax.axis_index("head")
    nblocks = ranks * qb
    lists = reach_lists(ranks)
    table = selected.T

    slot = 2 * BLK + 2 * qb

    def exchange(x):
        return lax.all_to_all(x, "ctx", split_axis=0, concat_axis=0, tiled=True)

    send = pl.pallas_call(
        functools.partial(pack_kernel, ranks, qb, lists),
        out_shape=jax.ShapeDtypeStruct((ranks, slot, hd), BF16),
        in_specs=[in_smem(), in_smem()] + [in_vmem()] * 4,
        out_specs=in_vmem(),
        compiler_params=params(ranks, 56),
        name="pack",
    )(me, table, keys, values, comp_keys, comp_values)
    fetched = exchange(send)

    gate = pl.pallas_call(
        functools.partial(gate_kernel, qb, heads),
        out_shape=jax.ShapeDtypeStruct((qb, 2, heads * BLK), F32),
        in_specs=[in_vmem()] * 2,
        out_specs=in_vmem(),
        compiler_params=params(ranks, 60),
        cost_estimate=pl.CostEstimate(
            flops=2 * inputs.size * w_gate.shape[1], bytes_accessed=2 * inputs.size, transcendentals=0
        ),
        name="gate",
    )(inputs, w_gate.T)
    half = w_gate.shape[0] // 2
    swap = [(0, 1), (1, 0)]
    w_send = lax.dynamic_slice_in_dim(w_gate, (1 - head) * half, half, 0)
    w_mine = lax.dynamic_slice_in_dim(w_gate, head * half, half, 0)
    w_other = lax.ppermute(w_send, "head", swap)

    nk = (1 + max(len(x) for x in lists)) * BLK + nblocks

    def row_specs(p):
        row = lambda i: (2 * p + i, 0)
        return [
            pl.BlockSpec((BLK, width), row),
            pl.BlockSpec((BLK, width), row),
            in_vmem(),
            in_vmem(),
            pl.BlockSpec((1, 2, heads * BLK), lambda i: (2 * p + i, 0, 0)),
        ]

    scratch = [
        pltpu.VMEM((nk, hd), BF16),
        pltpu.VMEM((nk, hd), BF16),
        pltpu.VMEM((hd, nk), BF16),
        pltpu.VMEM((heads * BLK, hd), BF16),
        pltpu.VMEM((heads * BLK, hd), BF16),
        pltpu.VMEM((2, nk, LANES), F32),
        pltpu.VMEM((2, nk, LANES), F32),
        pltpu.VMEM((nk, heads * BLK), BF16),
        pltpu.VMEM((nk, heads * BLK), BF16),
        pltpu.VMEM((nk, hd), F32),
        pltpu.VMEM((nk, hd), F32),
        pltpu.VMEM((2, 2, heads * BLK), F32),
        pltpu.VMEM((nblocks, 2 * hd), F32),
    ]
    cost = pl.CostEstimate(
        flops=10 * nk * heads * 2 * BLK * hd, bytes_accessed=4 << 20, transcendentals=0
    )
    pick_spec = pl.BlockSpec((ranks, 2 * BLK, hd), lambda i: (0, 0, 0))
    comp_spec = pl.BlockSpec((ranks, 2 * qb, hd), lambda i: (0, 2 * BLK // (2 * qb), 0))

    def attend(p, picks, previous):
        out_slot = slot if p else 2 * BLK
        out_shape = [
            jax.ShapeDtypeStruct((tokens if p else 2 * BLK, 2 * hd), F32),
            jax.ShapeDtypeStruct((2 * heads, tokens), F32),
            jax.ShapeDtypeStruct((nblocks, 2 * hd), F32),
            jax.ShapeDtypeStruct((ranks, out_slot, hd), BF16),
        ]
        out_specs = [in_vmem()] * 4
        if p == 0:
            out_shape = [jax.ShapeDtypeStruct(queries.shape, BF16)] + out_shape
            out_specs = [pl.BlockSpec((BLK, width), lambda i: (i, 0))] + out_specs
        return pl.pallas_call(
            functools.partial(attend_kernel, ranks, qb, heads, lists, p),
            grid=(2,),
            out_shape=out_shape,
            in_specs=[in_smem(), in_smem()] + row_specs(p) + [comp_spec, pick_spec]
            + [in_vmem()] * len(previous),
            out_specs=out_specs,
            scratch_shapes=scratch,
            compiler_params=params(ranks),
            cost_estimate=cost,
            name=f"attend{p}",
        )(me, table, queries, d_out, keys, values, gate, fetched, picks, *previous)

    dq, own0, dz, dc, send = attend(0, fetched, [])
    mixed = exchange(send)
    part, dz, dc, send = attend(1, mixed, [dz, dc, own0])
    home = exchange(send)
    d_queries = pl.pallas_call(
        functools.partial(tail_kernel, ranks, qb, heads, lists),
        grid=(2,),
        out_shape=jax.ShapeDtypeStruct(queries.shape, BF16),
        in_specs=[in_smem()] + row_specs(1) + [comp_spec, pick_spec, pl.BlockSpec(memory_space=pl.ANY)],
        out_specs=pl.BlockSpec((BLK, width), lambda i: (2 + i, 0)),
        scratch_shapes=scratch,
        input_output_aliases={8: 0},
        compiler_params=params(ranks, 60),
        cost_estimate=cost,
        name="tail",
    )(me, queries, d_out, keys, values, gate, fetched, mixed, dq)

    d_keys, d_values, d_ck, d_cv = pl.pallas_call(
        functools.partial(finish_kernel, ranks, qb, lists),
        out_shape=[
            jax.ShapeDtypeStruct(x.shape, BF16) for x in (keys, values, comp_keys, comp_values)
        ],
        in_specs=[in_smem(), in_smem()] + [in_vmem()] * 3,
        out_specs=[in_vmem()] * 4,
        scratch_shapes=[pltpu.VMEM((tokens, 2 * hd), F32)],
        compiler_params=params(ranks),
        name="finish",
    )(me, table, part, dc, home)

    dz = dz.astype(BF16)
    dz_other = lax.ppermute(dz, "head", swap)
    tn = (((0,), (1,)), ((), ()))
    d_inputs = (
        lax.dot_general(dz, w_mine, tn, preferred_element_type=F32)
        + lax.dot_general(dz_other, w_other, tn, preferred_element_type=F32)
    ).astype(BF16)

    return d_queries, d_keys, d_values, d_ck, d_cv, d_inputs


def solution(mesh):
    split = P("ctx", "head")
    in_specs = (split,) * 5 + (P(), P("ctx", None), P(None, "head"), split)
    return jax.shard_map(
        body, mesh=mesh, in_specs=in_specs, out_specs=(split,) * 6, check_vma=False
    )
```

```python
import functools

import jax
import jax.numpy as jnp
from jax import lax
from jax.experimental import pallas as pl
from jax.experimental.pallas import tpu as pltpu
from jax.sharding import PartitionSpec as P

BLK = 64
PICKS = 15
LOG2E = 1.4426950408889634
LANES = 256
NEG = -1e30
F32, BF16 = jnp.float32, jnp.bfloat16


def reach_lists(ranks):
    half = ranks // 2
    even, odd = [], []
    for j in range(PICKS):
        near = 1 + j * max(half - 1, 0) // 14
        far = half + 1 + j * max(half - 2, 0) // 14
        if j == 0 or near != 1 + (j - 1) * max(half - 1, 0) // 14:
            even.append((j, near))
        if j == 0 or far != half + 1 + (j - 1) * max(half - 2, 0) // 14:
            odd.append((j, far))
    return even, odd


def in_vmem():
    return pl.BlockSpec(memory_space=pltpu.VMEM)


def in_smem():
    return pl.BlockSpec(memory_space=pltpu.SMEM)


def params(ranks, limit=16):
    return pltpu.CompilerParams(vmem_limit_bytes=(limit if ranks <= 16 else 48) * 1024 * 1024)


def fill_picks(ranks, qb, lists, p, me, sel_ref, k_ref, v_ref, out_ref):
    for parity, reach in enumerate(lists):
        for j, r in reach:
            dest = jnp.where(me + r < ranks, me + r, me)
            named = sel_ref[j, dest * qb + 2 * p + parity]
            local = jnp.clip(named - me * qb, 0, qb - 1)
            rows = pl.ds(pl.multiple_of(local * BLK, BLK), BLK)
            out_ref[dest, :BLK, :] = k_ref[rows, :]
            out_ref[dest, BLK : 2 * BLK, :] = v_ref[rows, :]


def pack_kernel(ranks, qb, lists, rank_ref, sel_ref, k_ref, v_ref, ck_ref, cv_ref, out_ref):
    hd = k_ref.shape[1]
    me = rank_ref[0]
    comp = jnp.concatenate([ck_ref[...].astype(F32), cv_ref[...].astype(F32)], axis=0).astype(BF16)

    def every(n, carry):
        out_ref[n, 2 * BLK :, :] = comp
        return carry

    lax.fori_loop(0, ranks, every, 0)
    out_ref[me, : 2 * BLK, :] = jnp.zeros((2 * BLK, hd), BF16)
    fill_picks(ranks, qb, lists, 0, me, sel_ref, k_ref, v_ref, out_ref)


def gate_kernel(qb, heads, x_ref, w_ref, out_ref):
    nt = (((1,), (1,)), ((), ()))
    z = lax.dot_general(w_ref[...], x_ref[...], nt, preferred_element_type=F32)
    zt = jax.nn.sigmoid(z)
    for i in range(qb):
        for branch in range(2):
            for h in range(heads):
                row = branch * heads + h
                out_ref[i, branch : branch + 1, h * BLK : (h + 1) * BLK] = zt[
                    row : row + 1, i * BLK : (i + 1) * BLK
                ]


def fold(x, op):
    return op(x.reshape(x.shape[0] // 8, 8, x.shape[1]), axis=0)


def branch_grad(parts, lanes, gate, s_scr, u_scr, w_scr, d_scr):
    c2 = 128 ** -0.5 * LOG2E
    top = jnp.full((8, LANES), NEG, F32)
    for at, live, mask in parts:
        s = s_scr[at, :]
        if mask is not None:
            s = jnp.where(mask, s, NEG)
            s_scr[at, :] = s
        part = fold(s, jnp.max)
        top = jnp.maximum(top, part if live is None else jnp.where(live, part, NEG))
    top = jnp.max(top, axis=0, keepdims=True) * c2
    total = jnp.zeros((8, LANES), F32)
    mixed = jnp.zeros((8, LANES), F32)
    for at, live, mask in parts:
        e = jnp.exp2(s_scr[at, :] * c2 - (top if live is None else jnp.where(live, top, -NEG)))
        total = total + fold(e, jnp.sum)
        mixed = mixed + fold(e * u_scr[at, :], jnp.sum)
        s_scr[at, :] = e
    inv = 1.0 / jnp.sum(total, axis=0, keepdims=True)
    d_gate = jnp.sum(mixed, axis=0, keepdims=True) * inv
    weight = gate * inv
    for at, live, mask in parts:
        pw = s_scr[at, :] * weight
        w_scr[at, lanes] = pw.astype(BF16)
        d_scr[at, lanes] = (pw * (u_scr[at, :] - d_gate)).astype(BF16)
    return d_gate


def attend_kernel(ranks, qb, heads, lists, p, *refs):
    (rank_ref, sel_ref, q_ref, do_ref, k_ref, v_ref, gate_ref, comp_ref, picks_ref) = refs[:9]
    if p == 0:
        dq_ref, own_ref, dz_ref, dc_ref, send_ref, ckv_ref, *scratch = refs[9:]
    else:
        dz_in, dc_in, own_in, own_ref, dz_ref, dc_ref, send_ref, *scratch = refs[9:]
        dq_ref, ckv_ref = None, None
    hd = k_ref.shape[1]
    me = rank_ref[0]
    step = pl.program_id(0)
    dg_scr, dc_scr = scratch[-2:]

    @pl.when(step == 0)
    def _():
        if p == 0:
            dc_scr[...] = jnp.zeros_like(dc_scr)
            dz_ref[...] = jnp.zeros_like(dz_ref)
            send_ref[me] = jnp.zeros(send_ref.shape[1:], BF16)
            fill_picks(ranks, qb, lists, 1, me, sel_ref, k_ref, v_ref, send_ref)
        else:
            dc_scr[...] = dc_in[...]
            dz_ref[...] = dz_in[...]
            own_ref[: 2 * BLK, :] = own_in[...]
            own_ref[2 * BLK :, :] = jnp.zeros((own_ref.shape[0] - 2 * BLK, own_ref.shape[1]), F32)
            add_homes(ranks, qb, lists, 0, me, sel_ref, picks_ref, own_ref)

    for parity in range(2):

        @pl.when(step == parity)
        def _(parity=parity):
            attend_row(ranks, qb, heads, lists[parity], me, 2 * p + parity, parity, q_ref, do_ref, k_ref, v_ref,
                       gate_ref, comp_ref, picks_ref, dq_ref, own_ref, send_ref, ckv_ref, *scratch)

    @pl.when(step == 1)
    def _():
        dc_ref[...] = dc_scr[...]
        if p == 1:
            for r in range(1, ranks):

                @pl.when(me >= r)
                def _(r=r):
                    at = slice(r * qb, (r + 1) * qb)
                    piece = jnp.concatenate([dc_scr[at, :hd], dc_scr[at, hd:]], axis=0)
                    send_ref[me - r, 2 * BLK :, :] = piece.astype(BF16)

        for i in range(2):
            for branch in range(2):
                for h in range(heads):
                    row = branch * heads + h
                    lane = (2 * p + i) * BLK
                    dz_ref[row : row + 1, lane : lane + BLK] = dg_scr[
                        i, branch : branch + 1, h * BLK : (h + 1) * BLK
                    ]


def tail_kernel(ranks, qb, heads, lists, rank_ref, q_ref, do_ref, k_ref, v_ref, gate_ref, ckv_ref,
                picks_ref, _, dq_ref, *scratch):
    me = rank_ref[0]
    step = pl.program_id(0)
    for parity in range(2):

        @pl.when(step == parity)
        def _(parity=parity):
            attend_row(ranks, qb, heads, lists[parity], me, 2 + parity, parity, q_ref, do_ref, k_ref, v_ref,
                       gate_ref, ckv_ref, picks_ref, dq_ref, None, None, None, *scratch)


def attend_row(ranks, qb, heads, reach, me, row, parity, q_ref, do_ref, k_ref, v_ref, gate_ref,
               comp_ref, picks_ref, dq_ref, own_ref, send_ref, ckv_ref, kcat, vcat, kt, qs, ds,
               s_scr, u_scr, w_scr, d_scr, dv_acc, dk_acc, dg_scr, dc_scr):
    npick = len(reach)
    hd = k_ref.shape[1]
    nblocks = ranks * qb
    nsel = (1 + npick) * BLK
    nk = nsel + nblocks
    per = LANES // BLK
    scale = hd ** -0.5

    if len(comp_ref.shape) == 3:
        pieces = []
        for r in range(ranks):
            pieces.append(comp_ref[jnp.maximum(me - r, 0)].astype(F32))
        kcat[nsel:nk, :] = jnp.concatenate([x[:qb] for x in pieces], axis=0).astype(BF16)
        vcat[nsel:nk, :] = jnp.concatenate([x[qb:] for x in pieces], axis=0).astype(BF16)
        ckv_ref[:, :hd] = kcat[nsel:nk, :]
        ckv_ref[:, hd:] = vcat[nsel:nk, :]
    else:
        kcat[nsel:nk, :] = comp_ref[:, :hd]
        vcat[nsel:nk, :] = comp_ref[:, hd:]
    kcat[:BLK, :] = k_ref[row * BLK : (row + 1) * BLK, :]
    vcat[:BLK, :] = v_ref[row * BLK : (row + 1) * BLK, :]
    for n, (_, r) in enumerate(reach):
        src = jnp.where(me >= r, me - r, me)
        kcat[(n + 1) * BLK : (n + 2) * BLK, :] = picks_ref[src, :BLK, :]
        vcat[(n + 1) * BLK : (n + 2) * BLK, :] = picks_ref[src, BLK : 2 * BLK, :]
    if dq_ref is not None:
        kt[:, :nk] = kcat[:nk, :].astype(F32).T.astype(BF16)
    for h in range(heads):
        qs[h * BLK : (h + 1) * BLK, :] = q_ref[:, h * hd : (h + 1) * hd]
        ds[h * BLK : (h + 1) * BLK, :] = do_ref[:, h * hd : (h + 1) * hd]

    key_pos = lax.broadcasted_iota(jnp.int32, (BLK, LANES), 0)
    tok_pos = lax.rem(lax.broadcasted_iota(jnp.int32, (BLK, LANES), 1), BLK)
    sel_parts = [(slice(0, BLK), None, key_pos <= tok_pos)]
    for n, (_, r) in enumerate(reach):
        sel_parts.append((slice((n + 1) * BLK, (n + 2) * BLK), me >= r, None))
    comp_parts = []
    span = min(nblocks, BLK)
    for n in range(nblocks // span):
        place = lax.broadcasted_iota(jnp.int32, (span, LANES), 0) + n * span
        away, within = place // qb, lax.rem(place, qb)
        seen = (away <= me) & ((away > 0) | (within <= row))
        comp_parts.append((slice(nsel + n * span, nsel + (n + 1) * span), None, seen))

    nt = (((1,), (1,)), ((), ()))
    chunks = heads // per

    def lanes_of(c):
        return slice(c * LANES, (c + 1) * LANES)

    def scores(c):
        lanes = lanes_of(c)
        s_scr[c % 2, :nk, :] = lax.dot_general(kcat[:nk, :], qs[lanes, :], nt, preferred_element_type=F32)
        u_scr[c % 2, :nk, :] = lax.dot_general(vcat[:nk, :], ds[lanes, :], nt, preferred_element_type=F32)

    def soften(c):
        lanes = lanes_of(c)
        work = (s_scr.at[c % 2], u_scr.at[c % 2], w_scr, d_scr)
        for branch, parts in ((1, sel_parts), (0, comp_parts)):
            gate = gate_ref[0, branch : branch + 1, lanes]
            dg = branch_grad(parts, lanes, gate, *work)
            dg_scr[parity, branch : branch + 1, lanes] = dg * gate * (1.0 - gate)

    def gradients(c):
        lanes = lanes_of(c)
        if send_ref is not None:
            dv = jnp.dot(w_scr[:nk, lanes], ds[lanes, :], preferred_element_type=F32)
            dk = jnp.dot(d_scr[:nk, lanes], qs[lanes, :], preferred_element_type=F32)
            if c == 0:
                dv_acc[:nk, :] = dv
                dk_acc[:nk, :] = dk
            else:
                dv_acc[:nk, :] += dv
                dk_acc[:nk, :] += dk
        if dq_ref is not None:
            dqt = jnp.dot(kt[:, :nk], d_scr[:nk, lanes], preferred_element_type=F32)
            dq = (dqt.T * scale).astype(BF16)
            for h in range(per):
                head = c * per + h
                dq_ref[:, head * hd : (head + 1) * hd] = dq[h * BLK : (h + 1) * BLK, :]

    scores(0)
    for c in range(chunks):
        if c + 1 < chunks:
            scores(c + 1)
        if c > 0:
            gradients(c - 1)
        soften(c)
    gradients(chunks - 1)
    if send_ref is None:
        return

    own = slice(row * BLK, (row + 1) * BLK)
    if row < 2:
        own_ref[own, :hd] = dk_acc[:BLK, :] * scale
        own_ref[own, hd:] = dv_acc[:BLK, :]
    else:
        own_ref[own, :hd] += dk_acc[:BLK, :] * scale
        own_ref[own, hd:] += dv_acc[:BLK, :]
    dc_scr[:, :hd] += dk_acc[nsel:nk, :] * scale
    dc_scr[:, hd:] += dv_acc[nsel:nk, :]
    for n, (_, r) in enumerate(reach):
        at = slice((n + 1) * BLK, (n + 2) * BLK)
        dest = jnp.where(me >= r, me - r, me)
        send_ref[dest, :BLK, :] = (dk_acc[at, :] * scale).astype(BF16)
        send_ref[dest, BLK : 2 * BLK, :] = dv_acc[at, :].astype(BF16)


def add_homes(ranks, qb, lists, p, me, sel_ref, home_ref, acc):
    hd = home_ref.shape[2]
    for parity, reach in enumerate(lists):
        for j, r in reach:
            src = jnp.minimum(me + r, ranks - 1)
            named = sel_ref[j, src * qb + 2 * p + parity]
            local = jnp.clip(named - me * qb, 0, qb - 1)
            rows = pl.ds(pl.multiple_of(local * BLK, BLK), BLK)
            live = me + r < ranks
            acc[rows, :hd] += jnp.where(live, home_ref[src, :BLK, :].astype(F32), 0.0)
            acc[rows, hd:] += jnp.where(live, home_ref[src, BLK : 2 * BLK, :].astype(F32), 0.0)


def finish_kernel(ranks, qb, lists, rank_ref, sel_ref, part_ref, dc_ref, home_ref,
                  dk_ref, dv_ref, dck_ref, dcv_ref, acc):
    hd = dk_ref.shape[1]
    me = rank_ref[0]
    acc[...] = part_ref[...]
    add_homes(ranks, qb, lists, 1, me, sel_ref, home_ref, acc)
    dk_ref[...] = acc[:, :hd].astype(BF16)
    dv_ref[...] = acc[:, hd:].astype(BF16)

    def add(n, total):
        return total + home_ref[n, 2 * BLK :, :].astype(F32)

    total = lax.fori_loop(me + 1, ranks, add, jnp.zeros((2 * qb, hd), F32))
    dck_ref[...] = (total[:qb] + dc_ref[:qb, :hd]).astype(BF16)
    dcv_ref[...] = (total[qb:] + dc_ref[:qb, hd:]).astype(BF16)


def body(queries, keys, values, comp_keys, comp_values, selected, inputs, w_gate, d_out):
    tokens, width = queries.shape
    hd = keys.shape[1]
    heads = width // hd
    qb = tokens // BLK
    pair = qb // 2
    ranks = lax.axis_size("ctx")
    rank = lax.axis_index("ctx").astype(jnp.int32)
    me = rank.reshape(1)
    head = lax.axis_index("head")
    nblocks = ranks * qb
    lists = reach_lists(ranks)
    table = selected.T

    slot = 2 * BLK + 2 * qb

    def exchange(x):
        return lax.all_to_all(x, "ctx", split_axis=0, concat_axis=0, tiled=True)

    send = pl.pallas_call(
        functools.partial(pack_kernel, ranks, qb, lists),
        out_shape=jax.ShapeDtypeStruct((ranks, slot, hd), BF16),
        in_specs=[in_smem(), in_smem()] + [in_vmem()] * 4,
        out_specs=in_vmem(),
        compiler_params=params(ranks, 56),
        name="pack",
    )(me, table, keys, values, comp_keys, comp_values)
    fetched = exchange(send)

    gate = pl.pallas_call(
        functools.partial(gate_kernel, qb, heads),
        out_shape=jax.ShapeDtypeStruct((qb, 2, heads * BLK), F32),
        in_specs=[in_vmem()] * 2,
        out_specs=in_vmem(),
        compiler_params=params(ranks),
        cost_estimate=pl.CostEstimate(
            flops=2 * inputs.size * w_gate.shape[1], bytes_accessed=2 * inputs.size, transcendentals=0
        ),
        name="gate",
    )(inputs, w_gate.T)
    half = w_gate.shape[0] // 2
    swap = [(0, 1), (1, 0)]
    w_send = lax.dynamic_slice_in_dim(w_gate, (1 - head) * half, half, 0)
    w_mine = lax.dynamic_slice_in_dim(w_gate, head * half, half, 0)
    w_other = lax.ppermute(w_send, "head", swap)

    nk = (1 + max(len(x) for x in lists)) * BLK + nblocks

    def row_specs(p):
        row = lambda i: (2 * p + i, 0)
        return [
            pl.BlockSpec((BLK, width), row),
            pl.BlockSpec((BLK, width), row),
            in_vmem(),
            in_vmem(),
            pl.BlockSpec((1, 2, heads * BLK), lambda i: (2 * p + i, 0, 0)),
        ]

    scratch = [
        pltpu.VMEM((nk, hd), BF16),
        pltpu.VMEM((nk, hd), BF16),
        pltpu.VMEM((hd, nk), BF16),
        pltpu.VMEM((heads * BLK, hd), BF16),
        pltpu.VMEM((heads * BLK, hd), BF16),
        pltpu.VMEM((2, nk, LANES), F32),
        pltpu.VMEM((2, nk, LANES), F32),
        pltpu.VMEM((nk, heads * BLK), BF16),
        pltpu.VMEM((nk, heads * BLK), BF16),
        pltpu.VMEM((nk, hd), F32),
        pltpu.VMEM((nk, hd), F32),
        pltpu.VMEM((2, 2, heads * BLK), F32),
        pltpu.VMEM((nblocks, 2 * hd), F32),
    ]
    cost = pl.CostEstimate(
        flops=10 * nk * heads * 2 * BLK * hd, bytes_accessed=4 << 20, transcendentals=0
    )
    pick_spec = pl.BlockSpec((ranks, 2 * BLK, hd), lambda i: (0, 0, 0))

    def attend(p, comp, picks, previous):
        out_slot = slot if p else 2 * BLK
        comp_spec = in_vmem()
        out_shape = [
            jax.ShapeDtypeStruct((tokens if p else 2 * BLK, 2 * hd), F32),
            jax.ShapeDtypeStruct((2 * heads, tokens), F32),
            jax.ShapeDtypeStruct((nblocks, 2 * hd), F32),
            jax.ShapeDtypeStruct((ranks, out_slot, hd), BF16),
        ]
        out_specs = [in_vmem()] * 4
        if p == 0:
            comp_spec = pl.BlockSpec((ranks, 2 * qb, hd), lambda i: (0, 2 * BLK // (2 * qb), 0))
            out_shape = (
                [jax.ShapeDtypeStruct(queries.shape, BF16)]
                + out_shape
                + [jax.ShapeDtypeStruct((nblocks, 2 * hd), BF16)]
            )
            out_specs = [pl.BlockSpec((BLK, width), lambda i: (i, 0))] + out_specs + [in_vmem()]
        return pl.pallas_call(
            functools.partial(attend_kernel, ranks, qb, heads, lists, p),
            grid=(2,),
            out_shape=out_shape,
            in_specs=[in_smem(), in_smem()] + row_specs(p) + [comp_spec, pick_spec]
            + [in_vmem()] * len(previous),
            out_specs=out_specs,
            scratch_shapes=scratch,
            compiler_params=params(ranks),
            cost_estimate=cost,
            name=f"attend{p}",
        )(me, table, queries, d_out, keys, values, gate, comp, picks, *previous)

    dq, own0, dz, dc, send, ckv = attend(0, fetched, fetched, [])
    mixed = exchange(send)
    part, dz, dc, send = attend(1, ckv, mixed, [dz, dc, own0])
    home = exchange(send)
    d_queries = pl.pallas_call(
        functools.partial(tail_kernel, ranks, qb, heads, lists),
        grid=(2,),
        out_shape=jax.ShapeDtypeStruct(queries.shape, BF16),
        in_specs=[in_smem()] + row_specs(1) + [in_vmem(), pick_spec, pl.BlockSpec(memory_space=pl.ANY)],
        out_specs=pl.BlockSpec((BLK, width), lambda i: (2 + i, 0)),
        scratch_shapes=scratch,
        input_output_aliases={8: 0},
        compiler_params=params(ranks, 60),
        cost_estimate=cost,
        name="tail",
    )(me, queries, d_out, keys, values, gate, ckv, mixed, dq)

    d_keys, d_values, d_ck, d_cv = pl.pallas_call(
        functools.partial(finish_kernel, ranks, qb, lists),
        out_shape=[
            jax.ShapeDtypeStruct(x.shape, BF16) for x in (keys, values, comp_keys, comp_values)
        ],
        in_specs=[in_smem(), in_smem()] + [in_vmem()] * 3,
        out_specs=[in_vmem()] * 4,
        scratch_shapes=[pltpu.VMEM((tokens, 2 * hd), F32)],
        compiler_params=params(ranks),
        name="finish",
    )(me, table, part, dc, home)

    dz = dz.astype(BF16)
    dz_other = lax.ppermute(dz, "head", swap)
    tn = (((0,), (1,)), ((), ()))
    d_inputs = (
        lax.dot_general(dz, w_mine, tn, preferred_element_type=F32)
        + lax.dot_general(dz_other, w_other, tn, preferred_element_type=F32)
    ).astype(BF16)

    return d_queries, d_keys, d_values, d_ck, d_cv, d_inputs


def solution(mesh):
    split = P("ctx", "head")
    in_specs = (split,) * 5 + (P(), P("ctx", None), P(None, "head"), split)
    return jax.shard_map(
        body, mesh=mesh, in_specs=in_specs, out_specs=(split,) * 6, check_vma=False
    )
```

```python
import functools

import jax
import jax.numpy as jnp
from jax import lax
from jax.experimental import pallas as pl
from jax.experimental.pallas import tpu as pltpu
from jax.sharding import PartitionSpec as P

BLK = 64
PICKS = 15
LOG2E = 1.4426950408889634
LANES = 256
NEG = -1e30
F32, BF16 = jnp.float32, jnp.bfloat16


def reach_lists(ranks):
    half = ranks // 2
    even, odd = [], []
    for j in range(PICKS):
        near = 1 + j * max(half - 1, 0) // 14
        far = half + 1 + j * max(half - 2, 0) // 14
        if j == 0 or near != 1 + (j - 1) * max(half - 1, 0) // 14:
            even.append((j, near))
        if j == 0 or far != half + 1 + (j - 1) * max(half - 2, 0) // 14:
            odd.append((j, far))
    return even, odd


def in_vmem():
    return pl.BlockSpec(memory_space=pltpu.VMEM)


def in_smem():
    return pl.BlockSpec(memory_space=pltpu.SMEM)


def params(ranks, limit=16):
    return pltpu.CompilerParams(vmem_limit_bytes=(limit if ranks <= 16 else 48) * 1024 * 1024)


def fill_picks(ranks, qb, lists, p, me, sel_ref, k_ref, v_ref, out_ref):
    for parity, reach in enumerate(lists):
        for j, r in reach:
            dest = jnp.where(me + r < ranks, me + r, me)
            named = sel_ref[j, dest * qb + 2 * p + parity]
            local = jnp.clip(named - me * qb, 0, qb - 1)
            rows = pl.ds(pl.multiple_of(local * BLK, BLK), BLK)
            out_ref[dest, :BLK, :] = k_ref[rows, :]
            out_ref[dest, BLK : 2 * BLK, :] = v_ref[rows, :]


def pack_kernel(ranks, qb, lists, rank_ref, sel_ref, k_ref, v_ref, ck_ref, cv_ref, out_ref):
    hd = k_ref.shape[1]
    me = rank_ref[0]
    comp = jnp.concatenate([ck_ref[...].astype(F32), cv_ref[...].astype(F32)], axis=0).astype(BF16)

    def every(n, carry):
        out_ref[n, 2 * BLK :, :] = comp
        return carry

    lax.fori_loop(0, ranks, every, 0)
    out_ref[me, : 2 * BLK, :] = jnp.zeros((2 * BLK, hd), BF16)
    fill_picks(ranks, qb, lists, 0, me, sel_ref, k_ref, v_ref, out_ref)


def gate_kernel(qb, heads, x_ref, w_ref, do_ref, out_ref):
    del do_ref
    nt = (((1,), (1,)), ((), ()))
    z = lax.dot_general(w_ref[...], x_ref[...], nt, preferred_element_type=F32)
    zt = jax.nn.sigmoid(z)
    for i in range(qb):
        for branch in range(2):
            for h in range(heads):
                row = branch * heads + h
                out_ref[i, branch : branch + 1, h * BLK : (h + 1) * BLK] = zt[
                    row : row + 1, i * BLK : (i + 1) * BLK
                ]


def fold(x, op):
    return op(x.reshape(x.shape[0] // 8, 8, x.shape[1]), axis=0)


def branch_grad(parts, lanes, gate, s_scr, u_scr, w_scr, d_scr):
    c2 = 128 ** -0.5 * LOG2E
    top = jnp.full((8, LANES), NEG, F32)
    for at, live, mask in parts:
        s = s_scr[at, :]
        if mask is not None:
            s = jnp.where(mask, s, NEG)
            s_scr[at, :] = s
        part = fold(s, jnp.max)
        top = jnp.maximum(top, part if live is None else jnp.where(live, part, NEG))
    top = jnp.max(top, axis=0, keepdims=True) * c2
    total = jnp.zeros((8, LANES), F32)
    mixed = jnp.zeros((8, LANES), F32)
    for at, live, mask in parts:
        e = jnp.exp2(s_scr[at, :] * c2 - (top if live is None else jnp.where(live, top, -NEG)))
        total = total + fold(e, jnp.sum)
        mixed = mixed + fold(e * u_scr[at, :], jnp.sum)
        s_scr[at, :] = e
    inv = 1.0 / jnp.sum(total, axis=0, keepdims=True)
    d_gate = jnp.sum(mixed, axis=0, keepdims=True) * inv
    weight = gate * inv
    for at, live, mask in parts:
        pw = s_scr[at, :] * weight
        w_scr[at, lanes] = pw.astype(BF16)
        d_scr[at, lanes] = (pw * (u_scr[at, :] - d_gate)).astype(BF16)
    return d_gate


def attend_kernel(ranks, qb, heads, lists, p, *refs):
    (rank_ref, sel_ref, q_ref, do_ref, k_ref, v_ref, gate_ref, comp_ref, picks_ref) = refs[:9]
    if p == 0:
        dq_ref, own_ref, dz_ref, dc_ref, send_ref, ckv_ref, *scratch = refs[9:]
    else:
        dz_in, dc_in, own_in, own_ref, dz_ref, dc_ref, send_ref, *scratch = refs[9:]
        dq_ref, ckv_ref = None, None
    hd = k_ref.shape[1]
    me = rank_ref[0]
    step = pl.program_id(0)
    dg_scr, dc_scr = scratch[-2:]

    @pl.when(step == 0)
    def _():
        if p == 0:
            dc_scr[...] = jnp.zeros_like(dc_scr)
            dz_ref[...] = jnp.zeros_like(dz_ref)
            send_ref[me] = jnp.zeros(send_ref.shape[1:], BF16)
            fill_picks(ranks, qb, lists, 1, me, sel_ref, k_ref, v_ref, send_ref)
        else:
            dc_scr[...] = dc_in[...]
            dz_ref[...] = dz_in[...]
            own_ref[: 2 * BLK, :] = own_in[...]
            own_ref[2 * BLK :, :] = jnp.zeros((own_ref.shape[0] - 2 * BLK, own_ref.shape[1]), F32)
            add_homes(ranks, qb, lists, 0, me, sel_ref, picks_ref, own_ref)

    for parity in range(2):

        @pl.when(step == parity)
        def _(parity=parity):
            attend_row(ranks, qb, heads, lists[parity], me, 2 * p + parity, parity, q_ref, do_ref, k_ref, v_ref,
                       gate_ref, comp_ref, picks_ref, dq_ref, own_ref, send_ref, ckv_ref, *scratch)

    @pl.when(step == 1)
    def _():
        dc_ref[...] = dc_scr[...]
        if p == 1:
            for r in range(1, ranks):

                @pl.when(me >= r)
                def _(r=r):
                    at = slice(r * qb, (r + 1) * qb)
                    piece = jnp.concatenate([dc_scr[at, :hd], dc_scr[at, hd:]], axis=0)
                    send_ref[me - r, 2 * BLK :, :] = piece.astype(BF16)

        for i in range(2):
            for branch in range(2):
                for h in range(heads):
                    row = branch * heads + h
                    lane = (2 * p + i) * BLK
                    dz_ref[row : row + 1, lane : lane + BLK] = dg_scr[
                        i, branch : branch + 1, h * BLK : (h + 1) * BLK
                    ]


def tail_kernel(ranks, qb, heads, lists, rank_ref, q_ref, do_ref, k_ref, v_ref, gate_ref, ckv_ref,
                picks_ref, _, dq_ref, *scratch):
    me = rank_ref[0]
    step = pl.program_id(0)
    for parity in range(2):

        @pl.when(step == parity)
        def _(parity=parity):
            attend_row(ranks, qb, heads, lists[parity], me, 2 + parity, parity, q_ref, do_ref, k_ref, v_ref,
                       gate_ref, ckv_ref, picks_ref, dq_ref, None, None, None, *scratch)


def attend_row(ranks, qb, heads, reach, me, row, parity, q_ref, do_ref, k_ref, v_ref, gate_ref,
               comp_ref, picks_ref, dq_ref, own_ref, send_ref, ckv_ref, kcat, vcat, kt, qs, ds,
               s_scr, u_scr, w_scr, d_scr, dv_acc, dk_acc, dg_scr, dc_scr):
    npick = len(reach)
    hd = k_ref.shape[1]
    nblocks = ranks * qb
    nsel = (1 + npick) * BLK
    nk = nsel + nblocks
    per = LANES // BLK
    scale = hd ** -0.5

    if len(comp_ref.shape) == 3:
        pieces = []
        for r in range(ranks):
            pieces.append(comp_ref[jnp.maximum(me - r, 0)].astype(F32))
        kcat[nsel:nk, :] = jnp.concatenate([x[:qb] for x in pieces], axis=0).astype(BF16)
        vcat[nsel:nk, :] = jnp.concatenate([x[qb:] for x in pieces], axis=0).astype(BF16)
        ckv_ref[:, :hd] = kcat[nsel:nk, :]
        ckv_ref[:, hd:] = vcat[nsel:nk, :]
    else:
        kcat[nsel:nk, :] = comp_ref[:, :hd]
        vcat[nsel:nk, :] = comp_ref[:, hd:]
    kcat[:BLK, :] = k_ref[row * BLK : (row + 1) * BLK, :]
    vcat[:BLK, :] = v_ref[row * BLK : (row + 1) * BLK, :]
    for n, (_, r) in enumerate(reach):
        src = jnp.where(me >= r, me - r, me)
        kcat[(n + 1) * BLK : (n + 2) * BLK, :] = picks_ref[src, :BLK, :]
        vcat[(n + 1) * BLK : (n + 2) * BLK, :] = picks_ref[src, BLK : 2 * BLK, :]
    if dq_ref is not None:
        kt[:, :nk] = kcat[:nk, :].astype(F32).T.astype(BF16)
    for h in range(heads):
        qs[h * BLK : (h + 1) * BLK, :] = q_ref[:, h * hd : (h + 1) * hd]
        ds[h * BLK : (h + 1) * BLK, :] = do_ref[:, h * hd : (h + 1) * hd]

    key_pos = lax.broadcasted_iota(jnp.int32, (BLK, LANES), 0)
    tok_pos = lax.rem(lax.broadcasted_iota(jnp.int32, (BLK, LANES), 1), BLK)
    sel_parts = [(slice(0, BLK), None, key_pos <= tok_pos)]
    for n, (_, r) in enumerate(reach):
        sel_parts.append((slice((n + 1) * BLK, (n + 2) * BLK), me >= r, None))
    comp_parts = []
    span = min(nblocks, BLK)
    for n in range(nblocks // span):
        place = lax.broadcasted_iota(jnp.int32, (span, LANES), 0) + n * span
        away, within = place // qb, lax.rem(place, qb)
        seen = (away <= me) & ((away > 0) | (within <= row))
        comp_parts.append((slice(nsel + n * span, nsel + (n + 1) * span), None, seen))

    nt = (((1,), (1,)), ((), ()))
    chunks = heads // per

    def lanes_of(c):
        return slice(c * LANES, (c + 1) * LANES)

    def scores(c):
        lanes = lanes_of(c)
        s_scr[c % 2, :nk, :] = lax.dot_general(kcat[:nk, :], qs[lanes, :], nt, preferred_element_type=F32)
        u_scr[c % 2, :nk, :] = lax.dot_general(vcat[:nk, :], ds[lanes, :], nt, preferred_element_type=F32)

    def soften(c):
        lanes = lanes_of(c)
        work = (s_scr.at[c % 2], u_scr.at[c % 2], w_scr, d_scr)
        for branch, parts in ((1, sel_parts), (0, comp_parts)):
            gate = gate_ref[0, branch : branch + 1, lanes]
            dg = branch_grad(parts, lanes, gate, *work)
            dg_scr[parity, branch : branch + 1, lanes] = dg * gate * (1.0 - gate)

    def gradients(c):
        lanes = lanes_of(c)
        if send_ref is not None:
            dv = jnp.dot(w_scr[:nk, lanes], ds[lanes, :], preferred_element_type=F32)
            dk = jnp.dot(d_scr[:nk, lanes], qs[lanes, :], preferred_element_type=F32)
            if c == 0:
                dv_acc[:nk, :] = dv
                dk_acc[:nk, :] = dk
            else:
                dv_acc[:nk, :] += dv
                dk_acc[:nk, :] += dk
        if dq_ref is not None:
            dqt = jnp.dot(kt[:, :nk], d_scr[:nk, lanes], preferred_element_type=F32)
            dq = (dqt.T * scale).astype(BF16)
            for h in range(per):
                head = c * per + h
                dq_ref[:, head * hd : (head + 1) * hd] = dq[h * BLK : (h + 1) * BLK, :]

    scores(0)
    for c in range(chunks):
        if c + 1 < chunks:
            scores(c + 1)
        if c > 0:
            gradients(c - 1)
        soften(c)
    gradients(chunks - 1)
    if send_ref is None:
        return

    own = slice(row * BLK, (row + 1) * BLK)
    if row < 2:
        own_ref[own, :hd] = dk_acc[:BLK, :] * scale
        own_ref[own, hd:] = dv_acc[:BLK, :]
    else:
        own_ref[own, :hd] += dk_acc[:BLK, :] * scale
        own_ref[own, hd:] += dv_acc[:BLK, :]
    dc_scr[:, :hd] += dk_acc[nsel:nk, :] * scale
    dc_scr[:, hd:] += dv_acc[nsel:nk, :]
    for n, (_, r) in enumerate(reach):
        at = slice((n + 1) * BLK, (n + 2) * BLK)
        dest = jnp.where(me >= r, me - r, me)
        send_ref[dest, :BLK, :] = (dk_acc[at, :] * scale).astype(BF16)
        send_ref[dest, BLK : 2 * BLK, :] = dv_acc[at, :].astype(BF16)


def add_homes(ranks, qb, lists, p, me, sel_ref, home_ref, acc):
    hd = home_ref.shape[2]
    for parity, reach in enumerate(lists):
        for j, r in reach:
            src = jnp.minimum(me + r, ranks - 1)
            named = sel_ref[j, src * qb + 2 * p + parity]
            local = jnp.clip(named - me * qb, 0, qb - 1)
            rows = pl.ds(pl.multiple_of(local * BLK, BLK), BLK)
            live = me + r < ranks
            acc[rows, :hd] += jnp.where(live, home_ref[src, :BLK, :].astype(F32), 0.0)
            acc[rows, hd:] += jnp.where(live, home_ref[src, BLK : 2 * BLK, :].astype(F32), 0.0)


def finish_kernel(ranks, qb, lists, rank_ref, sel_ref, part_ref, dc_ref, home_ref,
                  dk_ref, dv_ref, dck_ref, dcv_ref, acc):
    hd = dk_ref.shape[1]
    me = rank_ref[0]
    acc[...] = part_ref[...]
    add_homes(ranks, qb, lists, 1, me, sel_ref, home_ref, acc)
    dk_ref[...] = acc[:, :hd].astype(BF16)
    dv_ref[...] = acc[:, hd:].astype(BF16)

    def add(n, total):
        return total + home_ref[n, 2 * BLK :, :].astype(F32)

    total = lax.fori_loop(me + 1, ranks, add, jnp.zeros((2 * qb, hd), F32))
    dck_ref[...] = (total[:qb] + dc_ref[:qb, :hd]).astype(BF16)
    dcv_ref[...] = (total[qb:] + dc_ref[:qb, hd:]).astype(BF16)


def body(queries, keys, values, comp_keys, comp_values, selected, inputs, w_gate, d_out):
    tokens, width = queries.shape
    hd = keys.shape[1]
    heads = width // hd
    qb = tokens // BLK
    pair = qb // 2
    ranks = lax.axis_size("ctx")
    rank = lax.axis_index("ctx").astype(jnp.int32)
    me = rank.reshape(1)
    head = lax.axis_index("head")
    nblocks = ranks * qb
    lists = reach_lists(ranks)
    table = selected.T

    slot = 2 * BLK + 2 * qb

    def exchange(x):
        return lax.all_to_all(x, "ctx", split_axis=0, concat_axis=0, tiled=True)

    send = pl.pallas_call(
        functools.partial(pack_kernel, ranks, qb, lists),
        out_shape=jax.ShapeDtypeStruct((ranks, slot, hd), BF16),
        in_specs=[in_smem(), in_smem()] + [in_vmem()] * 4,
        out_specs=in_vmem(),
        compiler_params=params(ranks, 56),
        name="pack",
    )(me, table, keys, values, comp_keys, comp_values)
    fetched = exchange(send)

    gate = pl.pallas_call(
        functools.partial(gate_kernel, qb, heads),
        out_shape=jax.ShapeDtypeStruct((qb, 2, heads * BLK), F32),
        in_specs=[in_vmem()] * 3,
        out_specs=in_vmem(),
        compiler_params=params(ranks),
        cost_estimate=pl.CostEstimate(
            flops=2 * inputs.size * w_gate.shape[1], bytes_accessed=2 * inputs.size, transcendentals=0
        ),
        name="gate",
    )(inputs, w_gate.T, d_out)
    half = w_gate.shape[0] // 2
    swap = [(0, 1), (1, 0)]
    w_send = lax.dynamic_slice_in_dim(w_gate, (1 - head) * half, half, 0)
    w_mine = lax.dynamic_slice_in_dim(w_gate, head * half, half, 0)
    w_other = lax.ppermute(w_send, "head", swap)

    nk = (1 + max(len(x) for x in lists)) * BLK + nblocks

    def row_specs(p):
        row = lambda i: (2 * p + i, 0)
        return [
            pl.BlockSpec((BLK, width), row),
            pl.BlockSpec((BLK, width), row),
            in_vmem(),
            in_vmem(),
            pl.BlockSpec((1, 2, heads * BLK), lambda i: (2 * p + i, 0, 0)),
        ]

    scratch = [
        pltpu.VMEM((nk, hd), BF16),
        pltpu.VMEM((nk, hd), BF16),
        pltpu.VMEM((hd, nk), BF16),
        pltpu.VMEM((heads * BLK, hd), BF16),
        pltpu.VMEM((heads * BLK, hd), BF16),
        pltpu.VMEM((2, nk, LANES), F32),
        pltpu.VMEM((2, nk, LANES), F32),
        pltpu.VMEM((nk, heads * BLK), BF16),
        pltpu.VMEM((nk, heads * BLK), BF16),
        pltpu.VMEM((nk, hd), F32),
        pltpu.VMEM((nk, hd), F32),
        pltpu.VMEM((2, 2, heads * BLK), F32),
        pltpu.VMEM((nblocks, 2 * hd), F32),
    ]
    cost = pl.CostEstimate(
        flops=10 * nk * heads * 2 * BLK * hd, bytes_accessed=4 << 20, transcendentals=0
    )
    pick_spec = pl.BlockSpec((ranks, 2 * BLK, hd), lambda i: (0, 0, 0))

    def attend(p, comp, picks, previous):
        out_slot = slot if p else 2 * BLK
        comp_spec = in_vmem()
        out_shape = [
            jax.ShapeDtypeStruct((tokens if p else 2 * BLK, 2 * hd), F32),
            jax.ShapeDtypeStruct((2 * heads, tokens), F32),
            jax.ShapeDtypeStruct((nblocks, 2 * hd), F32),
            jax.ShapeDtypeStruct((ranks, out_slot, hd), BF16),
        ]
        out_specs = [in_vmem()] * 4
        if p == 0:
            comp_spec = pl.BlockSpec((ranks, 2 * qb, hd), lambda i: (0, 2 * BLK // (2 * qb), 0))
            out_shape = (
                [jax.ShapeDtypeStruct(queries.shape, BF16)]
                + out_shape
                + [jax.ShapeDtypeStruct((nblocks, 2 * hd), BF16)]
            )
            out_specs = [pl.BlockSpec((BLK, width), lambda i: (i, 0))] + out_specs + [in_vmem()]
        return pl.pallas_call(
            functools.partial(attend_kernel, ranks, qb, heads, lists, p),
            grid=(2,),
            out_shape=out_shape,
            in_specs=[in_smem(), in_smem()] + row_specs(p) + [comp_spec, pick_spec]
            + [in_vmem()] * len(previous),
            out_specs=out_specs,
            scratch_shapes=scratch,
            compiler_params=params(ranks),
            cost_estimate=cost,
            name=f"attend{p}",
        )(me, table, queries, d_out, keys, values, gate, comp, picks, *previous)

    dq, own0, dz, dc, send, ckv = attend(0, fetched, fetched, [])
    mixed = exchange(send)
    part, dz, dc, send = attend(1, ckv, mixed, [dz, dc, own0])
    home = exchange(send)
    d_queries = pl.pallas_call(
        functools.partial(tail_kernel, ranks, qb, heads, lists),
        grid=(2,),
        out_shape=jax.ShapeDtypeStruct(queries.shape, BF16),
        in_specs=[in_smem()] + row_specs(1) + [in_vmem(), pick_spec, pl.BlockSpec(memory_space=pl.ANY)],
        out_specs=pl.BlockSpec((BLK, width), lambda i: (2 + i, 0)),
        scratch_shapes=scratch,
        input_output_aliases={8: 0},
        compiler_params=params(ranks, 60),
        cost_estimate=cost,
        name="tail",
    )(me, queries, d_out, keys, values, gate, ckv, mixed, dq)

    d_keys, d_values, d_ck, d_cv = pl.pallas_call(
        functools.partial(finish_kernel, ranks, qb, lists),
        out_shape=[
            jax.ShapeDtypeStruct(x.shape, BF16) for x in (keys, values, comp_keys, comp_values)
        ],
        in_specs=[in_smem(), in_smem()] + [in_vmem()] * 3,
        out_specs=[in_vmem()] * 4,
        scratch_shapes=[pltpu.VMEM((tokens, 2 * hd), F32)],
        compiler_params=params(ranks),
        name="finish",
    )(me, table, part, dc, home)

    dz = dz.astype(BF16)
    dz_other = lax.ppermute(dz, "head", swap)
    tn = (((0,), (1,)), ((), ()))
    d_inputs = (
        lax.dot_general(dz, w_mine, tn, preferred_element_type=F32)
        + lax.dot_general(dz_other, w_other, tn, preferred_element_type=F32)
    ).astype(BF16)

    return d_queries, d_keys, d_values, d_ck, d_cv, d_inputs


def solution(mesh):
    split = P("ctx", "head")
    in_specs = (split,) * 5 + (P(), P("ctx", None), P(None, "head"), split)
    return jax.shard_map(
        body, mesh=mesh, in_specs=in_specs, out_specs=(split,) * 6, check_vma=False
    )
```

```python
import functools

import jax
import jax.numpy as jnp
from jax import lax
from jax.experimental import pallas as pl
from jax.experimental.pallas import tpu as pltpu
from jax.sharding import PartitionSpec as P

BLK = 64
PICKS = 15
LOG2E = 1.4426950408889634
LANES = 256
NEG = -1e30
F32, BF16 = jnp.float32, jnp.bfloat16


def reach_lists(ranks):
    half = ranks // 2
    even, odd = [], []
    for j in range(PICKS):
        near = 1 + j * max(half - 1, 0) // 14
        far = half + 1 + j * max(half - 2, 0) // 14
        if j == 0 or near != 1 + (j - 1) * max(half - 1, 0) // 14:
            even.append((j, near))
        if j == 0 or far != half + 1 + (j - 1) * max(half - 2, 0) // 14:
            odd.append((j, far))
    return even, odd


def in_vmem():
    return pl.BlockSpec(memory_space=pltpu.VMEM)


def in_smem():
    return pl.BlockSpec(memory_space=pltpu.SMEM)


def params(ranks, limit=16):
    return pltpu.CompilerParams(vmem_limit_bytes=(limit if ranks <= 16 else 48) * 1024 * 1024)


def fill_picks(ranks, qb, lists, p, me, sel_ref, k_ref, v_ref, out_ref):
    for parity, reach in enumerate(lists):
        for j, r in reach:
            dest = jnp.where(me + r < ranks, me + r, me)
            named = sel_ref[j, dest * qb + 2 * p + parity]
            local = jnp.clip(named - me * qb, 0, qb - 1)
            rows = pl.ds(pl.multiple_of(local * BLK, BLK), BLK)
            out_ref[dest, :BLK, :] = k_ref[rows, :]
            out_ref[dest, BLK : 2 * BLK, :] = v_ref[rows, :]


def pack_kernel(ranks, qb, lists, rank_ref, sel_ref, k_ref, v_ref, ck_ref, cv_ref, out_ref):
    hd = k_ref.shape[1]
    me = rank_ref[0]
    comp = jnp.concatenate([ck_ref[...].astype(F32), cv_ref[...].astype(F32)], axis=0).astype(BF16)

    def every(n, carry):
        out_ref[n, 2 * BLK :, :] = comp
        return carry

    lax.fori_loop(0, ranks, every, 0)
    out_ref[me, : 2 * BLK, :] = jnp.zeros((2 * BLK, hd), BF16)
    fill_picks(ranks, qb, lists, 0, me, sel_ref, k_ref, v_ref, out_ref)


def gate_kernel(qb, heads, x_ref, w_ref, do_ref, out_ref):
    del do_ref
    nt = (((1,), (1,)), ((), ()))
    z = lax.dot_general(w_ref[...], x_ref[...], nt, preferred_element_type=F32)
    zt = jax.nn.sigmoid(z)
    for i in range(qb):
        for branch in range(2):
            for h in range(heads):
                row = branch * heads + h
                out_ref[i, branch : branch + 1, h * BLK : (h + 1) * BLK] = zt[
                    row : row + 1, i * BLK : (i + 1) * BLK
                ]


def fold(x, op):
    return op(x.reshape(x.shape[0] // 8, 8, x.shape[1]), axis=0)


def branch_grad(parts, lanes, gate, s_scr, u_scr, w_scr, d_scr):
    c2 = 128 ** -0.5 * LOG2E
    top = jnp.full((8, LANES), NEG, F32)
    for at, live, mask in parts:
        s = s_scr[at, :]
        if mask is not None:
            s = jnp.where(mask, s, NEG)
            s_scr[at, :] = s
        part = fold(s, jnp.max)
        top = jnp.maximum(top, part if live is None else jnp.where(live, part, NEG))
    top = jnp.max(top, axis=0, keepdims=True) * c2
    total = jnp.zeros((8, LANES), F32)
    mixed = jnp.zeros((8, LANES), F32)
    for at, live, mask in parts:
        e = jnp.exp2(s_scr[at, :] * c2 - (top if live is None else jnp.where(live, top, -NEG)))
        total = total + fold(e, jnp.sum)
        mixed = mixed + fold(e * u_scr[at, :], jnp.sum)
        s_scr[at, :] = e
    inv = 1.0 / jnp.sum(total, axis=0, keepdims=True)
    d_gate = jnp.sum(mixed, axis=0, keepdims=True) * inv
    weight = gate * inv
    for at, live, mask in parts:
        pw = s_scr[at, :] * weight
        w_scr[at, lanes] = pw.astype(BF16)
        d_scr[at, lanes] = (pw * (u_scr[at, :] - d_gate)).astype(BF16)
    return d_gate


def attend_kernel(ranks, qb, heads, lists, p, *refs):
    (rank_ref, sel_ref, q_ref, do_ref, k_ref, v_ref, gate_ref, comp_ref, picks_ref) = refs[:9]
    if p == 0:
        dq_ref, own_ref, dz_ref, dc_ref, send_ref, ckv_ref, *scratch = refs[9:]
    else:
        dz_in, dc_in, own_in, own_ref, dz_ref, dc_ref, send_ref, *scratch = refs[9:]
        dq_ref, ckv_ref = None, None
    hd = k_ref.shape[1]
    me = rank_ref[0]
    step = pl.program_id(0)
    dg_scr, dc_scr = scratch[-2:]

    @pl.when(step == 0)
    def _():
        if p == 0:
            dc_scr[...] = jnp.zeros_like(dc_scr)
            dz_ref[...] = jnp.zeros_like(dz_ref)
            send_ref[me] = jnp.zeros(send_ref.shape[1:], BF16)
            fill_picks(ranks, qb, lists, 1, me, sel_ref, k_ref, v_ref, send_ref)
        else:
            dc_scr[...] = dc_in[...]
            dz_ref[...] = dz_in[...]
            own_ref[: 2 * BLK, :] = own_in[...]
            own_ref[2 * BLK :, :] = jnp.zeros((own_ref.shape[0] - 2 * BLK, own_ref.shape[1]), F32)
            add_homes(ranks, qb, lists, 0, me, sel_ref, picks_ref, own_ref)

    for parity in range(2):

        @pl.when(step == parity)
        def _(parity=parity):
            attend_row(ranks, qb, heads, lists[parity], me, 2 * p + parity, parity, q_ref, do_ref, k_ref, v_ref,
                       gate_ref, comp_ref, picks_ref, dq_ref, own_ref, send_ref, ckv_ref, *scratch)

    @pl.when(step == 1)
    def _():
        dc_ref[...] = dc_scr[...]
        if p == 1:
            for r in range(1, ranks):

                @pl.when(me >= r)
                def _(r=r):
                    at = slice(r * qb, (r + 1) * qb)
                    piece = jnp.concatenate([dc_scr[at, :hd], dc_scr[at, hd:]], axis=0)
                    send_ref[me - r, 2 * BLK :, :] = piece.astype(BF16)

        for i in range(2):
            for branch in range(2):
                for h in range(heads):
                    row = branch * heads + h
                    lane = (2 * p + i) * BLK
                    dz_ref[row : row + 1, lane : lane + BLK] = dg_scr[
                        i, branch : branch + 1, h * BLK : (h + 1) * BLK
                    ]


def tail_kernel(ranks, qb, heads, lists, rank_ref, q_ref, do_ref, k_ref, v_ref, gate_ref, ckv_ref,
                picks_ref, _, dq_ref, *scratch):
    me = rank_ref[0]
    step = pl.program_id(0)
    for parity in range(2):

        @pl.when(step == parity)
        def _(parity=parity):
            attend_row(ranks, qb, heads, lists[parity], me, 2 + parity, parity, q_ref, do_ref, k_ref, v_ref,
                       gate_ref, ckv_ref, picks_ref, dq_ref, None, None, None, *scratch)


def attend_row(ranks, qb, heads, reach, me, row, parity, q_ref, do_ref, k_ref, v_ref, gate_ref,
               comp_ref, picks_ref, dq_ref, own_ref, send_ref, ckv_ref, kcat, vcat, kt, qs, ds,
               s_scr, u_scr, w_scr, d_scr, dv_acc, dk_acc, dg_scr, dc_scr):
    npick = len(reach)
    hd = k_ref.shape[1]
    nblocks = ranks * qb
    nsel = (1 + npick) * BLK
    nk = nsel + nblocks
    per = LANES // BLK
    scale = hd ** -0.5

    if len(comp_ref.shape) == 3:
        pieces = []
        for r in range(ranks):
            pieces.append(comp_ref[jnp.maximum(me - r, 0)].astype(F32))
        kcat[nsel:nk, :] = jnp.concatenate([x[:qb] for x in pieces], axis=0).astype(BF16)
        vcat[nsel:nk, :] = jnp.concatenate([x[qb:] for x in pieces], axis=0).astype(BF16)
        ckv_ref[:, :hd] = kcat[nsel:nk, :]
        ckv_ref[:, hd:] = vcat[nsel:nk, :]
    else:
        kcat[nsel:nk, :] = comp_ref[:, :hd]
        vcat[nsel:nk, :] = comp_ref[:, hd:]
    kcat[:BLK, :] = k_ref[row * BLK : (row + 1) * BLK, :]
    vcat[:BLK, :] = v_ref[row * BLK : (row + 1) * BLK, :]
    for n, (_, r) in enumerate(reach):
        src = jnp.where(me >= r, me - r, me)
        kcat[(n + 1) * BLK : (n + 2) * BLK, :] = picks_ref[src, :BLK, :]
        vcat[(n + 1) * BLK : (n + 2) * BLK, :] = picks_ref[src, BLK : 2 * BLK, :]
    for h in range(heads):
        qs[h * BLK : (h + 1) * BLK, :] = q_ref[:, h * hd : (h + 1) * hd]
        ds[h * BLK : (h + 1) * BLK, :] = do_ref[:, h * hd : (h + 1) * hd]

    key_pos = lax.broadcasted_iota(jnp.int32, (BLK, LANES), 0)
    tok_pos = lax.rem(lax.broadcasted_iota(jnp.int32, (BLK, LANES), 1), BLK)
    sel_parts = [(slice(0, BLK), None, key_pos <= tok_pos)]
    for n, (_, r) in enumerate(reach):
        sel_parts.append((slice((n + 1) * BLK, (n + 2) * BLK), me >= r, None))
    comp_parts = []
    span = min(nblocks, BLK)
    for n in range(nblocks // span):
        place = lax.broadcasted_iota(jnp.int32, (span, LANES), 0) + n * span
        away, within = place // qb, lax.rem(place, qb)
        seen = (away <= me) & ((away > 0) | (within <= row))
        comp_parts.append((slice(nsel + n * span, nsel + (n + 1) * span), None, seen))

    nt = (((1,), (1,)), ((), ()))
    chunks = heads // per

    def lanes_of(c):
        return slice(c * LANES, (c + 1) * LANES)

    def scores(c):
        lanes = lanes_of(c)
        s_scr[c % 2, :nk, :] = lax.dot_general(kcat[:nk, :], qs[lanes, :], nt, preferred_element_type=F32)
        u_scr[c % 2, :nk, :] = lax.dot_general(vcat[:nk, :], ds[lanes, :], nt, preferred_element_type=F32)

    def soften(c):
        lanes = lanes_of(c)
        work = (s_scr.at[c % 2], u_scr.at[c % 2], w_scr, d_scr)
        for branch, parts in ((1, sel_parts), (0, comp_parts)):
            gate = gate_ref[0, branch : branch + 1, lanes]
            dg = branch_grad(parts, lanes, gate, *work)
            dg_scr[parity, branch : branch + 1, lanes] = dg * gate * (1.0 - gate)

    def gradients(c):
        lanes = lanes_of(c)
        if send_ref is not None:
            dv = jnp.dot(w_scr[:nk, lanes], ds[lanes, :], preferred_element_type=F32)
            dk = jnp.dot(d_scr[:nk, lanes], qs[lanes, :], preferred_element_type=F32)
            if c == 0:
                dv_acc[:nk, :] = dv
                dk_acc[:nk, :] = dk
            else:
                dv_acc[:nk, :] += dv
                dk_acc[:nk, :] += dk
        if dq_ref is not None:
            dqt = jnp.dot(kt[:, :nk], d_scr[:nk, lanes], preferred_element_type=F32)
            dq = (dqt.T * scale).astype(BF16)
            for h in range(per):
                head = c * per + h
                dq_ref[:, head * hd : (head + 1) * hd] = dq[h * BLK : (h + 1) * BLK, :]

    scores(0)
    if dq_ref is not None:
        kt[:, :nk] = kcat[:nk, :].astype(F32).T.astype(BF16)
    for c in range(chunks):
        if c + 1 < chunks:
            scores(c + 1)
        if c > 0:
            gradients(c - 1)
        soften(c)
    gradients(chunks - 1)
    if send_ref is None:
        return

    own = slice(row * BLK, (row + 1) * BLK)
    if row < 2:
        own_ref[own, :hd] = dk_acc[:BLK, :] * scale
        own_ref[own, hd:] = dv_acc[:BLK, :]
    else:
        own_ref[own, :hd] += dk_acc[:BLK, :] * scale
        own_ref[own, hd:] += dv_acc[:BLK, :]
    dc_scr[:, :hd] += dk_acc[nsel:nk, :] * scale
    dc_scr[:, hd:] += dv_acc[nsel:nk, :]
    for n, (_, r) in enumerate(reach):
        at = slice((n + 1) * BLK, (n + 2) * BLK)
        dest = jnp.where(me >= r, me - r, me)
        send_ref[dest, :BLK, :] = (dk_acc[at, :] * scale).astype(BF16)
        send_ref[dest, BLK : 2 * BLK, :] = dv_acc[at, :].astype(BF16)


def add_homes(ranks, qb, lists, p, me, sel_ref, home_ref, acc):
    hd = home_ref.shape[2]
    for parity, reach in enumerate(lists):
        for j, r in reach:
            src = jnp.minimum(me + r, ranks - 1)
            named = sel_ref[j, src * qb + 2 * p + parity]
            local = jnp.clip(named - me * qb, 0, qb - 1)
            rows = pl.ds(pl.multiple_of(local * BLK, BLK), BLK)
            live = me + r < ranks
            acc[rows, :hd] += jnp.where(live, home_ref[src, :BLK, :].astype(F32), 0.0)
            acc[rows, hd:] += jnp.where(live, home_ref[src, BLK : 2 * BLK, :].astype(F32), 0.0)


def finish_kernel(ranks, qb, lists, rank_ref, sel_ref, part_ref, dc_ref, home_ref,
                  dk_ref, dv_ref, dck_ref, dcv_ref, acc):
    hd = dk_ref.shape[1]
    me = rank_ref[0]
    acc[...] = part_ref[...]
    add_homes(ranks, qb, lists, 1, me, sel_ref, home_ref, acc)
    dk_ref[...] = acc[:, :hd].astype(BF16)
    dv_ref[...] = acc[:, hd:].astype(BF16)

    def add(n, total):
        return total + home_ref[n, 2 * BLK :, :].astype(F32)

    total = lax.fori_loop(me + 1, ranks, add, jnp.zeros((2 * qb, hd), F32))
    dck_ref[...] = (total[:qb] + dc_ref[:qb, :hd]).astype(BF16)
    dcv_ref[...] = (total[qb:] + dc_ref[:qb, hd:]).astype(BF16)


def body(queries, keys, values, comp_keys, comp_values, selected, inputs, w_gate, d_out):
    tokens, width = queries.shape
    hd = keys.shape[1]
    heads = width // hd
    qb = tokens // BLK
    pair = qb // 2
    ranks = lax.axis_size("ctx")
    rank = lax.axis_index("ctx").astype(jnp.int32)
    me = rank.reshape(1)
    head = lax.axis_index("head")
    nblocks = ranks * qb
    lists = reach_lists(ranks)
    table = selected.T

    slot = 2 * BLK + 2 * qb

    def exchange(x):
        return lax.all_to_all(x, "ctx", split_axis=0, concat_axis=0, tiled=True)

    send = pl.pallas_call(
        functools.partial(pack_kernel, ranks, qb, lists),
        out_shape=jax.ShapeDtypeStruct((ranks, slot, hd), BF16),
        in_specs=[in_smem(), in_smem()] + [in_vmem()] * 4,
        out_specs=in_vmem(),
        compiler_params=params(ranks, 56),
        name="pack",
    )(me, table, keys, values, comp_keys, comp_values)
    fetched = exchange(send)

    gate = pl.pallas_call(
        functools.partial(gate_kernel, qb, heads),
        out_shape=jax.ShapeDtypeStruct((qb, 2, heads * BLK), F32),
        in_specs=[in_vmem()] * 3,
        out_specs=in_vmem(),
        compiler_params=params(ranks),
        cost_estimate=pl.CostEstimate(
            flops=2 * inputs.size * w_gate.shape[1], bytes_accessed=2 * inputs.size, transcendentals=0
        ),
        name="gate",
    )(inputs, w_gate.T, d_out)
    half = w_gate.shape[0] // 2
    swap = [(0, 1), (1, 0)]
    w_send = lax.dynamic_slice_in_dim(w_gate, (1 - head) * half, half, 0)
    w_mine = lax.dynamic_slice_in_dim(w_gate, head * half, half, 0)
    w_other = lax.ppermute(w_send, "head", swap)

    nk = (1 + max(len(x) for x in lists)) * BLK + nblocks

    def row_specs(p):
        row = lambda i: (2 * p + i, 0)
        return [
            pl.BlockSpec((BLK, width), row),
            pl.BlockSpec((BLK, width), row),
            in_vmem(),
            in_vmem(),
            pl.BlockSpec((1, 2, heads * BLK), lambda i: (2 * p + i, 0, 0)),
        ]

    scratch = [
        pltpu.VMEM((nk, hd), BF16),
        pltpu.VMEM((nk, hd), BF16),
        pltpu.VMEM((hd, nk), BF16),
        pltpu.VMEM((heads * BLK, hd), BF16),
        pltpu.VMEM((heads * BLK, hd), BF16),
        pltpu.VMEM((2, nk, LANES), F32),
        pltpu.VMEM((2, nk, LANES), F32),
        pltpu.VMEM((nk, heads * BLK), BF16),
        pltpu.VMEM((nk, heads * BLK), BF16),
        pltpu.VMEM((nk, hd), F32),
        pltpu.VMEM((nk, hd), F32),
        pltpu.VMEM((2, 2, heads * BLK), F32),
        pltpu.VMEM((nblocks, 2 * hd), F32),
    ]
    cost = pl.CostEstimate(
        flops=10 * nk * heads * 2 * BLK * hd, bytes_accessed=4 << 20, transcendentals=0
    )
    pick_spec = pl.BlockSpec((ranks, 2 * BLK, hd), lambda i: (0, 0, 0))

    def attend(p, comp, picks, previous):
        out_slot = slot if p else 2 * BLK
        comp_spec = in_vmem()
        out_shape = [
            jax.ShapeDtypeStruct((tokens if p else 2 * BLK, 2 * hd), F32),
            jax.ShapeDtypeStruct((2 * heads, tokens), F32),
            jax.ShapeDtypeStruct((nblocks, 2 * hd), F32),
            jax.ShapeDtypeStruct((ranks, out_slot, hd), BF16),
        ]
        out_specs = [in_vmem()] * 4
        if p == 0:
            comp_spec = pl.BlockSpec((ranks, 2 * qb, hd), lambda i: (0, 2 * BLK // (2 * qb), 0))
            out_shape = (
                [jax.ShapeDtypeStruct(queries.shape, BF16)]
                + out_shape
                + [jax.ShapeDtypeStruct((nblocks, 2 * hd), BF16)]
            )
            out_specs = [pl.BlockSpec((BLK, width), lambda i: (i, 0))] + out_specs + [in_vmem()]
        return pl.pallas_call(
            functools.partial(attend_kernel, ranks, qb, heads, lists, p),
            grid=(2,),
            out_shape=out_shape,
            in_specs=[in_smem(), in_smem()] + row_specs(p) + [comp_spec, pick_spec]
            + [in_vmem()] * len(previous),
            out_specs=out_specs,
            scratch_shapes=scratch,
            compiler_params=params(ranks),
            cost_estimate=cost,
            name=f"attend{p}",
        )(me, table, queries, d_out, keys, values, gate, comp, picks, *previous)

    dq, own0, dz, dc, send, ckv = attend(0, fetched, fetched, [])
    mixed = exchange(send)
    part, dz, dc, send = attend(1, ckv, mixed, [dz, dc, own0])
    home = exchange(send)
    d_queries = pl.pallas_call(
        functools.partial(tail_kernel, ranks, qb, heads, lists),
        grid=(2,),
        out_shape=jax.ShapeDtypeStruct(queries.shape, BF16),
        in_specs=[in_smem()] + row_specs(1) + [in_vmem(), pick_spec, pl.BlockSpec(memory_space=pl.ANY)],
        out_specs=pl.BlockSpec((BLK, width), lambda i: (2 + i, 0)),
        scratch_shapes=scratch,
        input_output_aliases={8: 0},
        compiler_params=params(ranks, 60),
        cost_estimate=cost,
        name="tail",
    )(me, queries, d_out, keys, values, gate, ckv, mixed, dq)

    d_keys, d_values, d_ck, d_cv = pl.pallas_call(
        functools.partial(finish_kernel, ranks, qb, lists),
        out_shape=[
            jax.ShapeDtypeStruct(x.shape, BF16) for x in (keys, values, comp_keys, comp_values)
        ],
        in_specs=[in_smem(), in_smem()] + [in_vmem()] * 3,
        out_specs=[in_vmem()] * 4,
        scratch_shapes=[pltpu.VMEM((tokens, 2 * hd), F32)],
        compiler_params=params(ranks),
        name="finish",
    )(me, table, part, dc, home)

    dz = dz.astype(BF16)
    dz_other = lax.ppermute(dz, "head", swap)
    tn = (((0,), (1,)), ((), ()))
    d_inputs = (
        lax.dot_general(dz, w_mine, tn, preferred_element_type=F32)
        + lax.dot_general(dz_other, w_other, tn, preferred_element_type=F32)
    ).astype(BF16)

    return d_queries, d_keys, d_values, d_ck, d_cv, d_inputs


def solution(mesh):
    split = P("ctx", "head")
    in_specs = (split,) * 5 + (P(), P("ctx", None), P(None, "head"), split)
    return jax.shard_map(
        body, mesh=mesh, in_specs=in_specs, out_specs=(split,) * 6, check_vma=False
    )
```
